32 devices in a mesh: ctx: 8 (over y, x, core), ch: 4 (over z).
Axes of the slice: x: 2, y: 2, z: 4, core: 2. Of those that a mesh axis runs over, the one named last changes fastest.
Arguments:
- pre_gate: bfloat16 [128, 65536], P('ch', 'ctx'), may hold values from -6 to 6
- value: bfloat16 [128, 65536], P('ch', 'ctx'), may hold values from -6 to 6
- post_gate: bfloat16 [128, 65536], P('ch', 'ctx'), may hold values from -6 to 6
- filter_taps: float32 [8, 65536], P('ch', 'ctx'), may hold values from -0.015625 to 0.015625, as said below
- skip: float32 [128], P('ch'), may hold values from -6 to 6
Outputs:
- mixed: bfloat16 [128, 65536], P(None, ('ctx', 'ch'))
The draws below stay inside these ranges and needn't reach their ends.
Inputs may be any that keep to these rules, and one draw needn't show every extreme that they name: `filter_taps`: one row of taps for each filter group.
All inputs are finite; a program needn't handle non-finite values.
Results may differ from the reference program's by a relative error of at most 0.013.
Values may be sent and summed in bfloat16 or wider, within the bound.
No kernel may reach another device: no remote copies, remote signals or barrier semaphores. Data moves between devices by JAX's collectives and lax.ppermute only.
A program may use at most 128 MiB of HBM per device.

```python
import math
import jax
import jax.numpy as jnp
from jax import lax

C = 128
GROUP = 16
SEQ = 65536
GROUPS = 8


def draw_filter_taps(key, part):
    key = jax.random.fold_in(key, 11)
    tap_scale = 1.0 / math.sqrt(SEQ)
    normal_taps = jax.random.normal(key, (GROUPS, SEQ), jnp.float32)
    return (tap_scale * jnp.clip(normal_taps, -4.0, 4.0)).astype(jnp.float32)


def block_levels(key, extent, cuts, low, largest):
    factor_of = 1.0
    for axis_at, blocks in cuts:
        draws = jax.random.uniform(jax.random.fold_in(jax.random.fold_in(key, 6), axis_at), (blocks,), jnp.float32, low / len(cuts), largest / len(cuts))
        factor_of = factor_of * jnp.repeat(jnp.exp(draws), extent[axis_at] // blocks).reshape((-1,) + (1,) * (len(extent) - 1 - axis_at))
    return factor_of


def scatter_about(own_key, shape, scale, most, shards=(), kind=jnp.bfloat16):
    loudness = block_levels(own_key, shape, shards, -0.22, 0.18) if shards else 1.0
    drawn = jax.random.normal(own_key, shape, jnp.float32) * scale * loudness
    return jnp.minimum(jnp.maximum(drawn, -most), most).astype(kind)


def setup_inputs(seed: int = 0) -> dict:
    seeds = jax.random.split(jax.random.key(seed), 6)
    pre_gate = scatter_about(seeds[0], (C, SEQ), 1.0, 6.0, ((0, 4), (1, 8)))
    value = scatter_about(seeds[1], (C, SEQ), 1.0, 6.0, ((0, 4), (1, 8)))
    post_gate = scatter_about(seeds[2], (C, SEQ), 1.0, 6.0, ((0, 4), (1, 8)))
    filter_taps = draw_filter_taps(jax.random.fold_in(seeds[5], 71), 0)
    skip = scatter_about(seeds[4], (C,), 1.0, 6.0, ((0, 4),), jnp.float32)
    return {"pre_gate": pre_gate, "value": value, "post_gate": post_gate, "filter_taps": filter_taps, "skip": skip}


def reference(pre_gate, value, post_gate, filter_taps, skip):
    fft_length = 2 * SEQ
    signal = (pre_gate.astype(jnp.float32) * value.astype(jnp.float32)).astype(jnp.bfloat16)
    signal_wide = signal.astype(jnp.float32)

    def one_group(items):
        rows_here, taps_here = items
        transformed = jnp.fft.rfft(rows_here, n=fft_length, axis=1)
        filt_spec = jnp.fft.rfft(taps_here, n=fft_length)
        product = transformed * filt_spec[None, :]
        return jnp.fft.irfft(product, n=fft_length, axis=1)[:, :SEQ]

    conv = lax.map(one_group, (signal_wide.reshape(GROUPS, GROUP, SEQ), filter_taps)).reshape(C, SEQ)
    mixed = post_gate.astype(jnp.float32) * (conv + skip[:, None] * signal_wide)
    return mixed.astype(jnp.bfloat16)
```

```python
import functools

import jax
import jax.numpy as jnp
from jax import lax
from jax.experimental import pallas as pl
from jax.experimental.pallas import tpu as pltpu
from jax.sharding import PartitionSpec as P

W = 256
HALF = 128
SEGMENT = 4


def whole_vmem():
    return pl.BlockSpec(memory_space=pltpu.VMEM)


def pack_kernel(parts, own, blocks, group, pre_ref, val_ref, post_ref, taps_ref, send_ref, gate_ref, sig_s, gate_s):
    rows = own * blocks
    for j in range(blocks):
        cols = pl.ds(W * j, W)
        product = pre_ref[:, cols].astype(jnp.float32) * val_ref[:, cols].astype(jnp.float32)
        gate = post_ref[:, cols].astype(jnp.float32)
        for i in range(parts):
            sig_s[i, pl.ds(own * j, own), :] = product[own * i : own * i + own, :]
            gate_s[i, pl.ds(own * j, own), :] = gate[own * i : own * i + own, :]
        row = taps_ref[:, cols]
        for i in range(parts):
            which = own * i // group
            sig_s[i, pl.ds(rows + j, 1), :] = row[which : which + 1, :]
    send_ref[...] = sig_s[...].astype(jnp.bfloat16)
    gate_ref[...] = gate_s[...].astype(jnp.bfloat16)


def pack(pre_gate, value, post_gate, taps, parts):
    channels, block = value.shape
    own = channels // parts
    group = channels // taps.shape[0]
    blocks = block // W
    rows = own * blocks
    return pl.pallas_call(
        functools.partial(pack_kernel, parts, own, blocks, group),
        out_shape=(
            jax.ShapeDtypeStruct((parts, rows + blocks, W), jnp.bfloat16),
            jax.ShapeDtypeStruct((parts, rows, W), jnp.bfloat16),
        ),
        in_specs=[whole_vmem()] * 4,
        out_specs=(whole_vmem(), whole_vmem()),
        scratch_shapes=[
            pltpu.VMEM((parts, rows + blocks, W), jnp.float32),
            pltpu.VMEM((parts, rows, W), jnp.float32),
        ],
        compiler_params=pltpu.CompilerParams(vmem_limit_bytes=32 * 2**20),
        name="pack",
    )(pre_gate, value, post_gate, taps)


def conv_kernel(own, step_rows, got_ref, skip_ref, out_ref, x_wide, x_tall, taps_s, t_a, t_b, total):
    parts, local, _ = got_ref.shape
    blocks = local // (own + 1)
    local_rows = own * blocks
    rows = parts * local_rows
    shifts = step_rows // own
    steps = rows // step_rows

    x_tall[0:step_rows, :] = jnp.zeros((step_rows, W), jnp.float32)
    taps_s[0:8, :] = jnp.zeros((8, W), jnp.float32)
    for p in range(parts):
        x_tall[step_rows + p * local_rows : step_rows + (p + 1) * local_rows, :] = got_ref[
            p, 0:local_rows, :
        ].astype(jnp.float32)
        taps_s[8 + p * blocks : 8 + (p + 1) * blocks, :] = got_ref[p, local_rows:local, :].astype(jnp.float32)
    taps_s[8 + parts * blocks :, :] = jnp.zeros((taps_s.shape[0] - 8 - parts * blocks, W), jnp.float32)
    for s in range(shifts):
        first = step_rows - own * s
        x_wide[:, W * s : W * (s + 1)] = x_tall[first : first + rows, :].astype(jnp.bfloat16)
    total[...] = jnp.zeros(total.shape, jnp.float32)

    lane = lax.broadcasted_iota(jnp.int32, (HALF, HALF), 1)
    sub = lax.broadcasted_iota(jnp.int32, (HALF, HALF), 0)
    upper = lane >= sub

    def rolled(near, block, half):
        row = near[8 + block : 9 + block, HALF * half : HALF * (half + 1)]
        wide = jnp.broadcast_to(row, (HALF, HALF))
        return pltpu.roll(wide, 0, 1, stride=1, stride_axis=0)

    def build(t_ref, step):
        near = taps_s[pl.ds(pl.multiple_of(step * shifts, 8), 8 + shifts), :]
        last = rolled(near, -1, 1)
        odd = jnp.where(upper, last, rolled(near, -1, 0)).astype(jnp.bfloat16)
        for s in range(shifts):
            first = rolled(near, s, 0)
            even = jnp.where(upper, first, last).astype(jnp.bfloat16)
            last = rolled(near, s, 1)
            t_ref[W * s + HALF : W * (s + 1), 0:HALF] = odd
            odd = jnp.where(upper, last, first).astype(jnp.bfloat16)
            t_ref[W * s : W * s + HALF, 0:HALF] = even
            t_ref[W * s + HALF : W * (s + 1), HALF:W] = even
            t_ref[W * s : W * s + HALF, HALF:W] = odd

    def accumulate(t_ref, step, count):
        at = pl.ds(pl.multiple_of(step * step_rows, step_rows), count)
        total[at, :] += jnp.dot(x_wide[0:count, :], t_ref[...], preferred_element_type=jnp.float32)

    build(t_a, 0)
    for segment in range(steps // SEGMENT):
        count = rows - segment * SEGMENT * step_rows

        def two(it, carry, segment=segment, count=count):
            step = segment * SEGMENT + 2 * it
            build(t_b, step + 1)
            accumulate(t_a, step, count)
            build(t_a, step + 2)
            accumulate(t_b, step + 1, count)
            return carry

        lax.fori_loop(0, SEGMENT // 2, two, 0)

    me = lax.axis_index("ctx")
    channel = lax.broadcasted_iota(jnp.int32, (step_rows, W), 0) % own
    weight = jnp.zeros((step_rows, W), jnp.float32)
    for c in range(own):
        weight = jnp.where(channel == c, skip_ref[own * me + c], weight)
    for at in range(0, rows, step_rows):
        out_ref[at : at + step_rows, :] = (
            total[at : at + step_rows, :] + weight * x_tall[step_rows + at : 2 * step_rows + at, :]
        )


def convolve(got, skip, own):
    parts, local, _ = got.shape
    blocks = local // (own + 1)
    rows = parts * blocks * own
    step_rows = 32 if own >= 4 else 16
    shifts = step_rows // own
    steps = rows // step_rows
    return pl.pallas_call(
        functools.partial(conv_kernel, own, step_rows),
        out_shape=jax.ShapeDtypeStruct((rows, W), jnp.float32),
        in_specs=[whole_vmem(), pl.BlockSpec(memory_space=pltpu.SMEM)],
        out_specs=whole_vmem(),
        scratch_shapes=[
            pltpu.VMEM((rows, W * shifts), jnp.bfloat16),
            pltpu.VMEM((rows + step_rows, W), jnp.float32),
            pltpu.VMEM((8 + (steps + 2) * shifts, W), jnp.float32),
            pltpu.VMEM((W * shifts, W), jnp.bfloat16),
            pltpu.VMEM((W * shifts, W), jnp.bfloat16),
            pltpu.VMEM((rows + SEGMENT * step_rows, W), jnp.float32),
        ],
        compiler_params=pltpu.CompilerParams(vmem_limit_bytes=48 * 2**20),
        cost_estimate=pl.CostEstimate(
            flops=rows * rows * W * W // own, bytes_accessed=4 * rows * W, transcendentals=0
        ),
        name="toeplitz",
    )(got, skip)


def gate_kernel(ctx_count, ch_count, z_ref, gate_ref, out_ref):
    rows = out_ref.shape[1]
    for k in range(ctx_count):
        for m in range(ch_count):
            at = (k * ch_count + m) * rows
            part = z_ref[at : at + rows, :] * gate_ref[at : at + rows, :].astype(jnp.float32)
            out_ref[m * ctx_count + k, :, :] = part.astype(jnp.bfloat16)


def gate_rows(z, gate, ctx_count, ch_count):
    count = z.shape[0] // (ctx_count * ch_count)
    if count % 16:
        mixed = (z * gate.astype(jnp.float32)).astype(jnp.bfloat16)
        return mixed.reshape(ctx_count, ch_count, count, W).swapaxes(0, 1).reshape(-1, count, W)
    return pl.pallas_call(
        functools.partial(gate_kernel, ctx_count, ch_count),
        out_shape=jax.ShapeDtypeStruct((ctx_count * ch_count, count, W), jnp.bfloat16),
        in_specs=[whole_vmem()] * 2,
        out_specs=whole_vmem(),
        compiler_params=pltpu.CompilerParams(vmem_limit_bytes=16 * 2**20),
        name="gate",
    )(z, gate)


def unpack_kernel(own, got_ref, out_ref, tall):
    sources, rows, _ = got_ref.shape
    for p in range(sources):
        part = got_ref[p].astype(jnp.float32)
        for j in range(rows // own):
            tall[pl.ds(own * p, own), W * j : W * (j + 1)] = part[own * j : own * (j + 1), :]
    out_ref[...] = tall[...].astype(jnp.bfloat16)


def unpack(got, own):
    sources, rows, _ = got.shape
    shape = (sources * own, rows // own * W)
    if rows % 16:
        return got.reshape(sources, rows // own, own, W).swapaxes(1, 2).reshape(shape)
    return pl.pallas_call(
        functools.partial(unpack_kernel, own),
        out_shape=jax.ShapeDtypeStruct(shape, jnp.bfloat16),
        in_specs=[whole_vmem()],
        out_specs=whole_vmem(),
        scratch_shapes=[pltpu.VMEM(shape, jnp.float32)],
        compiler_params=pltpu.CompilerParams(vmem_limit_bytes=16 * 2**20),
        name="unpack",
    )(got)


def body(pre_gate, value, post_gate, filter_taps, skip):
    ctx_count = lax.axis_size("ctx")
    ch_count = lax.axis_size("ch")
    own = value.shape[0] // ctx_count
    send, gate = pack(pre_gate, value, post_gate, filter_taps, ctx_count)
    got = lax.all_to_all(send, "ctx", split_axis=0, concat_axis=0, tiled=True)
    gate = lax.all_to_all(gate, "ctx", split_axis=0, concat_axis=0, tiled=True)
    z = convolve(got, skip, own)
    mixed = gate_rows(z, gate.reshape(z.shape), ctx_count, ch_count)
    mixed = lax.all_to_all(mixed, ("ch", "ctx"), split_axis=0, concat_axis=0, tiled=True)
    return unpack(mixed, own)


def solution(mesh):
    placed = (P("ch", "ctx"), P("ch", "ctx"), P("ch", "ctx"), P("ch", "ctx"), P("ch"))
    return jax.shard_map(
        body, mesh=mesh, in_specs=placed, out_specs=P(None, ("ctx", "ch")), check_vma=False
    )
```

```python
import functools

import jax
import jax.numpy as jnp
from jax import lax
from jax.experimental import pallas as pl
from jax.experimental.pallas import tpu as pltpu
from jax.sharding import PartitionSpec as P

W = 256
HALF = 128
TILE = 16
CUTS = 4


def whole_vmem():
    return pl.BlockSpec(memory_space=pltpu.VMEM)


def in_hbm():
    return pl.BlockSpec(memory_space=pltpu.HBM)


def pack_signal_kernel(parts, own, blocks, group, pre_ref, val_ref, taps_ref, *rest):
    out_refs = rest[:parts]
    pre_s, val_s, taps_s, tall, sems = rest[parts:]
    rows = own * blocks
    width = blocks * W // CUTS
    copies = []
    for q in range(CUTS):
        cols = pl.ds(q * width, width)
        copies.append(
            [
                pltpu.make_async_copy(pre_ref.at[:, cols], pre_s.at[:, cols], sems.at[q, 0]),
                pltpu.make_async_copy(val_ref.at[:, cols], val_s.at[:, cols], sems.at[q, 1]),
            ]
        )
    taps_copy = pltpu.make_async_copy(taps_ref, taps_s, sems.at[CUTS, 0])
    taps_copy.start()
    for pair in copies:
        for copy in pair:
            copy.start()
    taps_copy.wait()
    for j in range(blocks):
        row = taps_s[:, W * j : W * (j + 1)]
        for i in range(parts):
            which = own * i // group
            tall[i, rows + j : rows + j + 1, :] = row[which : which + 1, :]
    for j in range(blocks):
        if j % (blocks // CUTS) == 0:
            for copy in copies[j // (blocks // CUTS)]:
                copy.wait()
        cols = slice(W * j, W * (j + 1))
        product = pre_s[:, cols].astype(jnp.float32) * val_s[:, cols].astype(jnp.float32)
        for i in range(parts):
            tall[i, own * j : own * (j + 1), :] = product[own * i : own * (i + 1), :]
    me = lax.axis_index("ctx")
    for d in range(parts):
        out_refs[d][...] = tall[jnp.bitwise_xor(me, d)].astype(jnp.bfloat16)


def pack_signal(pre_gate, value, taps, parts):
    channels, block = value.shape
    own = channels // parts
    group = channels // taps.shape[0]
    blocks = block // W
    rows = own * blocks + blocks
    return pl.pallas_call(
        functools.partial(pack_signal_kernel, parts, own, blocks, group),
        out_shape=[jax.ShapeDtypeStruct((rows, W), jnp.bfloat16)] * parts,
        in_specs=[in_hbm()] * 3,
        out_specs=[whole_vmem()] * parts,
        scratch_shapes=[
            pltpu.VMEM(pre_gate.shape, jnp.bfloat16),
            pltpu.VMEM(value.shape, jnp.bfloat16),
            pltpu.VMEM(taps.shape, jnp.float32),
            pltpu.VMEM((parts, rows, W), jnp.float32),
            pltpu.SemaphoreType.DMA((CUTS + 1, 2)),
        ],
        compiler_params=pltpu.CompilerParams(vmem_limit_bytes=24 * 2**20),
        name="pack_signal",
    )(pre_gate, value, taps)


def pack_gate_kernel(parts, own, blocks, post_ref, *rest):
    out_refs = rest[:parts]
    post_s, tall, sems = rest[parts:]
    width = blocks * W // CUTS
    copies = []
    for q in range(CUTS):
        cols = pl.ds(q * width, width)
        copies.append(pltpu.make_async_copy(post_ref.at[:, cols], post_s.at[:, cols], sems.at[q]))
    for copy in copies:
        copy.start()
    for j in range(blocks):
        if j % (blocks // CUTS) == 0:
            copies[j // (blocks // CUTS)].wait()
        gate = post_s[:, W * j : W * (j + 1)].astype(jnp.float32)
        for i in range(parts):
            tall[i, own * j : own * (j + 1), :] = gate[own * i : own * (i + 1), :]
    me = lax.axis_index("ctx")
    for d in range(parts):
        out_refs[d][...] = tall[jnp.bitwise_xor(me, d)].astype(jnp.bfloat16)


def pack_gate(post_gate, parts):
    channels, block = post_gate.shape
    own = channels // parts
    blocks = block // W
    rows = own * blocks
    return pl.pallas_call(
        functools.partial(pack_gate_kernel, parts, own, blocks),
        out_shape=[jax.ShapeDtypeStruct((rows, W), jnp.bfloat16)] * parts,
        in_specs=[in_hbm()],
        out_specs=[whole_vmem()] * parts,
        scratch_shapes=[
            pltpu.VMEM(post_gate.shape, jnp.bfloat16),
            pltpu.VMEM((parts, rows, W), jnp.float32),
            pltpu.SemaphoreType.DMA((CUTS,)),
        ],
        compiler_params=pltpu.CompilerParams(vmem_limit_bytes=24 * 2**20),
        name="pack_gate",
    )(post_gate)


def swap_all(pieces):
    parts = len(pieces)
    got = [pieces[0]]
    for d in range(1, parts):
        got.append(lax.ppermute(pieces[d], "ctx", [(i, i ^ d) for i in range(parts)]))
    return got


def conv_kernel(own, step_rows, parts, skip_ref, *rest):
    got_refs = rest[:parts]
    out_ref, x_wide, x_tall, taps_s, t_a, t_b, total = rest[parts:]
    local = got_refs[0].shape[0]
    blocks = local // (own + 1)
    local_rows = own * blocks
    rows = parts * local_rows
    shifts = step_rows // own
    steps = rows // step_rows
    fine = TILE // own
    tiles = shifts // fine
    head = TILE * (tiles - 1)
    me = lax.axis_index("ctx")

    x_tall[0:TILE, :] = jnp.zeros((TILE, W), jnp.float32)
    taps_s[0:8, :] = jnp.zeros((8, W), jnp.float32)
    for d in range(parts):
        p = jnp.bitwise_xor(me, d)
        x_tall[pl.ds(pl.multiple_of(TILE + p * local_rows, 8), local_rows), :] = got_refs[d][
            0:local_rows, :
        ].astype(jnp.float32)
        taps_s[pl.ds(pl.multiple_of(8 + p * blocks, 8), blocks), :] = got_refs[d][local_rows:local, :].astype(
            jnp.float32
        )
    if head:
        x_wide[0:head, :] = jnp.zeros((head, W * fine), jnp.bfloat16)
    for s in range(fine):
        first = TILE - own * s
        x_wide[head : head + rows, W * s : W * (s + 1)] = x_tall[first : first + rows, :].astype(jnp.bfloat16)

    lane = lax.broadcasted_iota(jnp.int32, (HALF, HALF), 1)
    sub = lax.broadcasted_iota(jnp.int32, (HALF, HALF), 0)
    upper = lane >= sub

    def rolled(near, block, half):
        row = near[8 + block : 9 + block, HALF * half : HALF * (half + 1)]
        wide = jnp.broadcast_to(row, (HALF, HALF))
        return pltpu.roll(wide, 0, 1, stride=1, stride_axis=0)

    def build(t_ref, pair):
        near = taps_s[2 * pair * shifts : 2 * (pair + 1) * shifts + 8, :]
        last = rolled(near, -1, 1)
        odd = jnp.where(upper, last, rolled(near, -1, 0)).astype(jnp.bfloat16)
        for s in range(2 * shifts):
            first = rolled(near, s, 0)
            even = jnp.where(upper, first, last).astype(jnp.bfloat16)
            last = rolled(near, s, 1)
            row = W * (s % shifts)
            col = W * (s // shifts)
            t_ref[row + HALF : row + W, col : col + HALF] = odd
            odd = jnp.where(upper, last, first).astype(jnp.bfloat16)
            t_ref[row : row + HALF, col : col + HALF] = even
            t_ref[row + HALF : row + W, col + HALF : col + W] = even
            t_ref[row : row + HALF, col + HALF : col + W] = odd

    def accumulate(t_ref, pair):
        at = 2 * pair * step_rows
        count = rows - at
        depth = W * fine
        product = jnp.dot(
            x_wide[head : head + count, :], t_ref[0:depth, :], preferred_element_type=jnp.float32
        )
        for u in range(1, tiles):
            first = head - TILE * u
            product += jnp.dot(
                x_wide[first : first + count, :],
                t_ref[depth * u : depth * (u + 1), :],
                preferred_element_type=jnp.float32,
            )
        if pair == 0:
            total[...] = product[:, 0:W]
        else:
            total[at:rows, :] += product[:, 0:W]
        total[at + step_rows : rows, :] += product[0 : count - step_rows, W : 2 * W]

    build(t_a, 0)
    for pair in range(steps // 2):
        now, later = (t_a, t_b) if pair % 2 == 0 else (t_b, t_a)
        if pair + 1 < steps // 2:
            build(later, pair + 1)
        accumulate(now, pair)

    channel = lax.broadcasted_iota(jnp.int32, (step_rows, W), 0) % own
    weight = jnp.zeros((step_rows, W), jnp.float32)
    for c in range(own):
        weight = jnp.where(channel == c, skip_ref[own * me + c], weight)
    for at in range(0, rows, step_rows):
        out_ref[at : at + step_rows, :] = (
            total[at : at + step_rows, :] + weight * x_tall[TILE + at : TILE + at + step_rows, :]
        )


def convolve(got, skip, own):
    parts = len(got)
    local, _ = got[0].shape
    blocks = local // (own + 1)
    rows = parts * blocks * own
    step_rows = 32 if own >= 4 else TILE
    shifts = step_rows // own
    steps = rows // step_rows
    head = step_rows - TILE
    return pl.pallas_call(
        functools.partial(conv_kernel, own, step_rows, parts),
        out_shape=jax.ShapeDtypeStruct((rows, W), jnp.float32),
        in_specs=[pl.BlockSpec(memory_space=pltpu.SMEM)] + [whole_vmem()] * parts,
        out_specs=whole_vmem(),
        scratch_shapes=[
            pltpu.VMEM((head + rows, W * (TILE // own)), jnp.bfloat16),
            pltpu.VMEM((rows + TILE, W), jnp.float32),
            pltpu.VMEM((8 + steps * shifts, W), jnp.float32),
            pltpu.VMEM((W * shifts, 2 * W), jnp.bfloat16),
            pltpu.VMEM((W * shifts, 2 * W), jnp.bfloat16),
            pltpu.VMEM((rows, W), jnp.float32),
        ],
        compiler_params=pltpu.CompilerParams(vmem_limit_bytes=48 * 2**20),
        cost_estimate=pl.CostEstimate(
            flops=rows * rows * W * W // own, bytes_accessed=4 * rows * W, transcendentals=0
        ),
        name="toeplitz",
    )(skip, *got)


def gate_kernel(ctx_count, ch_count, z_ref, *rest):
    gate_refs = rest[:ctx_count]
    out_ref = rest[ctx_count]
    rows = out_ref.shape[1]
    me = lax.axis_index("ctx")
    for d in range(ctx_count):
        k = jnp.bitwise_xor(me, d)
        for m in range(ch_count):
            at = pl.multiple_of((k * ch_count + m) * rows, rows)
            part = z_ref[pl.ds(at, rows), :] * gate_refs[d][m * rows : (m + 1) * rows, :].astype(jnp.float32)
            out_ref[m * ctx_count + k] = part.astype(jnp.bfloat16)


def gate_rows(z, gates, ctx_count, ch_count):
    count = z.shape[0] // (ctx_count * ch_count)
    if count % TILE:
        me = lax.axis_index("ctx")
        order = jnp.bitwise_xor(me, jnp.arange(ctx_count))
        gate = jnp.stack(gates)[order].reshape(z.shape)
        mixed = (z * gate.astype(jnp.float32)).astype(jnp.bfloat16)
        return mixed.reshape(ctx_count, ch_count, count, W).swapaxes(0, 1).reshape(-1, count, W)
    return pl.pallas_call(
        functools.partial(gate_kernel, ctx_count, ch_count),
        out_shape=jax.ShapeDtypeStruct((ctx_count * ch_count, count, W), jnp.bfloat16),
        in_specs=[whole_vmem()] * (1 + ctx_count),
        out_specs=whole_vmem(),
        compiler_params=pltpu.CompilerParams(vmem_limit_bytes=16 * 2**20),
        name="gate",
    )(z, *gates)


def unpack_kernel(own, got_ref, out_ref, tall):
    sources, rows, _ = got_ref.shape
    for p in range(sources):
        part = got_ref[p].astype(jnp.float32)
        for j in range(rows // own):
            tall[own * p : own * (p + 1), W * j : W * (j + 1)] = part[own * j : own * (j + 1), :]
    out_ref[...] = tall[...].astype(jnp.bfloat16)


def unpack(got, own):
    sources, rows, _ = got.shape
    shape = (sources * own, rows // own * W)
    if rows % TILE:
        return got.reshape(sources, rows // own, own, W).swapaxes(1, 2).reshape(shape)
    return pl.pallas_call(
        functools.partial(unpack_kernel, own),
        out_shape=jax.ShapeDtypeStruct(shape, jnp.bfloat16),
        in_specs=[whole_vmem()],
        out_specs=whole_vmem(),
        scratch_shapes=[pltpu.VMEM(shape, jnp.float32)],
        compiler_params=pltpu.CompilerParams(vmem_limit_bytes=16 * 2**20),
        name="unpack",
    )(got)


def body(pre_gate, value, post_gate, filter_taps, skip):
    ctx_count = lax.axis_size("ctx")
    ch_count = lax.axis_size("ch")
    own = value.shape[0] // ctx_count
    got = swap_all(pack_signal(pre_gate, value, filter_taps, ctx_count))
    gates = swap_all(pack_gate(post_gate, ctx_count))
    z = convolve(got, skip, own)
    mixed = gate_rows(z, gates, ctx_count, ch_count)
    mixed = lax.all_to_all(mixed, ("ch", "ctx"), split_axis=0, concat_axis=0, tiled=True)
    return unpack(mixed, own)


def solution(mesh):
    placed = (P("ch", "ctx"), P("ch", "ctx"), P("ch", "ctx"), P("ch", "ctx"), P("ch"))
    return jax.shard_map(
        body, mesh=mesh, in_specs=placed, out_specs=P(None, ("ctx", "ch")), check_vma=False
    )
```

```python
import functools

import jax
import jax.numpy as jnp
import numpy as np
from jax import lax
from jax.experimental import pallas as pl
from jax.experimental.pallas import tpu as pltpu
from jax.sharding import PartitionSpec as P

W = 256
LANES = 128
TILE = 16
CHUNK = 64


def whole_vmem():
    return pl.BlockSpec(memory_space=pltpu.VMEM)


def dft_tables(blocks):
    length = blocks * W
    k = np.arange(blocks)[:, None]
    angle = 2 * np.pi * ((4 * k + 1) * np.arange(blocks)[None, :] % (4 * blocks)) / (4 * blocks)
    outer = np.concatenate([np.cos(angle), -np.sin(angle)], 0)
    turn = 2 * np.pi * ((4 * k + 1) * np.arange(W)[None, :]) / (4 * length)
    near = 2 * np.pi * (np.arange(W)[:, None] * np.arange(W)[None, :] % W) / W
    inner = np.concatenate([np.cos(near), np.sin(near)], 0)
    turns = np.concatenate([np.cos(turn), np.sin(turn)], 1)
    return [jnp.asarray(table, jnp.float32) for table in (outer, outer.T, inner, turns)]


def spread(flat, first, count, stride, value):
    for h in range(W // LANES):
        flat[h, pl.ds(first, count, stride=stride), :] = value[:, LANES * h : LANES * (h + 1)]


def joined(flat, first, count):
    return jnp.concatenate([flat[h, first : first + count, :] for h in range(W // LANES)], 1)


def pack_signal_kernel(own, blocks, group, signal_ref, taps_ref, out_ref, flat, taps_flat):
    parts = out_ref.shape[0]
    rows = own * blocks
    for j in range(blocks):
        spread(taps_flat, j, taps_ref.shape[0], blocks, taps_ref[:, W * j : W * (j + 1)])
        spread(flat, j, own * parts, blocks, signal_ref[:, W * j : W * (j + 1)].astype(jnp.float32))
    for i in range(parts):
        out_ref[i, 0:rows, :] = joined(flat, i * rows, rows).astype(jnp.bfloat16)
        which = own * i // group
        out_ref[i, rows : rows + blocks, :] = joined(taps_flat, which * blocks, blocks).astype(jnp.bfloat16)


def pack_signal(signal, taps, parts):
    channels, block = signal.shape
    own = channels // parts
    group = channels // taps.shape[0]
    blocks = block // W
    return pl.pallas_call(
        functools.partial(pack_signal_kernel, own, blocks, group),
        out_shape=jax.ShapeDtypeStruct((parts, (own + 1) * blocks, W), jnp.bfloat16),
        in_specs=[whole_vmem()] * 2,
        out_specs=whole_vmem(),
        scratch_shapes=[
            pltpu.VMEM((W // LANES, channels * blocks, LANES), jnp.float32),
            pltpu.VMEM((W // LANES, taps.shape[0] * blocks, LANES), jnp.float32),
        ],
        compiler_params=pltpu.CompilerParams(vmem_limit_bytes=24 * 2**20),
        name="pack_signal",
    )(signal, taps)


def pack_gate_kernel(blocks, gate_ref, out_ref, flat):
    parts, rows, _ = out_ref.shape
    for j in range(blocks):
        spread(flat, j, parts * rows // blocks, blocks, gate_ref[:, W * j : W * (j + 1)].astype(jnp.float32))
    for i in range(parts):
        out_ref[i] = joined(flat, i * rows, rows).astype(jnp.bfloat16)


def pack_gate(post_gate, parts):
    channels, block = post_gate.shape
    blocks = block // W
    return pl.pallas_call(
        functools.partial(pack_gate_kernel, blocks),
        out_shape=jax.ShapeDtypeStruct((parts, channels // parts * blocks, W), jnp.bfloat16),
        in_specs=[whole_vmem()],
        out_specs=whole_vmem(),
        scratch_shapes=[pltpu.VMEM((W // LANES, channels * blocks, LANES), jnp.float32)],
        compiler_params=pltpu.CompilerParams(vmem_limit_bytes=24 * 2**20),
        name="pack_gate",
    )(post_gate)


def conv_kernel(own, skip_ref, got_ref, outer_ref, back_ref, inner_ref, turns_ref, out_ref, x_all, r_all, ahead, rear):
    parts, local, _ = got_ref.shape
    near = local // (own + 1)
    blocks = parts * near
    length = blocks * W
    for p in range(parts):
        for c in range(own + 1):
            x_all[p * near : (p + 1) * near, W * c : W * (c + 1)] = got_ref[p, c * near : (c + 1) * near, :]

    near_cos, near_sin = inner_ref[0:W, :].astype(jnp.bfloat16), inner_ref[W:, :].astype(jnp.bfloat16)
    for table, sign in ((ahead, -1), (rear, 1)):
        table[0:W, 0:W] = near_cos
        table[0:W, W:] = near_sin * sign
        table[W:, 0:W] = near_sin * -sign
        table[W:, W:] = near_cos

    def dot(left, right):
        return jnp.dot(left, right, preferred_element_type=jnp.float32)

    for first in range(0, blocks, CHUNK):
        here = slice(first, first + CHUNK)
        there = slice(blocks + first, blocks + first + CHUNK)
        real = dot(outer_ref[here, :].astype(jnp.bfloat16), x_all[...])
        imag = dot(outer_ref[there, :].astype(jnp.bfloat16), x_all[...])
        turn_cos, turn_sin = turns_ref[here, 0:W], turns_ref[here, W:]
        rows = []
        for c in range(own + 1):
            re, im = real[:, W * c : W * (c + 1)], imag[:, W * c : W * (c + 1)]
            pair = [re * turn_cos + im * turn_sin, im * turn_cos - re * turn_sin]
            rows.append(jnp.concatenate(pair, 1).astype(jnp.bfloat16))
        spectrum = dot(jnp.concatenate(rows, 0), ahead[...])
        filt_re = spectrum[CHUNK * own :, 0:W] * (1.0 / length)
        filt_im = spectrum[CHUNK * own :, W:] * (1.0 / length)
        rows = []
        for c in range(own):
            part = spectrum[CHUNK * c : CHUNK * (c + 1), :]
            re, im = part[:, 0:W], part[:, W:]
            pair = [re * filt_re - im * filt_im, re * filt_im + im * filt_re]
            rows.append(jnp.concatenate(pair, 1).astype(jnp.bfloat16))
        middle = dot(jnp.concatenate(rows, 0), rear[...])
        for c in range(own):
            part = middle[CHUNK * c : CHUNK * (c + 1), :]
            re, im = part[:, 0:W], part[:, W:]
            cols = slice(W * c, W * (c + 1))
            r_all[here, cols] = (re * turn_cos - im * turn_sin).astype(jnp.bfloat16)
            r_all[there, cols] = (re * turn_sin + im * turn_cos).astype(jnp.bfloat16)

    me = lax.axis_index("ctx")
    for c in range(own):
        cols = slice(W * c, W * (c + 1))
        conv = dot(back_ref[...].astype(jnp.bfloat16), r_all[:, cols])
        out_ref[c] = conv + skip_ref[own * me + c] * x_all[:, cols].astype(jnp.float32)


def convolve(got, skip, own):
    parts, local, _ = got.shape
    blocks = parts * (local // (own + 1))
    tables = dft_tables(blocks)
    steps = 8 * blocks * W * W * (3 * own + 2)
    return pl.pallas_call(
        functools.partial(conv_kernel, own),
        out_shape=jax.ShapeDtypeStruct((own, blocks, W), jnp.float32),
        in_specs=[pl.BlockSpec(memory_space=pltpu.SMEM)] + [whole_vmem()] * (1 + len(tables)),
        out_specs=whole_vmem(),
        scratch_shapes=[
            pltpu.VMEM((blocks, W * (own + 1)), jnp.bfloat16),
            pltpu.VMEM((2 * blocks, W * own), jnp.bfloat16),
            pltpu.VMEM((2 * W, 2 * W), jnp.bfloat16),
            pltpu.VMEM((2 * W, 2 * W), jnp.bfloat16),
        ],
        compiler_params=pltpu.CompilerParams(vmem_limit_bytes=32 * 2**20),
        cost_estimate=pl.CostEstimate(flops=steps, bytes_accessed=4 * own * blocks * W, transcendentals=0),
        name="convolve",
    )(skip, got, *tables)


def gate_kernel(ch_count, z_ref, gate_ref, out_ref):
    own = z_ref.shape[0]
    ctx_count, local, _ = gate_ref.shape
    near = local // own
    some = near // ch_count
    for k in range(ctx_count):
        parts = []
        for c in range(own):
            gate = gate_ref[k, c * near : (c + 1) * near, :].astype(jnp.float32)
            parts.append(gate * z_ref[c, k * near : (k + 1) * near, :])
        for m in range(ch_count):
            rows = [part[m * some : (m + 1) * some, :] for part in parts]
            out_ref[m * ctx_count + k] = jnp.concatenate(rows, 0).astype(jnp.bfloat16)


def gate_rows(z, gate, ch_count):
    own = z.shape[0]
    ctx_count, local, _ = gate.shape
    near = local // own
    some = near // ch_count
    if some % 8 or own * some % TILE:
        gate = gate.reshape(ctx_count, own, near, W).swapaxes(0, 1).reshape(z.shape)
        mixed = (z * gate.astype(jnp.float32)).astype(jnp.bfloat16)
        mixed = mixed.reshape(own, ctx_count, ch_count, some, W)
        return mixed.transpose(2, 1, 0, 3, 4).reshape(-1, own * some, W)
    return pl.pallas_call(
        functools.partial(gate_kernel, ch_count),
        out_shape=jax.ShapeDtypeStruct((ctx_count * ch_count, own * some, W), jnp.bfloat16),
        in_specs=[whole_vmem()] * 2,
        out_specs=whole_vmem(),
        compiler_params=pltpu.CompilerParams(vmem_limit_bytes=16 * 2**20),
        name="gate",
    )(z, gate)


def unpack_kernel(own, got_ref, out_ref, flat):
    sources, rows, _ = got_ref.shape
    some = rows // own
    for p in range(sources):
        part = got_ref[p].astype(jnp.float32)
        for h in range(W // LANES):
            flat[h, p * rows : (p + 1) * rows, :] = part[:, LANES * h : LANES * (h + 1)]
    for j in range(some):
        for h in range(W // LANES):
            part = flat[h, pl.ds(j, sources * own, stride=some), :]
            first = W * j + LANES * h
            out_ref[:, first : first + LANES] = part.astype(jnp.bfloat16)


def unpack(got, own):
    sources, rows, _ = got.shape
    shape = (sources * own, rows // own * W)
    if rows % TILE:
        return got.reshape(shape)
    return pl.pallas_call(
        functools.partial(unpack_kernel, own),
        out_shape=jax.ShapeDtypeStruct(shape, jnp.bfloat16),
        in_specs=[whole_vmem()],
        out_specs=whole_vmem(),
        scratch_shapes=[pltpu.VMEM((W // LANES, sources * rows, LANES), jnp.float32)],
        compiler_params=pltpu.CompilerParams(vmem_limit_bytes=16 * 2**20),
        name="unpack",
    )(got)


def body(pre_gate, value, post_gate, filter_taps, skip):
    ctx_count = lax.axis_size("ctx")
    ch_count = lax.axis_size("ch")
    own = value.shape[0] // ctx_count
    signal = (pre_gate.astype(jnp.float32) * value.astype(jnp.float32)).astype(jnp.bfloat16)
    send = pack_signal(signal, filter_taps, ctx_count)
    got = lax.all_to_all(send, "ctx", split_axis=0, concat_axis=0, tiled=True)
    post_gate, _ = lax.optimization_barrier((post_gate, send))
    gate = pack_gate(post_gate, ctx_count)
    gate = lax.all_to_all(gate, "ctx", split_axis=0, concat_axis=0, tiled=True)
    z = convolve(got, skip, own)
    mixed = gate_rows(z, gate, ch_count)
    mixed = lax.all_to_all(mixed, ("ch", "ctx"), split_axis=0, concat_axis=0, tiled=True)
    return unpack(mixed, own)


def solution(mesh):
    placed = (P("ch", "ctx"), P("ch", "ctx"), P("ch", "ctx"), P("ch", "ctx"), P("ch"))
    return jax.shard_map(
        body, mesh=mesh, in_specs=placed, out_specs=P(None, ("ctx", "ch")), check_vma=False
    )
```

```python
import functools

import jax
import jax.numpy as jnp
import numpy as np
from jax import lax
from jax.experimental import pallas as pl
from jax.experimental.pallas import tpu as pltpu
from jax.sharding import PartitionSpec as P

W = 256
LANES = 128
TILE = 16
CHUNK = 64


def whole_vmem():
    return pl.BlockSpec(memory_space=pltpu.VMEM)


def dft_tables(blocks):
    length = blocks * W
    k = np.arange(blocks)[:, None]
    angle = 2 * np.pi * ((4 * k + 1) * np.arange(blocks)[None, :] % (4 * blocks)) / (4 * blocks)
    outer = np.concatenate([np.cos(angle), -np.sin(angle)], 0)
    turn = 2 * np.pi * ((4 * k + 1) * np.arange(W)[None, :]) / (4 * length)
    near = 2 * np.pi * (np.arange(W)[:, None] * np.arange(W)[None, :] % W) / W
    inner = np.concatenate([np.cos(near), np.sin(near)], 0)
    turns = np.concatenate([np.cos(turn), np.sin(turn)], 1)
    return [jnp.asarray(table, jnp.float32) for table in (outer, outer.T, inner, turns)]


def spread(flat, first, count, stride, value):
    for h in range(W // LANES):
        flat[h, pl.ds(first, count, stride=stride), :] = value[:, LANES * h : LANES * (h + 1)]


def joined(flat, first, count):
    return jnp.concatenate([flat[h, pl.ds(first, count), :] for h in range(W // LANES)], 1)


def pack_signal_kernel(own, blocks, group, pre_ref, val_ref, taps_ref, out_ref, flat, taps_flat):
    step = pl.program_id(0)
    rows = own * blocks
    channels = pre_ref.shape[0]

    @pl.when(step == 0)
    def _():
        for j in range(blocks):
            spread(taps_flat, j, taps_ref.shape[0], blocks, taps_ref[:, W * j : W * (j + 1)])

    for j in range(blocks):
        cols = slice(W * j, W * (j + 1))
        product = pre_ref[:, cols].astype(jnp.float32) * val_ref[:, cols].astype(jnp.float32)
        spread(flat, j, channels, blocks, product)
    for i in range(channels // own):
        out_ref[i, 0:rows, :] = joined(flat, i * rows, rows).astype(jnp.bfloat16)
        which = (step * channels + own * i) // group
        taps = joined(taps_flat, pl.multiple_of(which * blocks, 8), blocks)
        out_ref[i, rows : rows + blocks, :] = taps.astype(jnp.bfloat16)


def pack_signal(pre_gate, value, taps, parts):
    channels, block = value.shape
    own = channels // parts
    group = channels // taps.shape[0]
    blocks = block // W
    some = min(TILE, channels)
    return pl.pallas_call(
        functools.partial(pack_signal_kernel, own, blocks, group),
        grid=(channels // some,),
        out_shape=jax.ShapeDtypeStruct((parts, (own + 1) * blocks, W), jnp.bfloat16),
        in_specs=[pl.BlockSpec((some, block), lambda s: (s, 0))] * 2 + [pl.BlockSpec(taps.shape, lambda s: (0, 0))],
        out_specs=pl.BlockSpec((some // own, (own + 1) * blocks, W), lambda s: (s, 0, 0)),
        scratch_shapes=[
            pltpu.VMEM((W // LANES, some * blocks, LANES), jnp.float32),
            pltpu.VMEM((W // LANES, taps.shape[0] * blocks, LANES), jnp.float32),
        ],
        compiler_params=pltpu.CompilerParams(vmem_limit_bytes=60 * 2**20),
        name="pack_signal",
    )(pre_gate, value, taps)


def split_gate_kernel(gate_ref, *out_refs):
    me = lax.axis_index("ch")
    width = out_refs[0].shape[1]
    for d, out_ref in enumerate(out_refs):
        first = pl.multiple_of(jnp.bitwise_xor(me, d) * width, LANES)
        out_ref[...] = gate_ref[:, pl.ds(first, width)]


def split_gate(post_gate, parts):
    channels, block = post_gate.shape
    return pl.pallas_call(
        split_gate_kernel,
        out_shape=[jax.ShapeDtypeStruct((channels, block // parts), jnp.bfloat16)] * parts,
        in_specs=[whole_vmem()],
        out_specs=[whole_vmem()] * parts,
        compiler_params=pltpu.CompilerParams(vmem_limit_bytes=24 * 2**20),
        name="split_gate",
    )(post_gate)


def tables_kernel(outer_ref, back_ref, inner_ref, outer_out, back_out, ahead, rear):
    outer_out[...] = outer_ref[...].astype(jnp.bfloat16)
    back_out[...] = back_ref[...].astype(jnp.bfloat16)
    near_cos, near_sin = inner_ref[0:W, :].astype(jnp.bfloat16), inner_ref[W:, :].astype(jnp.bfloat16)
    for table, sign in ((ahead, -1), (rear, 1)):
        table[0:W, 0:W] = near_cos
        table[0:W, W:] = near_sin * sign
        table[W:, 0:W] = near_sin * -sign
        table[W:, W:] = near_cos


def make_tables(outer, back, inner):
    shapes = (outer.shape, back.shape, (2 * W, 2 * W), (2 * W, 2 * W))
    return pl.pallas_call(
        tables_kernel,
        out_shape=[jax.ShapeDtypeStruct(shape, jnp.bfloat16) for shape in shapes],
        in_specs=[whole_vmem()] * 3,
        out_specs=[whole_vmem()] * 4,
        compiler_params=pltpu.CompilerParams(vmem_limit_bytes=24 * 2**20),
        name="make_tables",
    )(outer, back, inner)


def conv_kernel(own, skip_ref, got_ref, outer_ref, back_ref, ahead, rear, turns_ref, out_ref, x_all, r_all, z_all):
    parts, local, _ = got_ref.shape
    near = local // (own + 1)
    blocks = parts * near
    length = blocks * W
    for p in range(parts):
        for c in range(own + 1):
            x_all[p * near : (p + 1) * near, W * c : W * (c + 1)] = got_ref[p, c * near : (c + 1) * near, :]

    def dot(left, right):
        return jnp.dot(left, right, preferred_element_type=jnp.float32)

    for first in range(0, blocks, CHUNK):
        here = slice(first, first + CHUNK)
        there = slice(blocks + first, blocks + first + CHUNK)
        real = dot(outer_ref[here, :], x_all[...])
        imag = dot(outer_ref[there, :], x_all[...])
        turn_cos, turn_sin = turns_ref[here, 0:W], turns_ref[here, W:]
        rows = []
        for c in range(own + 1):
            re, im = real[:, W * c : W * (c + 1)], imag[:, W * c : W * (c + 1)]
            pair = [re * turn_cos + im * turn_sin, im * turn_cos - re * turn_sin]
            rows.append(jnp.concatenate(pair, 1).astype(jnp.bfloat16))
        spectrum = dot(jnp.concatenate(rows, 0), ahead[...])
        filt_re = spectrum[CHUNK * own :, 0:W] * (1.0 / length)
        filt_im = spectrum[CHUNK * own :, W:] * (1.0 / length)
        rows = []
        for c in range(own):
            part = spectrum[CHUNK * c : CHUNK * (c + 1), :]
            re, im = part[:, 0:W], part[:, W:]
            pair = [re * filt_re - im * filt_im, re * filt_im + im * filt_re]
            rows.append(jnp.concatenate(pair, 1).astype(jnp.bfloat16))
        middle = dot(jnp.concatenate(rows, 0), rear[...])
        for c in range(own):
            part = middle[CHUNK * c : CHUNK * (c + 1), :]
            re, im = part[:, 0:W], part[:, W:]
            cols = slice(W * c, W * (c + 1))
            r_all[here, cols] = (re * turn_cos - im * turn_sin).astype(jnp.bfloat16)
            r_all[there, cols] = (re * turn_sin + im * turn_cos).astype(jnp.bfloat16)

    me = lax.axis_index("ctx")
    for c in range(own):
        cols = slice(W * c, W * (c + 1))
        conv = dot(back_ref[...], r_all[:, cols])
        z_all[c] = conv + skip_ref[own * me + c] * x_all[:, cols].astype(jnp.float32)
    some = out_ref.shape[1] // own
    ch_count = near // some
    for k in range(parts):
        for m in range(ch_count):
            first = k * near + m * some
            rows = [z_all[c, first : first + some, :] for c in range(own)]
            out_ref[m * parts + k] = jnp.concatenate(rows, 0).astype(jnp.bfloat16)


def convolve(got, skip, tables, own, ch_count):
    parts, local, _ = got.shape
    blocks = parts * (local // (own + 1))
    steps = 8 * blocks * W * W * (3 * own + 2)
    owners = parts * ch_count
    return pl.pallas_call(
        functools.partial(conv_kernel, own),
        out_shape=jax.ShapeDtypeStruct((owners, own * blocks // owners, W), jnp.bfloat16),
        in_specs=[pl.BlockSpec(memory_space=pltpu.SMEM)] + [whole_vmem()] * (1 + len(tables)),
        out_specs=whole_vmem(),
        scratch_shapes=[
            pltpu.VMEM((blocks, W * (own + 1)), jnp.bfloat16),
            pltpu.VMEM((2 * blocks, W * own), jnp.bfloat16),
            pltpu.VMEM((own, blocks, W), jnp.float32),
        ],
        compiler_params=pltpu.CompilerParams(vmem_limit_bytes=32 * 2**20),
        cost_estimate=pl.CostEstimate(flops=steps, bytes_accessed=4 * own * blocks * W, transcendentals=0),
        name="convolve",
    )(skip, got, *tables)


def unpack_kernel(own, got_ref, *rest):
    gate_refs, (out_ref, flat, gate_s) = rest[:-3], rest[-3:]
    sources, rows, _ = got_ref.shape
    some = rows // own
    me = lax.axis_index("ch")
    channels = gate_refs[0].shape[0]
    for d, gate_ref in enumerate(gate_refs):
        first = pl.multiple_of(jnp.bitwise_xor(me, d) * channels, TILE)
        gate_s[pl.ds(first, channels), :] = gate_ref[...]
    for p in range(sources):
        part = got_ref[p].astype(jnp.float32)
        for h in range(W // LANES):
            flat[h, p * rows : (p + 1) * rows, :] = part[:, LANES * h : LANES * (h + 1)]
    for j in range(some):
        for h in range(W // LANES):
            part = flat[h, pl.ds(j, sources * own, stride=some), :]
            first = W * j + LANES * h
            cols = slice(first, first + LANES)
            out_ref[:, cols] = (part * gate_s[:, cols].astype(jnp.float32)).astype(jnp.bfloat16)


def unpack(got, gates, own):
    sources, rows, _ = got.shape
    shape = (sources * own, rows // own * W)
    if rows % TILE:
        order = jnp.bitwise_xor(lax.axis_index("ch"), jnp.arange(len(gates)))
        gate = jnp.stack(gates)[order].reshape(shape)
        return (got.reshape(shape).astype(jnp.float32) * gate.astype(jnp.float32)).astype(jnp.bfloat16)
    return pl.pallas_call(
        functools.partial(unpack_kernel, own),
        out_shape=jax.ShapeDtypeStruct(shape, jnp.bfloat16),
        in_specs=[whole_vmem()] * (1 + len(gates)),
        out_specs=whole_vmem(),
        scratch_shapes=[
            pltpu.VMEM((W // LANES, sources * rows, LANES), jnp.float32),
            pltpu.VMEM(shape, jnp.bfloat16),
        ],
        compiler_params=pltpu.CompilerParams(vmem_limit_bytes=24 * 2**20),
        name="unpack",
    )(got, *gates)


def body(pre_gate, value, post_gate, filter_taps, skip):
    ctx_count = lax.axis_size("ctx")
    ch_count = lax.axis_size("ch")
    own = value.shape[0] // ctx_count
    blocks = value.shape[1] // W * ctx_count
    send = pack_signal(pre_gate, value, filter_taps, ctx_count)
    got = lax.all_to_all(send, "ctx", split_axis=0, concat_axis=0, tiled=True)
    tables = dft_tables(blocks)
    post_gate, tables, _ = lax.optimization_barrier((post_gate, tables, send))
    gates = list(split_gate(post_gate, ch_count))
    for d in range(1, ch_count):
        gates[d] = lax.ppermute(gates[d], "ch", [(i, i ^ d) for i in range(ch_count)])
    tables = list(make_tables(*tables[:3])) + [tables[3]]
    mixed = convolve(got, skip, tables, own, ch_count)
    mixed = lax.all_to_all(mixed, ("ch", "ctx"), split_axis=0, concat_axis=0, tiled=True)
    return unpack(mixed, gates, own)


def solution(mesh):
    placed = (P("ch", "ctx"), P("ch", "ctx"), P("ch", "ctx"), P("ch", "ctx"), P("ch"))
    return jax.shard_map(
        body, mesh=mesh, in_specs=placed, out_specs=P(None, ("ctx", "ch")), check_vma=False
    )
```

```python
import functools

import jax
import jax.numpy as jnp
import numpy as np
from jax import lax
from jax.experimental import pallas as pl
from jax.experimental.pallas import tpu as pltpu
from jax.sharding import PartitionSpec as P

W = 256
LANES = 128
TILE = 16
CHUNK = 64


def whole_vmem():
    return pl.BlockSpec(memory_space=pltpu.VMEM)


def dft_tables(blocks):
    length = blocks * W
    k = np.arange(blocks)[:, None]
    angle = 2 * np.pi * ((4 * k + 1) * np.arange(blocks)[None, :] % (4 * blocks)) / (4 * blocks)
    outer = np.concatenate([np.cos(angle), -np.sin(angle)], 0)
    turn = 2 * np.pi * ((4 * k + 1) * np.arange(W)[None, :]) / (4 * length)
    near = 2 * np.pi * (np.arange(W)[:, None] * np.arange(W)[None, :] % W) / W
    inner = np.concatenate([np.cos(near), np.sin(near)], 0)
    turns = np.concatenate([np.cos(turn), np.sin(turn)], 1)
    return [jnp.asarray(table, jnp.float32) for table in (outer, inner, turns)]


def spread(flat, first, count, stride, value):
    for h in range(W // LANES):
        flat[h, pl.ds(first, count, stride=stride), :] = value[:, LANES * h : LANES * (h + 1)]


def joined(flat, first, count):
    return jnp.concatenate([flat[h, pl.ds(first, count), :] for h in range(W // LANES)], 1)


def pack_signal_kernel(own, blocks, group, pre_ref, val_ref, taps_ref, out_ref, flat, taps_flat):
    step = pl.program_id(0)
    rows = own * blocks
    channels = pre_ref.shape[0]

    @pl.when(step == 0)
    def _():
        for j in range(blocks):
            spread(taps_flat, j, taps_ref.shape[0], blocks, taps_ref[:, W * j : W * (j + 1)])

    for j in range(blocks):
        cols = slice(W * j, W * (j + 1))
        product = pre_ref[:, cols].astype(jnp.float32) * val_ref[:, cols].astype(jnp.float32)
        spread(flat, j, channels, blocks, product)
    for i in range(channels // own):
        out_ref[i, 0:rows, :] = joined(flat, i * rows, rows).astype(jnp.bfloat16)
        which = (step * channels + own * i) // group
        taps = joined(taps_flat, pl.multiple_of(which * blocks, 8), blocks)
        out_ref[i, rows : rows + blocks, :] = taps.astype(jnp.bfloat16)


def pack_signal(pre_gate, value, taps, parts):
    channels, block = value.shape
    own = channels // parts
    group = channels // taps.shape[0]
    blocks = block // W
    some = min(TILE, channels)
    return pl.pallas_call(
        functools.partial(pack_signal_kernel, own, blocks, group),
        grid=(channels // some,),
        out_shape=jax.ShapeDtypeStruct((parts, (own + 1) * blocks, W), jnp.bfloat16),
        in_specs=[pl.BlockSpec((some, block), lambda s: (s, 0))] * 2 + [pl.BlockSpec(taps.shape, lambda s: (0, 0))],
        out_specs=pl.BlockSpec((some // own, (own + 1) * blocks, W), lambda s: (s, 0, 0)),
        scratch_shapes=[
            pltpu.VMEM((W // LANES, some * blocks, LANES), jnp.float32),
            pltpu.VMEM((W // LANES, taps.shape[0] * blocks, LANES), jnp.float32),
        ],
        compiler_params=pltpu.CompilerParams(vmem_limit_bytes=60 * 2**20),
        name="pack_signal",
    )(pre_gate, value, taps)


def split_gate_kernel(gate_ref, *out_refs):
    me = lax.axis_index("ch")
    width = out_refs[0].shape[1]
    for d, out_ref in enumerate(out_refs):
        first = pl.multiple_of(jnp.bitwise_xor(me, d) * width, LANES)
        out_ref[...] = gate_ref[:, pl.ds(first, width)]


def split_gate(post_gate, parts):
    channels, block = post_gate.shape
    return pl.pallas_call(
        split_gate_kernel,
        out_shape=[jax.ShapeDtypeStruct((channels, block // parts), jnp.bfloat16)] * parts,
        in_specs=[whole_vmem()],
        out_specs=[whole_vmem()] * parts,
        compiler_params=pltpu.CompilerParams(vmem_limit_bytes=24 * 2**20),
        name="split_gate",
    )(post_gate)


def tables_kernel(own, skip_ref, outer_ref, inner_ref, turns_ref, outer_out, inner_out, turns_out, weights):
    outer_out[...] = outer_ref[...].astype(jnp.bfloat16)
    inner_out[...] = inner_ref[...].astype(jnp.bfloat16)
    turns_out[...] = turns_ref[...]
    me = lax.axis_index("ctx")
    for c in range(own):
        weights[c] = jnp.full((8, W), skip_ref[own * me + c], jnp.float32)


def make_tables(skip, outer, inner, turns, own):
    return pl.pallas_call(
        functools.partial(tables_kernel, own),
        out_shape=[
            jax.ShapeDtypeStruct(outer.shape, jnp.bfloat16),
            jax.ShapeDtypeStruct(inner.shape, jnp.bfloat16),
            jax.ShapeDtypeStruct(turns.shape, jnp.float32),
            jax.ShapeDtypeStruct((own, 8, W), jnp.float32),
        ],
        in_specs=[pl.BlockSpec(memory_space=pltpu.SMEM)] + [whole_vmem()] * 3,
        out_specs=[whole_vmem()] * 4,
        compiler_params=pltpu.CompilerParams(vmem_limit_bytes=8 * 2**20),
        name="make_tables",
    )(skip, outer, inner, turns)


def conv_kernel(own, got_ref, outer_ref, inner_ref, turns_ref, weights_ref, out_ref, x_all, r_all, z_all, ahead, rear):
    parts, local, _ = got_ref.shape
    near = local // (own + 1)
    blocks = parts * near
    length = blocks * W
    for p in range(parts):
        for c in range(own + 1):
            x_all[p * near : (p + 1) * near, W * c : W * (c + 1)] = got_ref[p, c * near : (c + 1) * near, :]

    near_cos, near_sin = inner_ref[0:W, :], inner_ref[W:, :]
    for table, sign in ((ahead, -1), (rear, 1)):
        table[0:W, 0:W] = near_cos
        table[0:W, W:] = near_sin * sign
        table[W:, 0:W] = near_sin * -sign
        table[W:, W:] = near_cos

    def dot(left, right):
        return jnp.dot(left, right, preferred_element_type=jnp.float32)

    for first in range(0, blocks, CHUNK):
        here = slice(first, first + CHUNK)
        there = slice(blocks + first, blocks + first + CHUNK)
        real = dot(outer_ref[here, :], x_all[...])
        imag = dot(outer_ref[there, :], x_all[...])
        turn_cos, turn_sin = turns_ref[here, 0:W], turns_ref[here, W:]
        rows = []
        for c in range(own + 1):
            re, im = real[:, W * c : W * (c + 1)], imag[:, W * c : W * (c + 1)]
            pair = [re * turn_cos + im * turn_sin, im * turn_cos - re * turn_sin]
            rows.append(jnp.concatenate(pair, 1).astype(jnp.bfloat16))
        spectrum = dot(jnp.concatenate(rows, 0), ahead[...])
        filt_re = spectrum[CHUNK * own :, 0:W] * (1.0 / length)
        filt_im = spectrum[CHUNK * own :, W:] * (1.0 / length)
        rows = []
        for c in range(own):
            part = spectrum[CHUNK * c : CHUNK * (c + 1), :]
            re, im = part[:, 0:W], part[:, W:]
            pair = [re * filt_re - im * filt_im, re * filt_im + im * filt_re]
            rows.append(jnp.concatenate(pair, 1).astype(jnp.bfloat16))
        middle = dot(jnp.concatenate(rows, 0), rear[...])
        for c in range(own):
            part = middle[CHUNK * c : CHUNK * (c + 1), :]
            re, im = part[:, 0:W], part[:, W:]
            cols = slice(W * c, W * (c + 1))
            r_all[here, cols] = (re * turn_cos - im * turn_sin).astype(jnp.bfloat16)
            r_all[there, cols] = (re * turn_sin + im * turn_cos).astype(jnp.bfloat16)

    for c in range(own):
        cols = slice(W * c, W * (c + 1))
        conv = lax.dot_general(
            outer_ref[...], r_all[:, cols], (((0,), (0,)), ((), ())), preferred_element_type=jnp.float32
        )
        z_all[c] = conv + weights_ref[c, 0:1, :] * x_all[:, cols].astype(jnp.float32)
    some = out_ref.shape[1] // own
    ch_count = near // some
    for k in range(parts):
        for m in range(ch_count):
            first = k * near + m * some
            rows = [z_all[c, first : first + some, :] for c in range(own)]
            out_ref[m * parts + k] = jnp.concatenate(rows, 0).astype(jnp.bfloat16)


def convolve(got, tables, own, ch_count):
    parts, local, _ = got.shape
    blocks = parts * (local // (own + 1))
    owners = parts * ch_count
    return pl.pallas_call(
        functools.partial(conv_kernel, own),
        out_shape=jax.ShapeDtypeStruct((owners, own * blocks // owners, W), jnp.bfloat16),
        in_specs=[whole_vmem()] * (1 + len(tables)),
        out_specs=whole_vmem(),
        scratch_shapes=[
            pltpu.VMEM((blocks, W * (own + 1)), jnp.bfloat16),
            pltpu.VMEM((2 * blocks, W * own), jnp.bfloat16),
            pltpu.VMEM((own, blocks, W), jnp.float32),
            pltpu.VMEM((2 * W, 2 * W), jnp.bfloat16),
            pltpu.VMEM((2 * W, 2 * W), jnp.bfloat16),
        ],
        compiler_params=pltpu.CompilerParams(vmem_limit_bytes=32 * 2**20),
        cost_estimate=pl.CostEstimate(flops=blocks * W, bytes_accessed=4 * blocks * W, transcendentals=0),
        name="convolve",
    )(got, *tables)


def unpack_kernel(own, got_ref, *rest):
    gate_refs, (out_ref, flat, gate_s) = rest[:-3], rest[-3:]
    sources, rows, _ = got_ref.shape
    some = rows // own
    me = lax.axis_index("ch")
    channels = gate_refs[0].shape[0]
    for d, gate_ref in enumerate(gate_refs):
        first = pl.multiple_of(jnp.bitwise_xor(me, d) * channels, TILE)
        gate_s[pl.ds(first, channels), :] = gate_ref[...]
    for p in range(sources):
        part = got_ref[p].astype(jnp.float32)
        for h in range(W // LANES):
            flat[h, p * rows : (p + 1) * rows, :] = part[:, LANES * h : LANES * (h + 1)]
    for j in range(some):
        for h in range(W // LANES):
            part = flat[h, pl.ds(j, sources * own, stride=some), :]
            first = W * j + LANES * h
            cols = slice(first, first + LANES)
            out_ref[:, cols] = (part * gate_s[:, cols].astype(jnp.float32)).astype(jnp.bfloat16)


def unpack(got, gates, own):
    sources, rows, _ = got.shape
    shape = (sources * own, rows // own * W)
    if rows % TILE:
        order = jnp.bitwise_xor(lax.axis_index("ch"), jnp.arange(len(gates)))
        gate = jnp.stack(gates)[order].reshape(shape)
        return (got.reshape(shape).astype(jnp.float32) * gate.astype(jnp.float32)).astype(jnp.bfloat16)
    return pl.pallas_call(
        functools.partial(unpack_kernel, own),
        out_shape=jax.ShapeDtypeStruct(shape, jnp.bfloat16),
        in_specs=[whole_vmem()] * (1 + len(gates)),
        out_specs=whole_vmem(),
        scratch_shapes=[
            pltpu.VMEM((W // LANES, sources * rows, LANES), jnp.float32),
            pltpu.VMEM(shape, jnp.bfloat16),
        ],
        compiler_params=pltpu.CompilerParams(vmem_limit_bytes=24 * 2**20),
        name="unpack",
    )(got, *gates)


def body(pre_gate, value, post_gate, filter_taps, skip):
    ctx_count = lax.axis_size("ctx")
    ch_count = lax.axis_size("ch")
    own = value.shape[0] // ctx_count
    blocks = value.shape[1] // W * ctx_count
    send = pack_signal(pre_gate, value, filter_taps, ctx_count)
    got = lax.all_to_all(send, "ctx", split_axis=0, concat_axis=0, tiled=True)
    tables = dft_tables(blocks)
    post_gate, skip, tables, _ = lax.optimization_barrier((post_gate, skip, tables, send))
    gates = list(split_gate(post_gate, ch_count))
    for d in range(1, ch_count):
        gates[d] = lax.ppermute(gates[d], "ch", [(i, i ^ d) for i in range(ch_count)])
    tables = make_tables(skip, *tables, own)
    mixed = convolve(got, tables, own, ch_count)
    mixed, gates = lax.optimization_barrier((mixed, gates))
    mixed = lax.all_to_all(mixed, ("ch", "ctx"), split_axis=0, concat_axis=0, tiled=True)
    return unpack(mixed, gates, own)


def solution(mesh):
    placed = (P("ch", "ctx"), P("ch", "ctx"), P("ch", "ctx"), P("ch", "ctx"), P("ch"))
    return jax.shard_map(
        body, mesh=mesh, in_specs=placed, out_specs=P(None, ("ctx", "ch")), check_vma=False
    )
```

```python
import functools

import jax
import jax.numpy as jnp
import numpy as np
from jax import lax
from jax.experimental import pallas as pl
from jax.experimental.pallas import tpu as pltpu
from jax.sharding import PartitionSpec as P

W = 256
LANES = 128
CUTS = 4
TILE = 16
CHUNK = 128


def whole_vmem():
    return pl.BlockSpec(memory_space=pltpu.VMEM)


def in_hbm():
    return pl.BlockSpec(memory_space=pltpu.HBM)


def dft_tables(blocks):
    length = blocks * W
    k = np.arange(blocks)[:, None]
    angle = 2 * np.pi * ((4 * k + 1) * np.arange(blocks)[None, :] % (4 * blocks)) / (4 * blocks)
    outer = np.concatenate([np.cos(angle), -np.sin(angle)], 0)
    turn = 2 * np.pi * ((4 * k + 1) * np.arange(W)[None, :]) / (4 * length)
    near = 2 * np.pi * (np.arange(W)[:, None] * np.arange(W)[None, :] % W) / W
    inner = np.concatenate([np.cos(near), np.sin(near)], 0)
    turns = np.concatenate([np.cos(turn), np.sin(turn)], 1)
    return [jnp.asarray(table, jnp.float32) for table in (outer, inner, turns)]


def spread(flat, first, count, stride, value):
    for h in range(W // LANES):
        flat[h, pl.ds(first, count, stride=stride), :] = value[:, LANES * h : LANES * (h + 1)]


def joined(flat, first, count):
    return jnp.concatenate([flat[h, pl.ds(first, count), :] for h in range(W // LANES)], 1)


def pack_kernel(own, blocks, group, ch_count, pre_ref, val_ref, taps_ref, post_ref, out_ref, *rest):
    gate_refs = rest[:ch_count]
    pre_s, val_s, taps_s, flat, taps_flat, stage, in_sems, out_sems, gate_sems = rest[ch_count:]
    parts = out_ref.shape[0]
    channels = own * parts
    rows = own * blocks
    width = blocks * W // CUTS
    loads = []
    for q in range(CUTS):
        cols = pl.ds(q * width, width)
        loads.append(pltpu.make_async_copy(pre_ref.at[:, cols], pre_s.at[:, cols], in_sems.at[q, 0]))
        loads.append(pltpu.make_async_copy(val_ref.at[:, cols], val_s.at[:, cols], in_sems.at[q, 1]))
    taps_load = pltpu.make_async_copy(taps_ref, taps_s, in_sems.at[CUTS, 0])
    for copy in loads[:2] + [taps_load] + loads[2:]:
        copy.start()
    me = lax.axis_index("ch")
    piece = blocks * W // ch_count
    gates = []
    for d in range(ch_count):
        cols = pl.ds(pl.multiple_of(jnp.bitwise_xor(me, d) * piece, LANES), piece)
        gates.append(pltpu.make_async_copy(post_ref.at[:, cols], gate_refs[d], gate_sems.at[d]))
        gates[d].start()
    for j in range(blocks):
        if j % (blocks // CUTS) == 0:
            q = j // (blocks // CUTS)
            loads[2 * q].wait()
            loads[2 * q + 1].wait()
        cols = slice(W * j, W * (j + 1))
        product = pre_s[:, cols].astype(jnp.float32) * val_s[:, cols].astype(jnp.float32)
        spread(flat, j, channels, blocks, product)
        if j == 0:
            taps_load.wait()
        spread(taps_flat, j, taps_s.shape[0], blocks, taps_s[:, cols])
    stores = []
    for i in range(parts):
        stage[i, 0:rows, :] = joined(flat, i * rows, rows).astype(jnp.bfloat16)
        taps = joined(taps_flat, own * i // group * blocks, blocks)
        stage[i, rows : rows + blocks, :] = taps.astype(jnp.bfloat16)
        stores.append(pltpu.make_async_copy(stage.at[i], out_ref.at[i], out_sems.at[i]))
        stores[i].start()
    for copy in gates + stores:
        copy.wait()


def pack(pre_gate, value, post_gate, taps, parts, ch_count):
    channels, block = value.shape
    own = channels // parts
    group = channels // taps.shape[0]
    blocks = block // W
    local = (own + 1) * blocks
    return pl.pallas_call(
        functools.partial(pack_kernel, own, blocks, group, ch_count),
        out_shape=[jax.ShapeDtypeStruct((parts, local, W), jnp.bfloat16)]
        + [jax.ShapeDtypeStruct((channels, block // ch_count), jnp.bfloat16)] * ch_count,
        in_specs=[in_hbm()] * 4,
        out_specs=[in_hbm()] * (1 + ch_count),
        scratch_shapes=[
            pltpu.VMEM(pre_gate.shape, jnp.bfloat16),
            pltpu.VMEM(value.shape, jnp.bfloat16),
            pltpu.VMEM(taps.shape, jnp.float32),
            pltpu.VMEM((W // LANES, channels * blocks, LANES), jnp.float32),
            pltpu.VMEM((W // LANES, taps.shape[0] * blocks, LANES), jnp.float32),
            pltpu.VMEM((parts, local, W), jnp.bfloat16),
            pltpu.SemaphoreType.DMA((CUTS + 1, 2)),
            pltpu.SemaphoreType.DMA((parts,)),
            pltpu.SemaphoreType.DMA((ch_count,)),
        ],
        compiler_params=pltpu.CompilerParams(vmem_limit_bytes=60 * 2**20),
        name="pack",
    )(pre_gate, value, taps, post_gate)


def tables_kernel(own, skip_ref, outer_ref, inner_ref, turns_ref, outer_out, inner_out, turns_out, weights):
    outer_out[...] = outer_ref[...].astype(jnp.bfloat16)
    inner_out[...] = inner_ref[...].astype(jnp.bfloat16)
    turns_out[...] = turns_ref[...]
    me = lax.axis_index("ctx")
    for c in range(own):
        weights[c] = jnp.full((8, W), skip_ref[own * me + c], jnp.float32)


def make_tables(skip, outer, inner, turns, own):
    return pl.pallas_call(
        functools.partial(tables_kernel, own),
        out_shape=[
            jax.ShapeDtypeStruct(outer.shape, jnp.bfloat16),
            jax.ShapeDtypeStruct(inner.shape, jnp.bfloat16),
            jax.ShapeDtypeStruct(turns.shape, jnp.float32),
            jax.ShapeDtypeStruct((own, 8, W), jnp.float32),
        ],
        in_specs=[pl.BlockSpec(memory_space=pltpu.SMEM)] + [whole_vmem()] * 3,
        out_specs=[whole_vmem()] * 4,
        compiler_params=pltpu.CompilerParams(vmem_limit_bytes=8 * 2**20),
        name="make_tables",
    )(skip, outer, inner, turns)


def conv_kernel(own, got_ref, outer_ref, inner_ref, turns_ref, weights_ref, out_ref, x_all, r_all, z_all, ahead, rear):
    parts, local, _ = got_ref.shape
    near = local // (own + 1)
    blocks = parts * near
    length = blocks * W
    for p in range(parts):
        for c in range(own + 1):
            x_all[p * near : (p + 1) * near, W * c : W * (c + 1)] = got_ref[p, c * near : (c + 1) * near, :]

    near_cos, near_sin = inner_ref[0:W, :], inner_ref[W:, :]
    for table, sign in ((ahead, -1), (rear, 1)):
        table[0:W, 0:W] = near_cos
        table[0:W, W:] = near_sin * sign
        table[W:, 0:W] = near_sin * -sign
        table[W:, W:] = near_cos

    def dot(left, right):
        return jnp.dot(left, right, preferred_element_type=jnp.float32)

    for first in range(0, blocks, CHUNK):
        here = slice(first, first + CHUNK)
        there = slice(blocks + first, blocks + first + CHUNK)
        both = dot(jnp.concatenate([outer_ref[here, :], outer_ref[there, :]], 0), x_all[...])
        real, imag = both[0:CHUNK, :], both[CHUNK:, :]
        turn_cos, turn_sin = turns_ref[here, 0:W], turns_ref[here, W:]
        rows = []
        for c in range(own + 1):
            re, im = real[:, W * c : W * (c + 1)], imag[:, W * c : W * (c + 1)]
            pair = [re * turn_cos + im * turn_sin, im * turn_cos - re * turn_sin]
            rows.append(jnp.concatenate(pair, 1).astype(jnp.bfloat16))
        spectrum = dot(jnp.concatenate(rows, 0), ahead[...])
        filt_re = spectrum[CHUNK * own :, 0:W] * (1.0 / length)
        filt_im = spectrum[CHUNK * own :, W:] * (1.0 / length)
        rows = []
        for c in range(own):
            part = spectrum[CHUNK * c : CHUNK * (c + 1), :]
            re, im = part[:, 0:W], part[:, W:]
            pair = [re * filt_re - im * filt_im, re * filt_im + im * filt_re]
            rows.append(jnp.concatenate(pair, 1).astype(jnp.bfloat16))
        middle = dot(jnp.concatenate(rows, 0), rear[...])
        for c in range(own):
            part = middle[CHUNK * c : CHUNK * (c + 1), :]
            re, im = part[:, 0:W], part[:, W:]
            cols = slice(W * c, W * (c + 1))
            r_all[here, cols] = (re * turn_cos - im * turn_sin).astype(jnp.bfloat16)
            r_all[there, cols] = (re * turn_sin + im * turn_cos).astype(jnp.bfloat16)

    conv = lax.dot_general(
        outer_ref[...], r_all[...], (((0,), (0,)), ((), ())), preferred_element_type=jnp.float32
    )
    for c in range(own):
        cols = slice(W * c, W * (c + 1))
        z_all[c] = conv[:, cols] + weights_ref[c, 0:1, :] * x_all[:, cols].astype(jnp.float32)
    some = out_ref.shape[1] // own
    ch_count = near // some
    for k in range(parts):
        for m in range(ch_count):
            first = k * near + m * some
            rows = [z_all[c, first : first + some, :] for c in range(own)]
            out_ref[m * parts + k] = jnp.concatenate(rows, 0).astype(jnp.bfloat16)


def convolve(got, tables, own, ch_count):
    parts, local, _ = got.shape
    blocks = parts * (local // (own + 1))
    owners = parts * ch_count
    return pl.pallas_call(
        functools.partial(conv_kernel, own),
        out_shape=jax.ShapeDtypeStruct((owners, own * blocks // owners, W), jnp.bfloat16),
        in_specs=[whole_vmem()] * (1 + len(tables)),
        out_specs=whole_vmem(),
        scratch_shapes=[
            pltpu.VMEM((blocks, W * (own + 1)), jnp.bfloat16),
            pltpu.VMEM((2 * blocks, W * own), jnp.bfloat16),
            pltpu.VMEM((own, blocks, W), jnp.float32),
            pltpu.VMEM((2 * W, 2 * W), jnp.bfloat16),
            pltpu.VMEM((2 * W, 2 * W), jnp.bfloat16),
        ],
        compiler_params=pltpu.CompilerParams(vmem_limit_bytes=32 * 2**20),
        cost_estimate=pl.CostEstimate(flops=blocks * W, bytes_accessed=4 * blocks * W, transcendentals=0),
        name="convolve",
    )(got, *tables)


def unpack_kernel(own, got_ref, *rest):
    gate_refs, (out_ref, flat, gate_s, stage, sems) = rest[:-5], rest[-5:]
    sources, rows, _ = got_ref.shape
    some = rows // own
    me = lax.axis_index("ch")
    channels = gate_refs[0].shape[0]
    for d, gate_ref in enumerate(gate_refs):
        first = pl.multiple_of(jnp.bitwise_xor(me, d) * channels, TILE)
        gate_s[pl.ds(first, channels), :] = gate_ref[...]
    for p in range(sources):
        part = got_ref[p].astype(jnp.float32)
        for h in range(W // LANES):
            flat[h, p * rows : (p + 1) * rows, :] = part[:, LANES * h : LANES * (h + 1)]
    for j in range(some):
        for h in range(W // LANES):
            part = flat[h, pl.ds(j, sources * own, stride=some), :]
            first = W * j + LANES * h
            cols = slice(first, first + LANES)
            stage[:, cols] = (part * gate_s[:, cols].astype(jnp.float32)).astype(jnp.bfloat16)
        cols = pl.ds(W * j, W)
        pltpu.make_async_copy(stage.at[:, cols], out_ref.at[:, cols], sems.at[j]).start()
    for j in range(some):
        cols = pl.ds(W * j, W)
        pltpu.make_async_copy(stage.at[:, cols], out_ref.at[:, cols], sems.at[j]).wait()


def unpack(got, gates, own):
    sources, rows, _ = got.shape
    shape = (sources * own, rows // own * W)
    if rows % TILE:
        order = jnp.bitwise_xor(lax.axis_index("ch"), jnp.arange(len(gates)))
        gate = jnp.stack(gates)[order].reshape(shape)
        return (got.reshape(shape).astype(jnp.float32) * gate.astype(jnp.float32)).astype(jnp.bfloat16)
    return pl.pallas_call(
        functools.partial(unpack_kernel, own),
        out_shape=jax.ShapeDtypeStruct(shape, jnp.bfloat16),
        in_specs=[whole_vmem()] * (1 + len(gates)),
        out_specs=in_hbm(),
        scratch_shapes=[
            pltpu.VMEM((W // LANES, sources * rows, LANES), jnp.float32),
            pltpu.VMEM(shape, jnp.bfloat16),
            pltpu.VMEM(shape, jnp.bfloat16),
            pltpu.SemaphoreType.DMA((rows // own,)),
        ],
        compiler_params=pltpu.CompilerParams(vmem_limit_bytes=24 * 2**20),
        name="unpack",
    )(got, *gates)


def body(pre_gate, value, post_gate, filter_taps, skip):
    ctx_count = lax.axis_size("ctx")
    ch_count = lax.axis_size("ch")
    own = value.shape[0] // ctx_count
    blocks = value.shape[1] // W * ctx_count
    send, *gates = pack(pre_gate, value, post_gate, filter_taps, ctx_count, ch_count)
    got = lax.all_to_all(send, "ctx", split_axis=0, concat_axis=0, tiled=True)
    for d in range(1, ch_count):
        gates[d] = lax.ppermute(gates[d], "ch", [(i, i ^ d) for i in range(ch_count)])
    tables, skip, _ = lax.optimization_barrier((dft_tables(blocks), skip, send))
    tables = make_tables(skip, *tables, own)
    mixed = convolve(got, tables, own, ch_count)
    mixed, gates = lax.optimization_barrier((mixed, gates))
    mixed = lax.all_to_all(mixed, ("ch", "ctx"), split_axis=0, concat_axis=0, tiled=True)
    return unpack(mixed, gates, own)


def solution(mesh):
    placed = (P("ch", "ctx"), P("ch", "ctx"), P("ch", "ctx"), P("ch", "ctx"), P("ch"))
    return jax.shard_map(
        body, mesh=mesh, in_specs=placed, out_specs=P(None, ("ctx", "ch")), check_vma=False
    )
```

```python
import functools

import jax
import jax.numpy as jnp
import numpy as np
from jax import lax
from jax.experimental import pallas as pl
from jax.experimental.pallas import tpu as pltpu
from jax.sharding import PartitionSpec as P

W = 256
LANES = 128
CUTS = 4
TILE = 16
CHUNK = 128


def whole_vmem():
    return pl.BlockSpec(memory_space=pltpu.VMEM)


def in_hbm():
    return pl.BlockSpec(memory_space=pltpu.HBM)


def dft_tables(blocks):
    length = blocks * W
    k = np.arange(blocks)[:, None]
    angle = 2 * np.pi * ((4 * k + 1) * np.arange(blocks)[None, :] % (4 * blocks)) / (4 * blocks)
    outer = np.concatenate([np.cos(angle), -np.sin(angle)], 0)
    turn = 2 * np.pi * ((4 * k + 1) * np.arange(W)[None, :]) / (4 * length)
    near = 2 * np.pi * (np.arange(W)[:, None] * np.arange(W)[None, :] % W) / W
    inner = np.concatenate([np.cos(near), np.sin(near)], 0)
    turns = np.concatenate([np.cos(turn), np.sin(turn)], 1)
    return [jnp.asarray(table, jnp.float32) for table in (outer, inner, turns)]


def spread(flat, first, count, stride, value):
    for h in range(W // LANES):
        flat[h, pl.ds(first, count, stride=stride), :] = value[:, LANES * h : LANES * (h + 1)]


def joined(flat, first, count):
    return jnp.concatenate([flat[h, pl.ds(first, count), :] for h in range(W // LANES)], 1)


def pack_kernel(own, blocks, group, ch_count, pre_ref, val_ref, taps_ref, post_ref, out_ref, *rest):
    gate_refs = rest[:ch_count]
    pre_s, val_s, taps_s, flat, taps_flat, in_sems, gate_sems = rest[ch_count:]
    parts = out_ref.shape[0]
    channels = own * parts
    rows = own * blocks
    width = blocks * W // CUTS
    loads = []
    for q in range(CUTS):
        cols = pl.ds(q * width, width)
        loads.append(pltpu.make_async_copy(pre_ref.at[:, cols], pre_s.at[:, cols], in_sems.at[q, 0]))
        loads.append(pltpu.make_async_copy(val_ref.at[:, cols], val_s.at[:, cols], in_sems.at[q, 1]))
    taps_load = pltpu.make_async_copy(taps_ref, taps_s, in_sems.at[CUTS, 0])
    for copy in loads[:2] + [taps_load] + loads[2:]:
        copy.start()
    me = lax.axis_index("ch")
    piece = blocks * W // ch_count
    gates = []
    for d in range(ch_count):
        cols = pl.ds(pl.multiple_of(jnp.bitwise_xor(me, d) * piece, LANES), piece)
        gates.append(pltpu.make_async_copy(post_ref.at[:, cols], gate_refs[d], gate_sems.at[d]))
        gates[d].start()
    for j in range(blocks):
        if j % (blocks // CUTS) == 0:
            q = j // (blocks // CUTS)
            loads[2 * q].wait()
            loads[2 * q + 1].wait()
        cols = slice(W * j, W * (j + 1))
        product = pre_s[:, cols].astype(jnp.float32) * val_s[:, cols].astype(jnp.float32)
        spread(flat, j, channels, blocks, product)
        if j == 0:
            taps_load.wait()
        spread(taps_flat, j, taps_s.shape[0], blocks, taps_s[:, cols])
    for i in range(parts):
        out_ref[i, 0:rows, :] = joined(flat, i * rows, rows).astype(jnp.bfloat16)
        taps = joined(taps_flat, own * i // group * blocks, blocks)
        out_ref[i, rows : rows + blocks, :] = taps.astype(jnp.bfloat16)
    for copy in gates:
        copy.wait()


def pack(pre_gate, value, post_gate, taps, parts, ch_count):
    channels, block = value.shape
    own = channels // parts
    group = channels // taps.shape[0]
    blocks = block // W
    local = (own + 1) * blocks
    args = [pltpu.with_memory_space_constraint(arg, pltpu.HBM) for arg in (pre_gate, value, taps, post_gate)]
    return pl.pallas_call(
        functools.partial(pack_kernel, own, blocks, group, ch_count),
        out_shape=[pltpu.VMEM((parts, local, W), jnp.bfloat16)]
        + [pltpu.VMEM((channels, block // ch_count), jnp.bfloat16)] * ch_count,
        in_specs=[in_hbm()] * 4,
        out_specs=[whole_vmem()] * (1 + ch_count),
        scratch_shapes=[
            pltpu.VMEM(pre_gate.shape, jnp.bfloat16),
            pltpu.VMEM(value.shape, jnp.bfloat16),
            pltpu.VMEM(taps.shape, jnp.float32),
            pltpu.VMEM((W // LANES, channels * blocks, LANES), jnp.float32),
            pltpu.VMEM((W // LANES, taps.shape[0] * blocks, LANES), jnp.float32),
            pltpu.SemaphoreType.DMA((CUTS + 1, 2)),
            pltpu.SemaphoreType.DMA((ch_count,)),
        ],
        compiler_params=pltpu.CompilerParams(vmem_limit_bytes=16 * 2**20),
        name="pack",
    )(*args)


def tables_kernel(own, skip_ref, outer_ref, inner_ref, turns_ref, outer_out, inner_out, turns_out):
    outer_out[...] = outer_ref[...].astype(jnp.bfloat16)
    inner_out[...] = inner_ref[...].astype(jnp.bfloat16)
    count, width = turns_ref.shape
    turns_out[0:count, :] = turns_ref[...]
    me = lax.axis_index("ctx")
    for c in range(own):
        turns_out[count + 8 * c : count + 8 * (c + 1), :] = jnp.full((8, width), skip_ref[own * me + c], jnp.float32)


def make_tables(skip, outer, inner, turns, own):
    count, width = turns.shape
    return pl.pallas_call(
        functools.partial(tables_kernel, own),
        out_shape=[
            jax.ShapeDtypeStruct(outer.shape, jnp.bfloat16),
            jax.ShapeDtypeStruct(inner.shape, jnp.bfloat16),
            jax.ShapeDtypeStruct((count + 8 * own, width), jnp.float32),
        ],
        in_specs=[pl.BlockSpec(memory_space=pltpu.SMEM)] + [whole_vmem()] * 3,
        out_specs=[whole_vmem()] * 3,
        compiler_params=pltpu.CompilerParams(vmem_limit_bytes=8 * 2**20),
        name="make_tables",
    )(skip, outer, inner, turns)


def conv_kernel(own, got_ref, outer_ref, inner_ref, turns_ref, out_ref, x_all, r_all, z_all, ahead, rear):
    parts, local, _ = got_ref.shape
    near = local // (own + 1)
    blocks = parts * near
    length = blocks * W
    for p in range(parts):
        for c in range(own + 1):
            x_all[p * near : (p + 1) * near, W * c : W * (c + 1)] = got_ref[p, c * near : (c + 1) * near, :]

    near_cos, near_sin = inner_ref[0:W, :], inner_ref[W:, :]
    for table, sign in ((ahead, -1), (rear, 1)):
        table[0:W, 0:W] = near_cos
        table[0:W, W:] = near_sin * sign
        table[W:, 0:W] = near_sin * -sign
        table[W:, W:] = near_cos

    def dot(left, right):
        return jnp.dot(left, right, preferred_element_type=jnp.float32)

    for first in range(0, blocks, CHUNK):
        here = slice(first, first + CHUNK)
        there = slice(blocks + first, blocks + first + CHUNK)
        both = dot(jnp.concatenate([outer_ref[here, :], outer_ref[there, :]], 0), x_all[...])
        real, imag = both[0:CHUNK, :], both[CHUNK:, :]
        turn_cos, turn_sin = turns_ref[here, 0:W], turns_ref[here, W:]
        rows = []
        for c in range(own + 1):
            re, im = real[:, W * c : W * (c + 1)], imag[:, W * c : W * (c + 1)]
            pair = [re * turn_cos + im * turn_sin, im * turn_cos - re * turn_sin]
            rows.append(jnp.concatenate(pair, 1).astype(jnp.bfloat16))
        spectrum = dot(jnp.concatenate(rows, 0), ahead[...])
        filt_re = spectrum[CHUNK * own :, 0:W] * (1.0 / length)
        filt_im = spectrum[CHUNK * own :, W:] * (1.0 / length)
        rows = []
        for c in range(own):
            part = spectrum[CHUNK * c : CHUNK * (c + 1), :]
            re, im = part[:, 0:W], part[:, W:]
            pair = [re * filt_re - im * filt_im, re * filt_im + im * filt_re]
            rows.append(jnp.concatenate(pair, 1).astype(jnp.bfloat16))
        middle = dot(jnp.concatenate(rows, 0), rear[...])
        for c in range(own):
            part = middle[CHUNK * c : CHUNK * (c + 1), :]
            re, im = part[:, 0:W], part[:, W:]
            cols = slice(W * c, W * (c + 1))
            r_all[here, cols] = (re * turn_cos - im * turn_sin).astype(jnp.bfloat16)
            r_all[there, cols] = (re * turn_sin + im * turn_cos).astype(jnp.bfloat16)

    conv = lax.dot_general(
        outer_ref[...], r_all[...], (((0,), (0,)), ((), ())), preferred_element_type=jnp.float32
    )
    for c in range(own):
        cols = slice(W * c, W * (c + 1))
        z_all[c] = conv[:, cols] + turns_ref[blocks + 8 * c : blocks + 8 * c + 1, 0:W] * x_all[:, cols].astype(jnp.float32)
    some = out_ref.shape[1] // own
    ch_count = near // some
    for k in range(parts):
        for m in range(ch_count):
            first = k * near + m * some
            rows = [z_all[c, first : first + some, :] for c in range(own)]
            out_ref[m * parts + k] = jnp.concatenate(rows, 0).astype(jnp.bfloat16)


def convolve(got, tables, own, ch_count):
    parts, local, _ = got.shape
    blocks = parts * (local // (own + 1))
    owners = parts * ch_count
    return pl.pallas_call(
        functools.partial(conv_kernel, own),
        out_shape=jax.ShapeDtypeStruct((owners, own * blocks // owners, W), jnp.bfloat16),
        in_specs=[whole_vmem()] * (1 + len(tables)),
        out_specs=whole_vmem(),
        scratch_shapes=[
            pltpu.VMEM((blocks, W * (own + 1)), jnp.bfloat16),
            pltpu.VMEM((2 * blocks, W * own), jnp.bfloat16),
            pltpu.VMEM((own, blocks, W), jnp.float32),
            pltpu.VMEM((2 * W, 2 * W), jnp.bfloat16),
            pltpu.VMEM((2 * W, 2 * W), jnp.bfloat16),
        ],
        compiler_params=pltpu.CompilerParams(vmem_limit_bytes=32 * 2**20),
        cost_estimate=pl.CostEstimate(flops=blocks * W, bytes_accessed=4 * blocks * W, transcendentals=0),
        name="convolve",
    )(got, *tables)


def unpack_kernel(own, got_ref, *rest):
    gate_refs, (out_ref, flat, gate_s) = rest[:-3], rest[-3:]
    sources, rows, _ = got_ref.shape
    some = rows // own
    me = lax.axis_index("ch")
    channels = gate_refs[0].shape[0]
    for d, gate_ref in enumerate(gate_refs):
        first = pl.multiple_of(jnp.bitwise_xor(me, d) * channels, TILE)
        gate_s[pl.ds(first, channels), :] = gate_ref[...]
    for p in range(sources):
        part = got_ref[p].astype(jnp.float32)
        for h in range(W // LANES):
            flat[h, p * rows : (p + 1) * rows, :] = part[:, LANES * h : LANES * (h + 1)]
    for j in range(some):
        for h in range(W // LANES):
            part = flat[h, pl.ds(j, sources * own, stride=some), :]
            first = W * j + LANES * h
            cols = slice(first, first + LANES)
            out_ref[:, cols] = (part * gate_s[:, cols].astype(jnp.float32)).astype(jnp.bfloat16)


def unpack(got, gates, own):
    sources, rows, _ = got.shape
    shape = (sources * own, rows // own * W)
    if rows % TILE:
        order = jnp.bitwise_xor(lax.axis_index("ch"), jnp.arange(len(gates)))
        gate = jnp.stack(gates)[order].reshape(shape)
        return (got.reshape(shape).astype(jnp.float32) * gate.astype(jnp.float32)).astype(jnp.bfloat16)
    return pl.pallas_call(
        functools.partial(unpack_kernel, own),
        out_shape=jax.ShapeDtypeStruct(shape, jnp.bfloat16),
        in_specs=[whole_vmem()] * (1 + len(gates)),
        out_specs=whole_vmem(),
        scratch_shapes=[
            pltpu.VMEM((W // LANES, sources * rows, LANES), jnp.float32),
            pltpu.VMEM(shape, jnp.bfloat16),
        ],
        compiler_params=pltpu.CompilerParams(vmem_limit_bytes=24 * 2**20),
        name="unpack",
    )(got, *gates)


def body(pre_gate, value, post_gate, filter_taps, skip):
    ctx_count = lax.axis_size("ctx")
    ch_count = lax.axis_size("ch")
    own = value.shape[0] // ctx_count
    blocks = value.shape[1] // W * ctx_count
    send, *gates = pack(pre_gate, value, post_gate, filter_taps, ctx_count, ch_count)
    got = lax.all_to_all(send, "ctx", split_axis=0, concat_axis=0, tiled=True)
    for d in range(1, ch_count):
        gates[d] = lax.ppermute(gates[d], "ch", [(i, i ^ d) for i in range(ch_count)])
    tables, skip, _ = lax.optimization_barrier((dft_tables(blocks), skip, send))
    tables = make_tables(skip, *tables, own)
    mixed = convolve(got, tables, own, ch_count)
    mixed, gates = lax.optimization_barrier((mixed, gates))
    mixed = lax.all_to_all(mixed, ("ch", "ctx"), split_axis=0, concat_axis=0, tiled=True)
    return unpack(mixed, gates, own)


def solution(mesh):
    placed = (P("ch", "ctx"), P("ch", "ctx"), P("ch", "ctx"), P("ch", "ctx"), P("ch"))
    return jax.shard_map(
        body, mesh=mesh, in_specs=placed, out_specs=P(None, ("ctx", "ch")), check_vma=False
    )
```

```python
import functools

import jax
import jax.numpy as jnp
import numpy as np
from jax import lax
from jax.experimental import pallas as pl
from jax.experimental.pallas import tpu as pltpu
from jax.sharding import PartitionSpec as P

W = 256
LANES = 128
CUTS = 4
TILE = 16
CHUNK = 128


def whole_vmem():
    return pl.BlockSpec(memory_space=pltpu.VMEM)


def in_hbm():
    return pl.BlockSpec(memory_space=pltpu.HBM)


def dft_tables(blocks):
    length = blocks * W
    k = np.arange(blocks)[:, None]
    angle = 2 * np.pi * ((4 * k + 1) * np.arange(blocks)[None, :] % (4 * blocks)) / (4 * blocks)
    outer = np.concatenate([np.cos(angle), -np.sin(angle)], 0)
    turn = 2 * np.pi * ((4 * k + 1) * np.arange(W)[None, :]) / (4 * length)
    near = 2 * np.pi * (np.arange(W)[:, None] * np.arange(W)[None, :] % W) / W
    inner = np.concatenate([np.cos(near), np.sin(near)], 0)
    turns = np.concatenate([np.cos(turn), np.sin(turn)], 1)
    return [jnp.asarray(table, jnp.float32) for table in (outer, inner, turns)]


def lay(natural, j, value):
    count = value.shape[0]
    for h in range(W // LANES):
        first = (j * (W // LANES) + h) * count
        natural[first : first + count, :] = value[:, LANES * h : LANES * (h + 1)]


def pick(natural, channel, count, blocks):
    halves = W // LANES
    rows = [natural[pl.ds(h * count + channel, blocks, stride=halves * count), :] for h in range(halves)]
    return jnp.concatenate(rows, 1).astype(jnp.bfloat16)


def pack_kernel(own, blocks, group, ch_count, pre_ref, val_ref, taps_ref, post_ref, out_ref, *rest):
    gate_refs = rest[:ch_count]
    pre_s, val_s, taps_s, post_s, natural, natural_taps, stage, in_sems, out_sems, gate_sems = rest[ch_count:]
    parts = out_ref.shape[0]
    channels = own * parts
    rows = own * blocks
    width = blocks * W // CUTS
    loads = []
    for q in range(CUTS):
        cols = pl.ds(q * width, width)
        loads.append(pltpu.make_async_copy(pre_ref.at[:, cols], pre_s.at[:, cols], in_sems.at[q, 0]))
        loads.append(pltpu.make_async_copy(val_ref.at[:, cols], val_s.at[:, cols], in_sems.at[q, 1]))
    taps_load = pltpu.make_async_copy(taps_ref, taps_s, in_sems.at[CUTS, 0])
    gate_load = pltpu.make_async_copy(post_ref, post_s, in_sems.at[CUTS, 1])
    for copy in loads[:2] + [taps_load] + loads[2:] + [gate_load]:
        copy.start()
    groups = taps_s.shape[0]
    for j in range(blocks):
        if j % (blocks // CUTS) == 0:
            q = j // (blocks // CUTS)
            loads[2 * q].wait()
            loads[2 * q + 1].wait()
        cols = slice(W * j, W * (j + 1))
        lay(natural, j, pre_s[:, cols].astype(jnp.float32) * val_s[:, cols].astype(jnp.float32))
        if j == 0:
            taps_load.wait()
        lay(natural_taps, j, taps_s[:, cols])
    gate_load.wait()
    me = lax.axis_index("ch")
    piece = blocks * W // ch_count
    stores = []
    for d in range(ch_count):
        cols = pl.ds(pl.multiple_of(jnp.bitwise_xor(me, d) * piece, LANES), piece)
        stores.append(pltpu.make_async_copy(post_s.at[:, cols], gate_refs[d], gate_sems.at[d]))
        stores[-1].start()
    for i in range(parts):
        for c in range(own):
            stage[i, blocks * c : blocks * (c + 1), :] = pick(natural, own * i + c, channels, blocks)
        stage[i, rows : rows + blocks, :] = pick(natural_taps, own * i // group, groups, blocks)
        stores.append(pltpu.make_async_copy(stage.at[i], out_ref.at[i], out_sems.at[i]))
        stores[-1].start()
    for copy in stores:
        copy.wait()


def pack(pre_gate, value, post_gate, taps, parts, ch_count):
    channels, block = value.shape
    own = channels // parts
    group = channels // taps.shape[0]
    blocks = block // W
    local = (own + 1) * blocks
    halves = W // LANES
    args = [pltpu.with_memory_space_constraint(arg, pltpu.HBM) for arg in (pre_gate, value, taps, post_gate)]
    return pl.pallas_call(
        functools.partial(pack_kernel, own, blocks, group, ch_count),
        out_shape=[jax.ShapeDtypeStruct((parts, local, W), jnp.bfloat16)]
        + [jax.ShapeDtypeStruct((channels, block // ch_count), jnp.bfloat16)] * ch_count,
        in_specs=[in_hbm()] * 4,
        out_specs=[in_hbm()] * (1 + ch_count),
        scratch_shapes=[
            pltpu.VMEM(pre_gate.shape, jnp.bfloat16),
            pltpu.VMEM(value.shape, jnp.bfloat16),
            pltpu.VMEM(taps.shape, jnp.float32),
            pltpu.VMEM(post_gate.shape, jnp.bfloat16),
            pltpu.VMEM((blocks * halves * channels, LANES), jnp.float32),
            pltpu.VMEM((blocks * halves * taps.shape[0], LANES), jnp.float32),
            pltpu.VMEM((parts, local, W), jnp.bfloat16),
            pltpu.SemaphoreType.DMA((CUTS + 1, 2)),
            pltpu.SemaphoreType.DMA((parts,)),
            pltpu.SemaphoreType.DMA((ch_count,)),
        ],
        compiler_params=pltpu.CompilerParams(vmem_limit_bytes=16 * 2**20),
        name="pack",
    )(*args)


def tables_kernel(own, skip_ref, outer_ref, inner_ref, turns_ref, outer_out, inner_out, turns_out, outer_s, inner_s, sems):
    count, width = turns_ref.shape
    loads = [
        pltpu.make_async_copy(outer_ref, outer_s, sems.at[0]),
        pltpu.make_async_copy(inner_ref, inner_s, sems.at[1]),
        pltpu.make_async_copy(turns_ref, turns_out.at[0:count, :], sems.at[2]),
    ]
    for copy in loads:
        copy.start()
    me = lax.axis_index("ctx")
    for c in range(own):
        turns_out[count + 8 * c : count + 8 * (c + 1), :] = jnp.full((8, width), skip_ref[own * me + c], jnp.float32)
    loads[0].wait()
    outer_out[...] = outer_s[...].astype(jnp.bfloat16)
    loads[1].wait()
    inner_out[...] = inner_s[...].astype(jnp.bfloat16)
    loads[2].wait()


def make_tables(skip, outer, inner, turns, own):
    count, width = turns.shape
    args = [pltpu.with_memory_space_constraint(arg, pltpu.HBM) for arg in (outer, inner, turns)]
    return pl.pallas_call(
        functools.partial(tables_kernel, own),
        out_shape=[
            jax.ShapeDtypeStruct(outer.shape, jnp.bfloat16),
            jax.ShapeDtypeStruct(inner.shape, jnp.bfloat16),
            jax.ShapeDtypeStruct((count + 8 * own, width), jnp.float32),
        ],
        in_specs=[pl.BlockSpec(memory_space=pltpu.SMEM)] + [in_hbm()] * 3,
        out_specs=[whole_vmem()] * 3,
        scratch_shapes=[
            pltpu.VMEM(outer.shape, jnp.float32),
            pltpu.VMEM(inner.shape, jnp.float32),
            pltpu.SemaphoreType.DMA((3,)),
        ],
        compiler_params=pltpu.CompilerParams(vmem_limit_bytes=12 * 2**20),
        name="make_tables",
    )(skip, *args)


def conv_kernel(own, got_ref, outer_ref, inner_ref, turns_ref, out_ref, x_all, r_all, z_all, ahead, rear):
    parts, local, _ = got_ref.shape
    near = local // (own + 1)
    blocks = parts * near
    length = blocks * W
    for p in range(parts):
        for c in range(own + 1):
            x_all[p * near : (p + 1) * near, W * c : W * (c + 1)] = got_ref[p, c * near : (c + 1) * near, :]

    near_cos, near_sin = inner_ref[0:W, :], inner_ref[W:, :]
    for table, sign in ((ahead, -1), (rear, 1)):
        table[0:W, 0:W] = near_cos
        table[0:W, W:] = near_sin * sign
        table[W:, 0:W] = near_sin * -sign
        table[W:, W:] = near_cos

    def dot(left, right):
        return jnp.dot(left, right, preferred_element_type=jnp.float32)

    for first in range(0, blocks, CHUNK):
        here = slice(first, first + CHUNK)
        there = slice(blocks + first, blocks + first + CHUNK)
        both = dot(jnp.concatenate([outer_ref[here, :], outer_ref[there, :]], 0), x_all[...])
        real, imag = both[0:CHUNK, :], both[CHUNK:, :]
        turn_cos, turn_sin = turns_ref[here, 0:W], turns_ref[here, W:]
        rows = []
        for c in range(own + 1):
            re, im = real[:, W * c : W * (c + 1)], imag[:, W * c : W * (c + 1)]
            pair = [re * turn_cos + im * turn_sin, im * turn_cos - re * turn_sin]
            rows.append(jnp.concatenate(pair, 1).astype(jnp.bfloat16))
        spectrum = dot(jnp.concatenate(rows, 0), ahead[...])
        filt_re = spectrum[CHUNK * own :, 0:W] * (1.0 / length)
        filt_im = spectrum[CHUNK * own :, W:] * (1.0 / length)
        rows = []
        for c in range(own):
            part = spectrum[CHUNK * c : CHUNK * (c + 1), :]
            re, im = part[:, 0:W], part[:, W:]
            pair = [re * filt_re - im * filt_im, re * filt_im + im * filt_re]
            rows.append(jnp.concatenate(pair, 1).astype(jnp.bfloat16))
        middle = dot(jnp.concatenate(rows, 0), rear[...])
        for c in range(own):
            part = middle[CHUNK * c : CHUNK * (c + 1), :]
            re, im = part[:, 0:W], part[:, W:]
            cols = slice(W * c, W * (c + 1))
            r_all[here, cols] = (re * turn_cos - im * turn_sin).astype(jnp.bfloat16)
            r_all[there, cols] = (re * turn_sin + im * turn_cos).astype(jnp.bfloat16)

    conv = lax.dot_general(
        outer_ref[...], r_all[...], (((0,), (0,)), ((), ())), preferred_element_type=jnp.float32
    )
    for c in range(own):
        cols = slice(W * c, W * (c + 1))
        z_all[c] = conv[:, cols] + turns_ref[blocks + 8 * c : blocks + 8 * c + 1, 0:W] * x_all[:, cols].astype(jnp.float32)
    some = out_ref.shape[1] // own
    ch_count = near // some
    for k in range(parts):
        for m in range(ch_count):
            first = k * near + m * some
            rows = [z_all[c, first : first + some, :] for c in range(own)]
            out_ref[k * ch_count + m] = jnp.concatenate(rows, 0).astype(jnp.bfloat16)


def convolve(got, tables, own, ch_count):
    parts, local, _ = got.shape
    blocks = parts * (local // (own + 1))
    owners = parts * ch_count
    return pl.pallas_call(
        functools.partial(conv_kernel, own),
        out_shape=jax.ShapeDtypeStruct((owners, own * blocks // owners, W), jnp.bfloat16),
        in_specs=[whole_vmem()] * (1 + len(tables)),
        out_specs=whole_vmem(),
        scratch_shapes=[
            pltpu.VMEM((blocks, W * (own + 1)), jnp.bfloat16),
            pltpu.VMEM((2 * blocks, W * own), jnp.bfloat16),
            pltpu.VMEM((own, blocks, W), jnp.float32),
            pltpu.VMEM((2 * W, 2 * W), jnp.bfloat16),
            pltpu.VMEM((2 * W, 2 * W), jnp.bfloat16),
        ],
        compiler_params=pltpu.CompilerParams(vmem_limit_bytes=32 * 2**20),
        cost_estimate=pl.CostEstimate(flops=blocks * W, bytes_accessed=4 * blocks * W, transcendentals=0),
        name="convolve",
    )(got, *tables)


def unpack_kernel(own, got_ref, *rest):
    gate_refs, (out_ref, flat, gate_s) = rest[:-3], rest[-3:]
    sources, rows, _ = got_ref.shape
    some = rows // own
    me = lax.axis_index("ch")
    channels = gate_refs[0].shape[0]
    for d, gate_ref in enumerate(gate_refs):
        first = pl.multiple_of(jnp.bitwise_xor(me, d) * channels, TILE)
        gate_s[pl.ds(first, channels), :] = gate_ref[...]
    ch_count = len(gate_refs)
    for p in range(sources):
        part = got_ref[p].astype(jnp.float32)
        first = (p % ch_count * (sources // ch_count) + p // ch_count) * rows
        for h in range(W // LANES):
            flat[h, first : first + rows, :] = part[:, LANES * h : LANES * (h + 1)]
    for j in range(some):
        for h in range(W // LANES):
            part = flat[h, pl.ds(j, sources * own, stride=some), :]
            first = W * j + LANES * h
            cols = slice(first, first + LANES)
            out_ref[:, cols] = (part * gate_s[:, cols].astype(jnp.float32)).astype(jnp.bfloat16)


def unpack(got, gates, own):
    sources, rows, _ = got.shape
    shape = (sources * own, rows // own * W)
    if rows % TILE:
        order = jnp.bitwise_xor(lax.axis_index("ch"), jnp.arange(len(gates)))
        gate = jnp.stack(gates)[order].reshape(shape)
        got = got.reshape(-1, len(gates), rows, W).swapaxes(0, 1)
        return (got.reshape(shape).astype(jnp.float32) * gate.astype(jnp.float32)).astype(jnp.bfloat16)
    return pl.pallas_call(
        functools.partial(unpack_kernel, own),
        out_shape=jax.ShapeDtypeStruct(shape, jnp.bfloat16),
        in_specs=[whole_vmem()] * (1 + len(gates)),
        out_specs=whole_vmem(),
        scratch_shapes=[
            pltpu.VMEM((W // LANES, sources * rows, LANES), jnp.float32),
            pltpu.VMEM(shape, jnp.bfloat16),
        ],
        compiler_params=pltpu.CompilerParams(vmem_limit_bytes=24 * 2**20),
        name="unpack",
    )(got, *[pltpu.with_memory_space_constraint(gate, pltpu.VMEM) for gate in gates])


def body(pre_gate, value, post_gate, filter_taps, skip):
    ctx_count = lax.axis_size("ctx")
    ch_count = lax.axis_size("ch")
    own = value.shape[0] // ctx_count
    blocks = value.shape[1] // W * ctx_count
    send, *gates = pack(pre_gate, value, post_gate, filter_taps, ctx_count, ch_count)
    got = lax.all_to_all(send, "ctx", split_axis=0, concat_axis=0, tiled=True)
    for d in reversed(range(1, ch_count)):
        gates[d] = lax.ppermute(gates[d], "ch", [(i, i ^ d) for i in range(ch_count)])
    tables, skip, _ = lax.optimization_barrier((dft_tables(blocks), skip, send))
    tables = make_tables(skip, *tables, own)
    mixed = convolve(got, tables, own, ch_count)
    mixed, gates = lax.optimization_barrier((mixed, gates))
    mixed = lax.all_to_all(mixed, ("ctx", "ch"), split_axis=0, concat_axis=0, tiled=True)
    return unpack(mixed, gates, own)


def solution(mesh):
    placed = (P("ch", "ctx"), P("ch", "ctx"), P("ch", "ctx"), P("ch", "ctx"), P("ch"))
    return jax.shard_map(
        body, mesh=mesh, in_specs=placed, out_specs=P(None, ("ctx", "ch")), check_vma=False
    )
```

```python
import functools

import jax
import jax.numpy as jnp
import numpy as np
from jax import lax
from jax.experimental import pallas as pl
from jax.experimental.pallas import tpu as pltpu
from jax.sharding import PartitionSpec as P

W = 256
LANES = 128
TILE = 16
CHUNK = 128


def whole_vmem():
    return pl.BlockSpec(memory_space=pltpu.VMEM)


def in_hbm():
    return pl.BlockSpec(memory_space=pltpu.HBM)


def dft_tables(blocks):
    length = blocks * W
    k = np.arange(blocks)[:, None]
    angle = 2 * np.pi * ((4 * k + 1) * np.arange(blocks)[None, :] % (4 * blocks)) / (4 * blocks)
    outer = np.concatenate([np.cos(angle), -np.sin(angle)], 0)
    turn = 2 * np.pi * ((4 * k + 1) * np.arange(W)[None, :]) / (4 * length)
    near = 2 * np.pi * (np.arange(W)[:, None] * np.arange(W)[None, :] % W) / W
    inner = np.concatenate([np.cos(near), np.sin(near)], 0)
    turns = np.concatenate([np.cos(turn), np.sin(turn)], 1)
    return [jnp.asarray(table, jnp.float32) for table in (outer, inner, turns)]


def lay(natural, j, value):
    count = value.shape[0]
    for h in range(W // LANES):
        first = (j * (W // LANES) + h) * count
        natural[first : first + count, :] = value[:, LANES * h : LANES * (h + 1)]


def pick(natural, channel, count, blocks):
    halves = W // LANES
    rows = [natural[pl.ds(h * count + channel, blocks, stride=halves * count), :] for h in range(halves)]
    return jnp.concatenate(rows, 1)


def early_blocks(own, near, ch_count):
    some = near // ch_count // 2
    return some if own * some % TILE == 0 else 0


def pack_kernel(own, blocks, group, ch_count, pre_ref, val_ref, taps_ref, post_ref, out_ref, *rest):
    gate_refs = rest[:ch_count]
    pre_s, val_s, taps_s, post_s, natural, natural_taps, natural_gate, stage, in_sems, out_sems, gate_sems = rest[ch_count:]
    parts = out_ref.shape[0]
    channels = own * parts
    some = min(TILE, channels)
    rows = own * blocks
    main = rows + blocks
    early = early_blocks(own, blocks, ch_count)
    loads = []
    for g in range(channels // some):
        here = pl.ds(g * some, some)
        loads.append(pltpu.make_async_copy(pre_ref.at[here], pre_s.at[here], in_sems.at[g, 0]))
        loads.append(pltpu.make_async_copy(val_ref.at[here], val_s.at[here], in_sems.at[g, 1]))
    taps_load = pltpu.make_async_copy(taps_ref, taps_s, in_sems.at[channels // some, 0])
    gate_load = pltpu.make_async_copy(post_ref, post_s, in_sems.at[channels // some, 1])
    for copy in loads[:2] + [taps_load] + loads[2:] + [gate_load]:
        copy.start()
    groups = taps_s.shape[0]
    taps_load.wait()
    for j in range(blocks):
        lay(natural_taps, j, taps_s[:, W * j : W * (j + 1)])
    stores = []
    for g in range(channels // some):
        loads[2 * g].wait()
        loads[2 * g + 1].wait()
        here = slice(g * some, (g + 1) * some)
        for j in range(blocks):
            cols = slice(W * j, W * (j + 1))
            product = pre_s[here, cols].astype(jnp.float32) * val_s[here, cols].astype(jnp.float32)
            lay(natural.at[g], j, product)
        for i in range(g * some // own, (g + 1) * some // own):
            for c in range(own):
                mine = pick(natural.at[g], own * i + c - g * some, some, blocks)
                stage[i, blocks * c : blocks * (c + 1), :] = mine.astype(jnp.bfloat16)
            taps = pick(natural_taps, own * i // group, groups, blocks)
            stage[i, rows:main, :] = taps.astype(jnp.bfloat16)
            stores.append(pltpu.make_async_copy(stage.at[i, 0:main], out_ref.at[i, 0:main], out_sems.at[i, 0]))
            stores[-1].start()
    gate_load.wait()
    me = lax.axis_index("ch")
    piece = blocks * W // ch_count
    for d in range(ch_count):
        first = jnp.bitwise_xor(me, d) * piece
        width = piece
        if d == ch_count - 1 and early:
            for j in range(early):
                cols = pl.ds(pl.multiple_of(first + W * j, LANES), W)
                lay(natural_gate, j, post_s[:, cols].astype(jnp.float32))
            first = first + W * early
            width = piece - W * early
        cols = pl.ds(pl.multiple_of(first, LANES), width)
        stores.append(pltpu.make_async_copy(post_s.at[:, cols], gate_refs[d], gate_sems.at[d]))
        stores[-1].start()
    if early:
        for i in range(parts):
            gate = [pick(natural_gate, own * i + c, channels, early) for c in range(own)]
            stage[i, main:, :] = jnp.concatenate(gate, 0).astype(jnp.bfloat16)
            stores.append(pltpu.make_async_copy(stage.at[i, main:], out_ref.at[i, main:], out_sems.at[i, 1]))
            stores[-1].start()
    for copy in stores:
        copy.wait()


def pack(pre_gate, value, post_gate, taps, parts, ch_count):
    channels, block = value.shape
    own = channels // parts
    group = channels // taps.shape[0]
    blocks = block // W
    early = early_blocks(own, blocks, ch_count)
    local = (own + 1) * blocks + own * early
    halves = W // LANES
    some = min(TILE, channels)
    piece = block // ch_count
    widths = [piece] * (ch_count - 1) + [piece - W * early]
    args = [pltpu.with_memory_space_constraint(arg, pltpu.HBM) for arg in (pre_gate, value, taps, post_gate)]
    return pl.pallas_call(
        functools.partial(pack_kernel, own, blocks, group, ch_count),
        out_shape=[jax.ShapeDtypeStruct((parts, local, W), jnp.bfloat16)]
        + [jax.ShapeDtypeStruct((channels, width), jnp.bfloat16) for width in widths],
        in_specs=[in_hbm()] * 4,
        out_specs=[in_hbm()] * (1 + ch_count),
        scratch_shapes=[
            pltpu.VMEM(pre_gate.shape, jnp.bfloat16),
            pltpu.VMEM(value.shape, jnp.bfloat16),
            pltpu.VMEM(taps.shape, jnp.float32),
            pltpu.VMEM(post_gate.shape, jnp.bfloat16),
            pltpu.VMEM((channels // some, blocks * halves * some, LANES), jnp.float32),
            pltpu.VMEM((blocks * halves * taps.shape[0], LANES), jnp.float32),
            pltpu.VMEM((max(early, 1) * halves * channels, LANES), jnp.float32),
            pltpu.VMEM((parts, local, W), jnp.bfloat16),
            pltpu.SemaphoreType.DMA((channels // some + 1, 2)),
            pltpu.SemaphoreType.DMA((parts, 2)),
            pltpu.SemaphoreType.DMA((ch_count,)),
        ],
        compiler_params=pltpu.CompilerParams(vmem_limit_bytes=16 * 2**20),
        name="pack",
    )(*args)


def tables_kernel(own, skip_ref, outer_ref, inner_ref, turns_ref, outer_out, inner_out, turns_out, outer_s, inner_s, sems):
    count, width = turns_ref.shape
    loads = [
        pltpu.make_async_copy(outer_ref, outer_s, sems.at[0]),
        pltpu.make_async_copy(inner_ref, inner_s, sems.at[1]),
        pltpu.make_async_copy(turns_ref, turns_out.at[0:count, :], sems.at[2]),
    ]
    for copy in loads:
        copy.start()
    me = lax.axis_index("ctx")
    for c in range(own):
        turns_out[count + 8 * c : count + 8 * (c + 1), :] = jnp.full((8, width), skip_ref[own * me + c], jnp.float32)
    loads[0].wait()
    outer_out[...] = outer_s[...].astype(jnp.bfloat16)
    loads[1].wait()
    inner_out[...] = inner_s[...].astype(jnp.bfloat16)
    loads[2].wait()


def make_tables(skip, outer, inner, turns, own):
    count, width = turns.shape
    args = [pltpu.with_memory_space_constraint(arg, pltpu.HBM) for arg in (outer, inner, turns)]
    return pl.pallas_call(
        functools.partial(tables_kernel, own),
        out_shape=[
            jax.ShapeDtypeStruct(outer.shape, jnp.bfloat16),
            jax.ShapeDtypeStruct(inner.shape, jnp.bfloat16),
            jax.ShapeDtypeStruct((count + 8 * own, width), jnp.float32),
        ],
        in_specs=[pl.BlockSpec(memory_space=pltpu.SMEM)] + [in_hbm()] * 3,
        out_specs=[whole_vmem()] * 3,
        scratch_shapes=[
            pltpu.VMEM(outer.shape, jnp.float32),
            pltpu.VMEM(inner.shape, jnp.float32),
            pltpu.SemaphoreType.DMA((3,)),
        ],
        compiler_params=pltpu.CompilerParams(vmem_limit_bytes=12 * 2**20),
        name="make_tables",
    )(skip, *args)


def conv_kernel(own, near, ch_count, got_ref, outer_ref, inner_ref, turns_ref, out_ref, x_all, r_all, z_all, ahead, rear):
    parts = got_ref.shape[0]
    blocks = parts * near
    length = blocks * W
    for p in range(parts):
        for c in range(own + 1):
            x_all[p * near : (p + 1) * near, W * c : W * (c + 1)] = got_ref[p, c * near : (c + 1) * near, :]

    near_cos, near_sin = inner_ref[0:W, :], inner_ref[W:, :]
    for table, sign in ((ahead, -1), (rear, 1)):
        table[0:W, 0:W] = near_cos
        table[0:W, W:] = near_sin * sign
        table[W:, 0:W] = near_sin * -sign
        table[W:, W:] = near_cos

    def dot(left, right):
        return jnp.dot(left, right, preferred_element_type=jnp.float32)

    for first in range(0, blocks, CHUNK):
        here = slice(first, first + CHUNK)
        there = slice(blocks + first, blocks + first + CHUNK)
        both = dot(jnp.concatenate([outer_ref[here, :], outer_ref[there, :]], 0), x_all[...])
        real, imag = both[0:CHUNK, :], both[CHUNK:, :]
        turn_cos, turn_sin = turns_ref[here, 0:W], turns_ref[here, W:]
        rows = []
        for c in range(own + 1):
            re, im = real[:, W * c : W * (c + 1)], imag[:, W * c : W * (c + 1)]
            pair = [re * turn_cos + im * turn_sin, im * turn_cos - re * turn_sin]
            rows.append(jnp.concatenate(pair, 1).astype(jnp.bfloat16))
        spectrum = dot(jnp.concatenate(rows, 0), ahead[...])
        filt_re = spectrum[CHUNK * own :, 0:W] * (1.0 / length)
        filt_im = spectrum[CHUNK * own :, W:] * (1.0 / length)
        rows = []
        for c in range(own):
            part = spectrum[CHUNK * c : CHUNK * (c + 1), :]
            re, im = part[:, 0:W], part[:, W:]
            pair = [re * filt_re - im * filt_im, re * filt_im + im * filt_re]
            rows.append(jnp.concatenate(pair, 1).astype(jnp.bfloat16))
        middle = dot(jnp.concatenate(rows, 0), rear[...])
        for c in range(own):
            part = middle[CHUNK * c : CHUNK * (c + 1), :]
            re, im = part[:, 0:W], part[:, W:]
            cols = slice(W * c, W * (c + 1))
            r_all[here, cols] = (re * turn_cos - im * turn_sin).astype(jnp.bfloat16)
            r_all[there, cols] = (re * turn_sin + im * turn_cos).astype(jnp.bfloat16)

    conv = lax.dot_general(
        outer_ref[...], r_all[...], (((0,), (0,)), ((), ())), preferred_element_type=jnp.float32
    )
    for c in range(own):
        cols = slice(W * c, W * (c + 1))
        z_all[c] = conv[:, cols] + turns_ref[blocks + 8 * c : blocks + 8 * c + 1, 0:W] * x_all[:, cols].astype(jnp.float32)
    some = out_ref.shape[1] // own
    early = early_blocks(own, near, ch_count)
    far = jnp.bitwise_xor(lax.axis_index("ch"), ch_count - 1)
    for k in range(parts):
        factors = []
        if early:
            gate = got_ref[k, (own + 1) * near :, :].astype(jnp.float32)
            for c in range(own):
                rest = jnp.ones((some - early, W), jnp.float32)
                factors.append(jnp.concatenate([gate[early * c : early * (c + 1), :], rest], 0))
        for m in range(ch_count):
            first = k * near + m * some
            rows = [z_all[c, first : first + some, :] for c in range(own)]
            if early:
                rows = [jnp.where(far == m, factors[c], 1.0) * rows[c] for c in range(own)]
            out_ref[k * ch_count + m] = jnp.concatenate(rows, 0).astype(jnp.bfloat16)


def convolve(got, tables, own, near, ch_count):
    parts = got.shape[0]
    blocks = parts * near
    owners = parts * ch_count
    return pl.pallas_call(
        functools.partial(conv_kernel, own, near, ch_count),
        out_shape=jax.ShapeDtypeStruct((owners, own * blocks // owners, W), jnp.bfloat16),
        in_specs=[whole_vmem()] * (1 + len(tables)),
        out_specs=whole_vmem(),
        scratch_shapes=[
            pltpu.VMEM((blocks, W * (own + 1)), jnp.bfloat16),
            pltpu.VMEM((2 * blocks, W * own), jnp.bfloat16),
            pltpu.VMEM((own, blocks, W), jnp.float32),
            pltpu.VMEM((2 * W, 2 * W), jnp.bfloat16),
            pltpu.VMEM((2 * W, 2 * W), jnp.bfloat16),
        ],
        compiler_params=pltpu.CompilerParams(vmem_limit_bytes=32 * 2**20),
        cost_estimate=pl.CostEstimate(flops=blocks * W, bytes_accessed=4 * blocks * W, transcendentals=0),
        name="convolve",
    )(got, *tables)


def unpack_kernel(own, got_ref, *rest):
    gate_refs, (out_ref, flat, gate_s) = rest[:-3], rest[-3:]
    sources, rows, _ = got_ref.shape
    some = rows // own
    me = lax.axis_index("ch")
    channels = gate_refs[0].shape[0]
    for d, gate_ref in enumerate(gate_refs):
        here = pl.ds(pl.multiple_of(jnp.bitwise_xor(me, d) * channels, TILE), channels)
        early = gate_s.shape[1] - gate_ref.shape[1]
        if early:
            gate_s[here, 0:early] = jnp.ones((channels, early), jnp.bfloat16)
        gate_s[here, early:] = gate_ref[...]
    ch_count = len(gate_refs)
    for p in range(sources):
        part = got_ref[p].astype(jnp.float32)
        first = (p % ch_count * (sources // ch_count) + p // ch_count) * rows
        for h in range(W // LANES):
            flat[h, first : first + rows, :] = part[:, LANES * h : LANES * (h + 1)]
    for j in range(some):
        for h in range(W // LANES):
            part = flat[h, pl.ds(j, sources * own, stride=some), :]
            first = W * j + LANES * h
            cols = slice(first, first + LANES)
            out_ref[:, cols] = (part * gate_s[:, cols].astype(jnp.float32)).astype(jnp.bfloat16)


def unpack(got, gates, own):
    sources, rows, _ = got.shape
    shape = (sources * own, rows // own * W)
    if rows % TILE:
        order = jnp.bitwise_xor(lax.axis_index("ch"), jnp.arange(len(gates)))
        gate = jnp.stack(gates)[order].reshape(shape)
        got = got.reshape(-1, len(gates), rows, W).swapaxes(0, 1)
        return (got.reshape(shape).astype(jnp.float32) * gate.astype(jnp.float32)).astype(jnp.bfloat16)
    return pl.pallas_call(
        functools.partial(unpack_kernel, own),
        out_shape=jax.ShapeDtypeStruct(shape, jnp.bfloat16),
        in_specs=[whole_vmem()] * (1 + len(gates)),
        out_specs=whole_vmem(),
        scratch_shapes=[
            pltpu.VMEM((W // LANES, sources * rows, LANES), jnp.float32),
            pltpu.VMEM(shape, jnp.bfloat16),
        ],
        compiler_params=pltpu.CompilerParams(vmem_limit_bytes=24 * 2**20),
        name="unpack",
    )(got, *[pltpu.with_memory_space_constraint(gate, pltpu.VMEM) for gate in gates])


def body(pre_gate, value, post_gate, filter_taps, skip):
    ctx_count = lax.axis_size("ctx")
    ch_count = lax.axis_size("ch")
    own = value.shape[0] // ctx_count
    blocks = value.shape[1] // W * ctx_count
    send, *gates = pack(pre_gate, value, post_gate, filter_taps, ctx_count, ch_count)
    got = lax.all_to_all(send, "ctx", split_axis=0, concat_axis=0, tiled=True)
    for d in reversed(range(1, ch_count)):
        gates[d] = lax.ppermute(gates[d], "ch", [(i, i ^ d) for i in range(ch_count)])
    tables, skip, _ = lax.optimization_barrier((dft_tables(blocks), skip, send))
    tables = make_tables(skip, *tables, own)
    mixed = convolve(got, tables, own, blocks // ctx_count, ch_count)
    mixed, gates = lax.optimization_barrier((mixed, gates))
    mixed = lax.all_to_all(mixed, ("ctx", "ch"), split_axis=0, concat_axis=0, tiled=True)
    return unpack(mixed, gates, own)


def solution(mesh):
    placed = (P("ch", "ctx"), P("ch", "ctx"), P("ch", "ctx"), P("ch", "ctx"), P("ch"))
    return jax.shard_map(
        body, mesh=mesh, in_specs=placed, out_specs=P(None, ("ctx", "ch")), check_vma=False
    )
```

```python
import functools

import jax
import jax.numpy as jnp
import numpy as np
from jax import lax
from jax.experimental import pallas as pl
from jax.experimental.pallas import tpu as pltpu
from jax.sharding import PartitionSpec as P

W = 256
LANES = 128
TILE = 16
CHUNK = 128


def whole_vmem():
    return pl.BlockSpec(memory_space=pltpu.VMEM)


def in_hbm():
    return pl.BlockSpec(memory_space=pltpu.HBM)


def dft_tables(blocks):
    length = blocks * W
    k = np.arange(blocks)[:, None]
    angle = 2 * np.pi * ((4 * k + 1) * np.arange(blocks)[None, :] % (4 * blocks)) / (4 * blocks)
    outer = np.concatenate([np.cos(angle), -np.sin(angle)], 0)
    turn = 2 * np.pi * ((4 * k + 1) * np.arange(W)[None, :]) / (4 * length)
    near = 2 * np.pi * (np.arange(W)[:, None] * np.arange(W)[None, :] % W) / W
    inner = np.concatenate([np.cos(near), np.sin(near)], 0)
    turns = np.concatenate([np.cos(turn), np.sin(turn)], 1)
    return [jnp.asarray(table, jnp.float32) for table in (outer, inner, turns)]


def lay(natural, j, value):
    count = value.shape[0]
    for h in range(W // LANES):
        first = (j * (W // LANES) + h) * count
        natural[first : first + count, :] = value[:, LANES * h : LANES * (h + 1)]


def pick(natural, channel, count, blocks):
    halves = W // LANES
    rows = [natural[pl.ds(h * count + channel, blocks, stride=halves * count), :] for h in range(halves)]
    return jnp.concatenate(rows, 1)


def pack_kernel(own, blocks, group, ch_count, parts, pre_ref, val_ref, taps_ref, post_ref, *rest):
    out_refs, gate_refs = rest[:parts], rest[parts : parts + ch_count // 2]
    pre_s, val_s, taps_s, post_s, natural, natural_taps, natural_gate, stage, in_sems = rest[parts + ch_count // 2 :]
    channels = own * parts
    some = min(TILE, channels)
    rows = own * blocks
    main = rows + blocks
    loads = []
    for g in range(channels // some):
        here = pl.ds(g * some, some)
        loads.append(pltpu.make_async_copy(pre_ref.at[here], pre_s.at[here], in_sems.at[g, 0]))
        loads.append(pltpu.make_async_copy(val_ref.at[here], val_s.at[here], in_sems.at[g, 1]))
    taps_load = pltpu.make_async_copy(taps_ref, taps_s, in_sems.at[channels // some, 0])
    gate_load = pltpu.make_async_copy(post_ref, post_s, in_sems.at[channels // some, 1])
    for copy in loads[:2] + [taps_load] + loads[2:] + [gate_load]:
        copy.start()
    groups = taps_s.shape[0]
    taps_load.wait()
    for j in range(blocks):
        lay(natural_taps, j, taps_s[:, W * j : W * (j + 1)])
    for g in range(channels // some):
        loads[2 * g].wait()
        loads[2 * g + 1].wait()
        here = slice(g * some, (g + 1) * some)
        for j in range(blocks):
            cols = slice(W * j, W * (j + 1))
            product = pre_s[here, cols].astype(jnp.float32) * val_s[here, cols].astype(jnp.float32)
            lay(natural.at[g], j, product)
        for i in range(g * some // own, (g + 1) * some // own):
            for c in range(own):
                mine = pick(natural.at[g], own * i + c - g * some, some, blocks)
                stage[i, blocks * c : blocks * (c + 1), :] = mine.astype(jnp.bfloat16)
            taps = pick(natural_taps, own * i // group, groups, blocks)
            stage[i, rows:main, :] = taps.astype(jnp.bfloat16)
    gate_load.wait()
    place = lax.axis_index("ch")
    piece = blocks // ch_count
    for d in range(ch_count):
        first = jnp.bitwise_xor(place, d) * (piece * W)
        if d < ch_count // 2:
            gate_refs[d][...] = post_s[:, pl.ds(pl.multiple_of(first, LANES), piece * W)]
        else:
            for j in range(piece):
                cols = pl.ds(pl.multiple_of(first + W * j, LANES), W)
                lay(natural_gate, (d - ch_count // 2) * piece + j, post_s[:, cols].astype(jnp.float32))
    early = piece * (ch_count - ch_count // 2)
    for i in range(parts):
        gate = [pick(natural_gate, own * i + c, channels, early) for c in range(own)]
        stage[i, main:, :] = jnp.concatenate(gate, 0).astype(jnp.bfloat16)
    me = lax.axis_index("ctx")
    for d in range(parts):
        out_refs[d][...] = stage[jnp.bitwise_xor(me, d)]


def pack(pre_gate, value, post_gate, taps, parts, ch_count):
    channels, block = value.shape
    own = channels // parts
    group = channels // taps.shape[0]
    blocks = block // W
    piece = blocks // ch_count
    early = piece * (ch_count - ch_count // 2)
    local = (own + 1) * blocks + own * early
    halves = W // LANES
    some = min(TILE, channels)
    args = [pltpu.with_memory_space_constraint(arg, pltpu.HBM) for arg in (pre_gate, value, taps, post_gate)]
    out = pl.pallas_call(
        functools.partial(pack_kernel, own, blocks, group, ch_count, parts),
        out_shape=[jax.ShapeDtypeStruct((local, W), jnp.bfloat16)] * parts
        + [jax.ShapeDtypeStruct((channels, piece * W), jnp.bfloat16)] * (ch_count // 2),
        in_specs=[in_hbm()] * 4,
        out_specs=[whole_vmem()] * (parts + ch_count // 2),
        scratch_shapes=[
            pltpu.VMEM(pre_gate.shape, jnp.bfloat16),
            pltpu.VMEM(value.shape, jnp.bfloat16),
            pltpu.VMEM(taps.shape, jnp.float32),
            pltpu.VMEM(post_gate.shape, jnp.bfloat16),
            pltpu.VMEM((channels // some, blocks * halves * some, LANES), jnp.float32),
            pltpu.VMEM((blocks * halves * taps.shape[0], LANES), jnp.float32),
            pltpu.VMEM((early * halves * channels, LANES), jnp.float32),
            pltpu.VMEM((parts, local, W), jnp.bfloat16),
            pltpu.SemaphoreType.DMA((channels // some + 1, 2)),
        ],
        compiler_params=pltpu.CompilerParams(vmem_limit_bytes=16 * 2**20),
        name="pack",
    )(*args)
    return list(out[:parts]), list(out[parts:])


def swap(piece, axis, count, d):
    return lax.ppermute(piece, axis, [(i, i ^ d) for i in range(count)])


def tables_kernel(own, skip_ref, outer_ref, inner_ref, turns_ref, outer_out, inner_out, turns_out, outer_s, inner_s, sems):
    count, width = turns_ref.shape
    loads = [
        pltpu.make_async_copy(outer_ref, outer_s, sems.at[0]),
        pltpu.make_async_copy(inner_ref, inner_s, sems.at[1]),
        pltpu.make_async_copy(turns_ref, turns_out.at[0:count, :], sems.at[2]),
    ]
    for copy in loads:
        copy.start()
    me = lax.axis_index("ctx")
    for c in range(own):
        turns_out[count + 8 * c : count + 8 * (c + 1), :] = jnp.full((8, width), skip_ref[own * me + c], jnp.float32)
    loads[0].wait()
    outer_out[...] = outer_s[...].astype(jnp.bfloat16)
    loads[1].wait()
    inner_out[...] = inner_s[...].astype(jnp.bfloat16)
    loads[2].wait()


def make_tables(skip, outer, inner, turns, own):
    count, width = turns.shape
    args = [pltpu.with_memory_space_constraint(arg, pltpu.HBM) for arg in (outer, inner, turns)]
    return pl.pallas_call(
        functools.partial(tables_kernel, own),
        out_shape=[
            jax.ShapeDtypeStruct(outer.shape, jnp.bfloat16),
            jax.ShapeDtypeStruct(inner.shape, jnp.bfloat16),
            jax.ShapeDtypeStruct((count + 8 * own, width), jnp.float32),
        ],
        in_specs=[pl.BlockSpec(memory_space=pltpu.SMEM)] + [in_hbm()] * 3,
        out_specs=[whole_vmem()] * 3,
        scratch_shapes=[
            pltpu.VMEM(outer.shape, jnp.float32),
            pltpu.VMEM(inner.shape, jnp.float32),
            pltpu.SemaphoreType.DMA((3,)),
        ],
        compiler_params=pltpu.CompilerParams(vmem_limit_bytes=12 * 2**20),
        name="make_tables",
    )(skip, *args)


def conv_kernel(own, near, ch_count, parts, *rest):
    got_refs = rest[:parts]
    outer_ref, inner_ref, turns_ref, out_ref, x_all, r_all, z_all, ahead, rear = rest[parts:]
    blocks = parts * near
    length = blocks * W
    me = lax.axis_index("ctx")
    for d in range(parts):
        here = pl.ds(pl.multiple_of(jnp.bitwise_xor(me, d) * near, TILE), near)
        for c in range(own + 1):
            x_all[here, W * c : W * (c + 1)] = got_refs[d][c * near : (c + 1) * near, :]

    near_cos, near_sin = inner_ref[0:W, :], inner_ref[W:, :]
    for table, sign in ((ahead, -1), (rear, 1)):
        table[0:W, 0:W] = near_cos
        table[0:W, W:] = near_sin * sign
        table[W:, 0:W] = near_sin * -sign
        table[W:, W:] = near_cos

    def dot(left, right):
        return jnp.dot(left, right, preferred_element_type=jnp.float32)

    for first in range(0, blocks, CHUNK):
        here = slice(first, first + CHUNK)
        there = slice(blocks + first, blocks + first + CHUNK)
        both = dot(jnp.concatenate([outer_ref[here, :], outer_ref[there, :]], 0), x_all[...])
        real, imag = both[0:CHUNK, :], both[CHUNK:, :]
        turn_cos, turn_sin = turns_ref[here, 0:W], turns_ref[here, W:]
        rows = []
        for c in range(own + 1):
            re, im = real[:, W * c : W * (c + 1)], imag[:, W * c : W * (c + 1)]
            pair = [re * turn_cos + im * turn_sin, im * turn_cos - re * turn_sin]
            rows.append(jnp.concatenate(pair, 1).astype(jnp.bfloat16))
        spectrum = dot(jnp.concatenate(rows, 0), ahead[...])
        filt_re = spectrum[CHUNK * own :, 0:W] * (1.0 / length)
        filt_im = spectrum[CHUNK * own :, W:] * (1.0 / length)
        rows = []
        for c in range(own):
            part = spectrum[CHUNK * c : CHUNK * (c + 1), :]
            re, im = part[:, 0:W], part[:, W:]
            pair = [re * filt_re - im * filt_im, re * filt_im + im * filt_re]
            rows.append(jnp.concatenate(pair, 1).astype(jnp.bfloat16))
        middle = dot(jnp.concatenate(rows, 0), rear[...])
        for c in range(own):
            part = middle[CHUNK * c : CHUNK * (c + 1), :]
            re, im = part[:, 0:W], part[:, W:]
            cols = slice(W * c, W * (c + 1))
            r_all[here, cols] = (re * turn_cos - im * turn_sin).astype(jnp.bfloat16)
            r_all[there, cols] = (re * turn_sin + im * turn_cos).astype(jnp.bfloat16)

    conv = lax.dot_general(
        outer_ref[...], r_all[...], (((0,), (0,)), ((), ())), preferred_element_type=jnp.float32
    )
    for c in range(own):
        cols = slice(W * c, W * (c + 1))
        z_all[c] = conv[:, cols] + turns_ref[blocks + 8 * c : blocks + 8 * c + 1, 0:W] * x_all[:, cols].astype(jnp.float32)
    some = out_ref.shape[1] // own
    early = some * (ch_count - ch_count // 2)
    place = lax.axis_index("ch")
    for d in range(parts):
        k = jnp.bitwise_xor(me, d)
        gate = got_refs[d][(own + 1) * near :, :].astype(jnp.float32)
        mine = [z_all[c, pl.ds(pl.multiple_of(k * near, TILE), near), :] for c in range(own)]
        for m in range(ch_count):
            rows = [part[m * some : (m + 1) * some, :] for part in mine]
            for e in range(ch_count // 2, ch_count):
                at = (e - ch_count // 2) * some
                for c in range(own):
                    factor = jnp.where(jnp.bitwise_xor(place, e) == m, gate[c * early + at : c * early + at + some, :], 1.0)
                    rows[c] = rows[c] * factor
            out_ref[k * ch_count + m] = jnp.concatenate(rows, 0).astype(jnp.bfloat16)


def convolve(got, tables, own, near, ch_count):
    parts = len(got)
    blocks = parts * near
    owners = parts * ch_count
    return pl.pallas_call(
        functools.partial(conv_kernel, own, near, ch_count, parts),
        out_shape=jax.ShapeDtypeStruct((owners, own * blocks // owners, W), jnp.bfloat16),
        in_specs=[whole_vmem()] * (parts + len(tables)),
        out_specs=whole_vmem(),
        scratch_shapes=[
            pltpu.VMEM((blocks, W * (own + 1)), jnp.bfloat16),
            pltpu.VMEM((2 * blocks, W * own), jnp.bfloat16),
            pltpu.VMEM((own, blocks, W), jnp.float32),
            pltpu.VMEM((2 * W, 2 * W), jnp.bfloat16),
            pltpu.VMEM((2 * W, 2 * W), jnp.bfloat16),
        ],
        compiler_params=pltpu.CompilerParams(vmem_limit_bytes=32 * 2**20),
        cost_estimate=pl.CostEstimate(flops=blocks * W, bytes_accessed=4 * blocks * W, transcendentals=0),
        name="convolve",
    )(*got, *tables)


def unpack_kernel(own, got_ref, *rest):
    gate_refs, (out_ref, flat, gate_s) = rest[:-3], rest[-3:]
    sources, rows, _ = got_ref.shape
    some = rows // own
    place = lax.axis_index("ch")
    channels, width = gate_refs[0].shape
    ch_count = out_ref.shape[0] // channels
    for d in range(ch_count):
        here = pl.ds(pl.multiple_of(jnp.bitwise_xor(place, d) * channels, TILE), channels)
        gate_s[here, :] = gate_refs[d][...] if d < len(gate_refs) else jnp.ones((channels, width), jnp.bfloat16)
    for p in range(sources):
        part = got_ref[p].astype(jnp.float32)
        first = (p % ch_count * (sources // ch_count) + p // ch_count) * rows
        for h in range(W // LANES):
            flat[h, first : first + rows, :] = part[:, LANES * h : LANES * (h + 1)]
    for j in range(some):
        for h in range(W // LANES):
            part = flat[h, pl.ds(j, sources * own, stride=some), :]
            first = W * j + LANES * h
            cols = slice(first, first + LANES)
            out_ref[:, cols] = (part * gate_s[:, cols].astype(jnp.float32)).astype(jnp.bfloat16)


def unpack(got, gates, own, ch_count):
    sources, rows, _ = got.shape
    shape = (sources * own, rows // own * W)
    if rows % TILE:
        ones = [jnp.ones_like(gates[0])] * (ch_count - len(gates))
        order = jnp.bitwise_xor(lax.axis_index("ch"), jnp.arange(ch_count))
        gate = jnp.stack(gates + ones)[order].reshape(shape)
        got = got.reshape(-1, ch_count, rows, W).swapaxes(0, 1)
        return (got.reshape(shape).astype(jnp.float32) * gate.astype(jnp.float32)).astype(jnp.bfloat16)
    return pl.pallas_call(
        functools.partial(unpack_kernel, own),
        out_shape=jax.ShapeDtypeStruct(shape, jnp.bfloat16),
        in_specs=[whole_vmem()] * (1 + len(gates)),
        out_specs=whole_vmem(),
        scratch_shapes=[
            pltpu.VMEM((W // LANES, sources * rows, LANES), jnp.float32),
            pltpu.VMEM(shape, jnp.bfloat16),
        ],
        compiler_params=pltpu.CompilerParams(vmem_limit_bytes=24 * 2**20),
        name="unpack",
    )(got, *[pltpu.with_memory_space_constraint(gate, pltpu.VMEM) for gate in gates])


def body(pre_gate, value, post_gate, filter_taps, skip):
    ctx_count = lax.axis_size("ctx")
    ch_count = lax.axis_size("ch")
    own = value.shape[0] // ctx_count
    near = value.shape[1] // W
    got, gates = pack(pre_gate, value, post_gate, filter_taps, ctx_count, ch_count)
    tables, skip, _ = lax.optimization_barrier((dft_tables(near * ctx_count), skip, got[0]))
    for d in range(1, ctx_count):
        got[d] = swap(got[d], "ctx", ctx_count, d)
    for d in range(1, ch_count // 2):
        gates[d] = swap(gates[d], "ch", ch_count, d)
    tables = list(make_tables(skip, *tables, own))
    mixed = convolve(got, tables, own, near, ch_count)
    mixed, gates = lax.optimization_barrier((mixed, gates))
    mixed = lax.all_to_all(mixed, ("ctx", "ch"), split_axis=0, concat_axis=0, tiled=True)
    return unpack(mixed, gates, own, ch_count)


def solution(mesh):
    placed = (P("ch", "ctx"), P("ch", "ctx"), P("ch", "ctx"), P("ch", "ctx"), P("ch"))
    return jax.shard_map(
        body, mesh=mesh, in_specs=placed, out_specs=P(None, ("ctx", "ch")), check_vma=False
    )
```

```python
import functools

import jax
import jax.numpy as jnp
import numpy as np
from jax import lax
from jax.experimental import pallas as pl
from jax.experimental.pallas import tpu as pltpu
from jax.sharding import PartitionSpec as P

W = 256
LANES = 128
TILE = 16
CHUNK = 128


def whole_vmem():
    return pl.BlockSpec(memory_space=pltpu.VMEM)


def in_hbm():
    return pl.BlockSpec(memory_space=pltpu.HBM)


def dft_tables(blocks):
    length = blocks * W
    k = np.arange(blocks)[:, None]
    angle = 2 * np.pi * ((4 * k + 1) * np.arange(blocks)[None, :] % (4 * blocks)) / (4 * blocks)
    outer = np.concatenate([np.cos(angle), -np.sin(angle)], 0)
    turn = 2 * np.pi * ((4 * k + 1) * np.arange(W)[None, :]) / (4 * length)
    near = 2 * np.pi * (np.arange(W)[:, None] * np.arange(W)[None, :] % W) / W
    inner = np.concatenate([np.cos(near), np.sin(near)], 0)
    turns = np.concatenate([np.cos(turn), np.sin(turn)], 1)
    return [jnp.asarray(table, jnp.float32) for table in (outer, inner, turns)]


def lay(natural, j, value):
    count = value.shape[0]
    for h in range(W // LANES):
        first = (j * (W // LANES) + h) * count
        natural[first : first + count, :] = value[:, LANES * h : LANES * (h + 1)]


def pick(natural, channel, count, blocks):
    halves = W // LANES
    rows = [natural[pl.ds(h * count + channel, blocks, stride=halves * count), :] for h in range(halves)]
    return jnp.concatenate(rows, 1)


def pack_kernel(own, blocks, group, ch_count, parts, pre_ref, val_ref, taps_ref, post_ref, *rest):
    out_refs, gate_refs = rest[:parts], rest[parts : parts + ch_count // 2]
    pre_s, val_s, taps_s, post_s, natural, natural_taps, natural_gate, stage, in_sems = rest[parts + ch_count // 2 :]
    channels = own * parts
    some = min(TILE, channels)
    rows = own * blocks
    main = rows + blocks
    loads = []
    for g in range(channels // some):
        here = pl.ds(g * some, some)
        loads.append(pltpu.make_async_copy(pre_ref.at[here], pre_s.at[here], in_sems.at[g, 0]))
        loads.append(pltpu.make_async_copy(val_ref.at[here], val_s.at[here], in_sems.at[g, 1]))
    taps_load = pltpu.make_async_copy(taps_ref, taps_s, in_sems.at[channels // some, 0])
    gate_load = pltpu.make_async_copy(post_ref, post_s, in_sems.at[channels // some, 1])
    for copy in loads[:2] + [taps_load] + loads[2:] + [gate_load]:
        copy.start()
    groups = taps_s.shape[0]
    taps_load.wait()
    for j in range(blocks):
        lay(natural_taps, j, taps_s[:, W * j : W * (j + 1)])
    for g in range(channels // some):
        loads[2 * g].wait()
        loads[2 * g + 1].wait()
        here = slice(g * some, (g + 1) * some)
        for j in range(blocks):
            cols = slice(W * j, W * (j + 1))
            product = pre_s[here, cols].astype(jnp.float32) * val_s[here, cols].astype(jnp.float32)
            lay(natural.at[g], j, product)
        for i in range(g * some // own, (g + 1) * some // own):
            for c in range(own):
                mine = pick(natural.at[g], own * i + c - g * some, some, blocks)
                stage[i, blocks * c : blocks * (c + 1), :] = mine.astype(jnp.bfloat16)
            taps = pick(natural_taps, own * i // group, groups, blocks)
            stage[i, rows:main, :] = taps.astype(jnp.bfloat16)
    gate_load.wait()
    place = lax.axis_index("ch")
    piece = blocks // ch_count
    for d in range(ch_count):
        first = jnp.bitwise_xor(place, d) * (piece * W)
        if d < ch_count // 2:
            gate_refs[d][...] = post_s[:, pl.ds(pl.multiple_of(first, LANES), piece * W)]
        else:
            for j in range(piece):
                cols = pl.ds(pl.multiple_of(first + W * j, LANES), W)
                lay(natural_gate, (d - ch_count // 2) * piece + j, post_s[:, cols].astype(jnp.float32))
    early = piece * (ch_count - ch_count // 2)
    for i in range(parts):
        gate = [pick(natural_gate, own * i + c, channels, early) for c in range(own)]
        stage[i, main:, :] = jnp.concatenate(gate, 0).astype(jnp.bfloat16)
    me = lax.axis_index("ctx")
    for d in range(parts):
        out_refs[d][...] = stage[jnp.bitwise_xor(me, d)]


def pack(pre_gate, value, post_gate, taps, parts, ch_count):
    channels, block = value.shape
    own = channels // parts
    group = channels // taps.shape[0]
    blocks = block // W
    piece = blocks // ch_count
    early = piece * (ch_count - ch_count // 2)
    local = (own + 1) * blocks + own * early
    halves = W // LANES
    some = min(TILE, channels)
    args = [pltpu.with_memory_space_constraint(arg, pltpu.HBM) for arg in (pre_gate, value, taps, post_gate)]
    out = pl.pallas_call(
        functools.partial(pack_kernel, own, blocks, group, ch_count, parts),
        out_shape=[jax.ShapeDtypeStruct((local, W), jnp.bfloat16)] * parts
        + [jax.ShapeDtypeStruct((channels, piece * W), jnp.bfloat16)] * (ch_count // 2),
        in_specs=[in_hbm()] * 4,
        out_specs=[whole_vmem()] * (parts + ch_count // 2),
        scratch_shapes=[
            pltpu.VMEM(pre_gate.shape, jnp.bfloat16),
            pltpu.VMEM(value.shape, jnp.bfloat16),
            pltpu.VMEM(taps.shape, jnp.float32),
            pltpu.VMEM(post_gate.shape, jnp.bfloat16),
            pltpu.VMEM((channels // some, blocks * halves * some, LANES), jnp.float32),
            pltpu.VMEM((blocks * halves * taps.shape[0], LANES), jnp.float32),
            pltpu.VMEM((early * halves * channels, LANES), jnp.float32),
            pltpu.VMEM((parts, local, W), jnp.bfloat16),
            pltpu.SemaphoreType.DMA((channels // some + 1, 2)),
        ],
        compiler_params=pltpu.CompilerParams(vmem_limit_bytes=16 * 2**20),
        name="pack",
    )(*args)
    return list(out[:parts]), list(out[parts:])


def partner_order(count):
    corners = [d for d in range(1, count) if bin(d >> 1).count("1") > 1]
    straight = [d for d in range(count - 1, 1, -1) if bin(d >> 1).count("1") == 1 and d % 2 == 0]
    order = [0]
    for n in range(max(len(corners), len(straight))):
        order += straight[n : n + 1] + corners[n : n + 1]
    return order + [d for d in range(count - 1, 0, -1) if d not in order][::-1][1:] + [1]


def swap(piece, axis, count, d):
    return lax.ppermute(piece, axis, [(i, i ^ d) for i in range(count)])


def tables_kernel(own, skip_ref, outer_ref, inner_ref, turns_ref, outer_out, inner_out, turns_out, outer_s, inner_s, sems):
    count, width = turns_ref.shape
    loads = [
        pltpu.make_async_copy(outer_ref, outer_s, sems.at[0]),
        pltpu.make_async_copy(inner_ref, inner_s, sems.at[1]),
        pltpu.make_async_copy(turns_ref, turns_out.at[0:count, :], sems.at[2]),
    ]
    for copy in loads:
        copy.start()
    me = lax.axis_index("ctx")
    for c in range(own):
        turns_out[count + 8 * c : count + 8 * (c + 1), :] = jnp.full((8, width), skip_ref[own * me + c], jnp.float32)
    loads[0].wait()
    outer_out[...] = outer_s[...].astype(jnp.bfloat16)
    loads[1].wait()
    inner_out[...] = inner_s[...].astype(jnp.bfloat16)
    loads[2].wait()


def make_tables(skip, outer, inner, turns, own):
    count, width = turns.shape
    args = [pltpu.with_memory_space_constraint(arg, pltpu.HBM) for arg in (outer, inner, turns)]
    return pl.pallas_call(
        functools.partial(tables_kernel, own),
        out_shape=[
            jax.ShapeDtypeStruct(outer.shape, jnp.bfloat16),
            jax.ShapeDtypeStruct(inner.shape, jnp.bfloat16),
            jax.ShapeDtypeStruct((count + 8 * own, width), jnp.float32),
        ],
        in_specs=[pl.BlockSpec(memory_space=pltpu.SMEM)] + [in_hbm()] * 3,
        out_specs=[whole_vmem()] * 3,
        scratch_shapes=[
            pltpu.VMEM(outer.shape, jnp.float32),
            pltpu.VMEM(inner.shape, jnp.float32),
            pltpu.SemaphoreType.DMA((3,)),
        ],
        compiler_params=pltpu.CompilerParams(vmem_limit_bytes=12 * 2**20),
        name="make_tables",
    )(skip, *args)


def conv_kernel(own, near, ch_count, parts, *rest):
    got_refs = rest[:parts]
    outer_ref, inner_ref, turns_ref, out_ref, x_all, r_all, z_all, ahead, rear = rest[parts:]
    blocks = parts * near
    length = blocks * W
    me = lax.axis_index("ctx")
    order = partner_order(parts)
    for d, got_ref in zip(order, got_refs):
        here = pl.ds(pl.multiple_of(jnp.bitwise_xor(me, d) * near, TILE), near)
        for c in range(own + 1):
            x_all[here, W * c : W * (c + 1)] = got_ref[c * near : (c + 1) * near, :]

    near_cos, near_sin = inner_ref[0:W, :], inner_ref[W:, :]
    for table, sign in ((ahead, -1), (rear, 1)):
        table[0:W, 0:W] = near_cos
        table[0:W, W:] = near_sin * sign
        table[W:, 0:W] = near_sin * -sign
        table[W:, W:] = near_cos

    def dot(left, right):
        return jnp.dot(left, right, preferred_element_type=jnp.float32)

    for first in range(0, blocks, CHUNK):
        here = slice(first, first + CHUNK)
        there = slice(blocks + first, blocks + first + CHUNK)
        both = dot(jnp.concatenate([outer_ref[here, :], outer_ref[there, :]], 0), x_all[...])
        real, imag = both[0:CHUNK, :], both[CHUNK:, :]
        turn_cos, turn_sin = turns_ref[here, 0:W], turns_ref[here, W:]
        rows = []
        for c in range(own + 1):
            re, im = real[:, W * c : W * (c + 1)], imag[:, W * c : W * (c + 1)]
            pair = [re * turn_cos + im * turn_sin, im * turn_cos - re * turn_sin]
            rows.append(jnp.concatenate(pair, 1).astype(jnp.bfloat16))
        spectrum = dot(jnp.concatenate(rows, 0), ahead[...])
        filt_re = spectrum[CHUNK * own :, 0:W] * (1.0 / length)
        filt_im = spectrum[CHUNK * own :, W:] * (1.0 / length)
        rows = []
        for c in range(own):
            part = spectrum[CHUNK * c : CHUNK * (c + 1), :]
            re, im = part[:, 0:W], part[:, W:]
            pair = [re * filt_re - im * filt_im, re * filt_im + im * filt_re]
            rows.append(jnp.concatenate(pair, 1).astype(jnp.bfloat16))
        middle = dot(jnp.concatenate(rows, 0), rear[...])
        for c in range(own):
            part = middle[CHUNK * c : CHUNK * (c + 1), :]
            re, im = part[:, 0:W], part[:, W:]
            cols = slice(W * c, W * (c + 1))
            r_all[here, cols] = (re * turn_cos - im * turn_sin).astype(jnp.bfloat16)
            r_all[there, cols] = (re * turn_sin + im * turn_cos).astype(jnp.bfloat16)

    conv = lax.dot_general(
        outer_ref[...], r_all[...], (((0,), (0,)), ((), ())), preferred_element_type=jnp.float32
    )
    for c in range(own):
        cols = slice(W * c, W * (c + 1))
        z_all[c] = conv[:, cols] + turns_ref[blocks + 8 * c : blocks + 8 * c + 1, 0:W] * x_all[:, cols].astype(jnp.float32)
    some = out_ref.shape[1] // own
    early = some * (ch_count - ch_count // 2)
    place = lax.axis_index("ch")
    for d, got_ref in zip(order, got_refs):
        k = jnp.bitwise_xor(me, d)
        gate = got_ref[(own + 1) * near :, :].astype(jnp.float32)
        mine = [z_all[c, pl.ds(pl.multiple_of(k * near, TILE), near), :] for c in range(own)]
        for m in range(ch_count):
            rows = [part[m * some : (m + 1) * some, :] for part in mine]
            for e in range(ch_count // 2, ch_count):
                at = (e - ch_count // 2) * some
                for c in range(own):
                    factor = jnp.where(jnp.bitwise_xor(place, e) == m, gate[c * early + at : c * early + at + some, :], 1.0)
                    rows[c] = rows[c] * factor
            out_ref[k * ch_count + m] = jnp.concatenate(rows, 0).astype(jnp.bfloat16)


def convolve(got, tables, own, near, ch_count):
    parts = len(got)
    blocks = parts * near
    owners = parts * ch_count
    return pl.pallas_call(
        functools.partial(conv_kernel, own, near, ch_count, parts),
        out_shape=jax.ShapeDtypeStruct((owners, own * blocks // owners, W), jnp.bfloat16),
        in_specs=[whole_vmem()] * (parts + len(tables)),
        out_specs=whole_vmem(),
        scratch_shapes=[
            pltpu.VMEM((blocks, W * (own + 1)), jnp.bfloat16),
            pltpu.VMEM((2 * blocks, W * own), jnp.bfloat16),
            pltpu.VMEM((own, blocks, W), jnp.float32),
            pltpu.VMEM((2 * W, 2 * W), jnp.bfloat16),
            pltpu.VMEM((2 * W, 2 * W), jnp.bfloat16),
        ],
        compiler_params=pltpu.CompilerParams(vmem_limit_bytes=32 * 2**20),
        cost_estimate=pl.CostEstimate(flops=blocks * W, bytes_accessed=4 * blocks * W, transcendentals=0),
        name="convolve",
    )(*got, *tables)


def unpack_kernel(own, got_ref, *rest):
    gate_refs, (out_ref, flat, gate_s) = rest[:-3], rest[-3:]
    sources, rows, _ = got_ref.shape
    some = rows // own
    place = lax.axis_index("ch")
    channels, width = gate_refs[0].shape
    ch_count = out_ref.shape[0] // channels
    for d in range(ch_count):
        here = pl.ds(pl.multiple_of(jnp.bitwise_xor(place, d) * channels, TILE), channels)
        gate_s[here, :] = gate_refs[d][...] if d < len(gate_refs) else jnp.ones((channels, width), jnp.bfloat16)
    for p in range(sources):
        part = got_ref[p].astype(jnp.float32)
        first = (p % ch_count * (sources // ch_count) + p // ch_count) * rows
        for h in range(W // LANES):
            flat[h, first : first + rows, :] = part[:, LANES * h : LANES * (h + 1)]
    for j in range(some):
        for h in range(W // LANES):
            part = flat[h, pl.ds(j, sources * own, stride=some), :]
            first = W * j + LANES * h
            cols = slice(first, first + LANES)
            out_ref[:, cols] = (part * gate_s[:, cols].astype(jnp.float32)).astype(jnp.bfloat16)


def unpack(got, gates, own, ch_count):
    sources, rows, _ = got.shape
    shape = (sources * own, rows // own * W)
    if rows % TILE:
        ones = [jnp.ones_like(gates[0])] * (ch_count - len(gates))
        order = jnp.bitwise_xor(lax.axis_index("ch"), jnp.arange(ch_count))
        gate = jnp.stack(gates + ones)[order].reshape(shape)
        got = got.reshape(-1, ch_count, rows, W).swapaxes(0, 1)
        return (got.reshape(shape).astype(jnp.float32) * gate.astype(jnp.float32)).astype(jnp.bfloat16)
    return pl.pallas_call(
        functools.partial(unpack_kernel, own),
        out_shape=jax.ShapeDtypeStruct(shape, jnp.bfloat16),
        in_specs=[whole_vmem()] * (1 + len(gates)),
        out_specs=whole_vmem(),
        scratch_shapes=[
            pltpu.VMEM((W // LANES, sources * rows, LANES), jnp.float32),
            pltpu.VMEM(shape, jnp.bfloat16),
        ],
        compiler_params=pltpu.CompilerParams(vmem_limit_bytes=24 * 2**20),
        name="unpack",
    )(got, *[pltpu.with_memory_space_constraint(gate, pltpu.VMEM) for gate in gates])


def body(pre_gate, value, post_gate, filter_taps, skip):
    ctx_count = lax.axis_size("ctx")
    ch_count = lax.axis_size("ch")
    own = value.shape[0] // ctx_count
    near = value.shape[1] // W
    got, gates = pack(pre_gate, value, post_gate, filter_taps, ctx_count, ch_count)
    tables, skip, _ = lax.optimization_barrier((dft_tables(near * ctx_count), skip, got[0]))
    got = [swap(got[d], "ctx", ctx_count, d) if d else got[d] for d in partner_order(ctx_count)]
    for d in range(1, ch_count // 2):
        gates[d] = swap(gates[d], "ch", ch_count, d)
    tables = list(make_tables(skip, *tables, own))
    mixed = convolve(got, tables, own, near, ch_count)
    mixed, gates = lax.optimization_barrier((mixed, gates))
    mixed = lax.all_to_all(mixed, ("ctx", "ch"), split_axis=0, concat_axis=0, tiled=True)
    return unpack(mixed, gates, own, ch_count)


def solution(mesh):
    placed = (P("ch", "ctx"), P("ch", "ctx"), P("ch", "ctx"), P("ch", "ctx"), P("ch"))
    return jax.shard_map(
        body, mesh=mesh, in_specs=placed, out_specs=P(None, ("ctx", "ch")), check_vma=False
    )
```

```python
import functools

import jax
import jax.numpy as jnp
import numpy as np
from jax import lax
from jax.experimental import pallas as pl
from jax.experimental.pallas import tpu as pltpu
from jax.sharding import PartitionSpec as P

W = 256
LANES = 128
TILE = 16
CHUNK = 256


def whole_vmem():
    return pl.BlockSpec(memory_space=pltpu.VMEM)


def in_hbm():
    return pl.BlockSpec(memory_space=pltpu.HBM)


def dft_tables(blocks):
    length = blocks * W
    k = np.arange(blocks)[:, None]
    angle = 2 * np.pi * ((4 * k + 1) * np.arange(blocks)[None, :] % (4 * blocks)) / (4 * blocks)
    outer = np.concatenate([np.cos(angle), -np.sin(angle)], 0)
    turn = 2 * np.pi * ((4 * k + 1) * np.arange(W)[None, :]) / (4 * length)
    near = 2 * np.pi * (np.arange(W)[:, None] * np.arange(W)[None, :] % W) / W
    inner = np.concatenate([np.cos(near), np.sin(near)], 0)
    turns = np.concatenate([np.cos(turn), np.sin(turn)], 1)
    return [jnp.asarray(table, jnp.float32) for table in (outer, outer.T, inner, turns)]


def lay(natural, j, value):
    count = value.shape[0]
    for h in range(W // LANES):
        first = (j * (W // LANES) + h) * count
        natural[first : first + count, :] = value[:, LANES * h : LANES * (h + 1)]


def pick(natural, channel, count, blocks):
    halves = W // LANES
    rows = [natural[pl.ds(h * count + channel, blocks, stride=halves * count), :] for h in range(halves)]
    return jnp.concatenate(rows, 1)


def pack_kernel(own, blocks, group, ch_count, parts, pre_ref, val_ref, taps_ref, post_ref, *rest):
    out_refs, gate_refs = rest[:parts], rest[parts : parts + ch_count // 2]
    pre_s, val_s, taps_s, post_s, natural, natural_taps, natural_gate, stage, in_sems = rest[parts + ch_count // 2 :]
    channels = own * parts
    some = min(TILE, channels)
    rows = own * blocks
    main = rows + blocks
    loads = []
    for g in range(channels // some):
        here = pl.ds(g * some, some)
        loads.append(pltpu.make_async_copy(pre_ref.at[here], pre_s.at[here], in_sems.at[g, 0]))
        loads.append(pltpu.make_async_copy(val_ref.at[here], val_s.at[here], in_sems.at[g, 1]))
    taps_load = pltpu.make_async_copy(taps_ref, taps_s, in_sems.at[channels // some, 0])
    gate_load = pltpu.make_async_copy(post_ref, post_s, in_sems.at[channels // some, 1])
    for copy in loads[:2] + [taps_load] + loads[2:] + [gate_load]:
        copy.start()
    groups = taps_s.shape[0]
    taps_load.wait()
    for j in range(blocks):
        lay(natural_taps, j, taps_s[:, W * j : W * (j + 1)])
    for g in range(channels // some):
        loads[2 * g].wait()
        loads[2 * g + 1].wait()
        here = slice(g * some, (g + 1) * some)
        for j in range(blocks):
            cols = slice(W * j, W * (j + 1))
            product = pre_s[here, cols].astype(jnp.float32) * val_s[here, cols].astype(jnp.float32)
            lay(natural.at[g], j, product)
        for i in range(g * some // own, (g + 1) * some // own):
            for c in range(own):
                mine = pick(natural.at[g], own * i + c - g * some, some, blocks)
                stage[i, blocks * c : blocks * (c + 1), :] = mine.astype(jnp.bfloat16)
            taps = pick(natural_taps, own * i // group, groups, blocks)
            stage[i, rows:main, :] = taps.astype(jnp.bfloat16)
    gate_load.wait()
    place = lax.axis_index("ch")
    piece = blocks // ch_count
    for d in range(ch_count):
        first = jnp.bitwise_xor(place, d) * (piece * W)
        if d < ch_count // 2:
            gate_refs[d][...] = post_s[:, pl.ds(pl.multiple_of(first, LANES), piece * W)]
        else:
            for j in range(piece):
                cols = pl.ds(pl.multiple_of(first + W * j, LANES), W)
                lay(natural_gate, (d - ch_count // 2) * piece + j, post_s[:, cols].astype(jnp.float32))
    early = piece * (ch_count - ch_count // 2)
    for i in range(parts):
        gate = [pick(natural_gate, own * i + c, channels, early) for c in range(own)]
        stage[i, main:, :] = jnp.concatenate(gate, 0).astype(jnp.bfloat16)
    me = lax.axis_index("ctx")
    for d in range(parts):
        out_refs[d][...] = stage[jnp.bitwise_xor(me, d)]


def pack(pre_gate, value, post_gate, taps, parts, ch_count):
    channels, block = value.shape
    own = channels // parts
    group = channels // taps.shape[0]
    blocks = block // W
    piece = blocks // ch_count
    early = piece * (ch_count - ch_count // 2)
    local = (own + 1) * blocks + own * early
    halves = W // LANES
    some = min(TILE, channels)
    args = [pltpu.with_memory_space_constraint(arg, pltpu.HBM) for arg in (pre_gate, value, taps, post_gate)]
    out = pl.pallas_call(
        functools.partial(pack_kernel, own, blocks, group, ch_count, parts),
        out_shape=[jax.ShapeDtypeStruct((local, W), jnp.bfloat16)] * parts
        + [jax.ShapeDtypeStruct((channels, piece * W), jnp.bfloat16)] * (ch_count // 2),
        in_specs=[in_hbm()] * 4,
        out_specs=[whole_vmem()] * (parts + ch_count // 2),
        scratch_shapes=[
            pltpu.VMEM(pre_gate.shape, jnp.bfloat16),
            pltpu.VMEM(value.shape, jnp.bfloat16),
            pltpu.VMEM(taps.shape, jnp.float32),
            pltpu.VMEM(post_gate.shape, jnp.bfloat16),
            pltpu.VMEM((channels // some, blocks * halves * some, LANES), jnp.float32),
            pltpu.VMEM((blocks * halves * taps.shape[0], LANES), jnp.float32),
            pltpu.VMEM((early * halves * channels, LANES), jnp.float32),
            pltpu.VMEM((parts, local, W), jnp.bfloat16),
            pltpu.SemaphoreType.DMA((channels // some + 1, 2)),
        ],
        compiler_params=pltpu.CompilerParams(vmem_limit_bytes=16 * 2**20),
        name="pack",
    )(*args)
    return list(out[:parts]), list(out[parts:])


def partner_order(count):
    corners = [d for d in range(1, count) if bin(d >> 1).count("1") > 1]
    straight = [d for d in range(count - 1, 1, -1) if bin(d >> 1).count("1") == 1 and d % 2 == 0]
    order = [0]
    for n in range(max(len(corners), len(straight))):
        order += straight[n : n + 1] + corners[n : n + 1]
    order += [d for d in range(2, count) if d not in order]
    return order + [1]


def swap(piece, axis, count, d):
    return lax.ppermute(piece, axis, [(i, i ^ d) for i in range(count)])


def tables_kernel(own, skip_ref, *rest):
    outer_ref, back_ref, inner_ref, turns_ref, outer_out, back_out, ahead, rear, turns_out = rest[:9]
    outer_s, back_s, inner_s, sems = rest[9:]
    count, width = turns_ref.shape
    loads = [
        pltpu.make_async_copy(inner_ref, inner_s, sems.at[0]),
        pltpu.make_async_copy(outer_ref, outer_s, sems.at[1]),
        pltpu.make_async_copy(back_ref, back_s, sems.at[2]),
        pltpu.make_async_copy(turns_ref, turns_out.at[0:count, :], sems.at[3]),
    ]
    for copy in loads:
        copy.start()
    me = lax.axis_index("ctx")
    for c in range(own):
        turns_out[count + 8 * c : count + 8 * (c + 1), :] = jnp.full((8, width), skip_ref[own * me + c], jnp.float32)
    loads[0].wait()
    near_cos, near_sin = inner_s[0:W, :].astype(jnp.bfloat16), inner_s[W:, :].astype(jnp.bfloat16)
    for table, sign in ((ahead, -1), (rear, 1)):
        table[0:W, 0:W] = near_cos
        table[0:W, W:] = near_sin * sign
        table[W:, 0:W] = near_sin * -sign
        table[W:, W:] = near_cos
    loads[1].wait()
    outer_out[...] = outer_s[...].astype(jnp.bfloat16)
    loads[2].wait()
    back_out[...] = back_s[...].astype(jnp.bfloat16)
    loads[3].wait()


def make_tables(skip, outer, back, inner, turns, own):
    count, width = turns.shape
    args = [pltpu.with_memory_space_constraint(arg, pltpu.HBM) for arg in (outer, back, inner, turns)]
    narrow = (outer.shape, back.shape, (2 * W, 2 * W), (2 * W, 2 * W))
    return pl.pallas_call(
        functools.partial(tables_kernel, own),
        out_shape=[jax.ShapeDtypeStruct(shape, jnp.bfloat16) for shape in narrow]
        + [jax.ShapeDtypeStruct((count + 8 * own, width), jnp.float32)],
        in_specs=[pl.BlockSpec(memory_space=pltpu.SMEM)] + [in_hbm()] * 4,
        out_specs=[whole_vmem()] * 5,
        scratch_shapes=[
            pltpu.VMEM(outer.shape, jnp.float32),
            pltpu.VMEM(back.shape, jnp.float32),
            pltpu.VMEM(inner.shape, jnp.float32),
            pltpu.SemaphoreType.DMA((4,)),
        ],
        compiler_params=pltpu.CompilerParams(vmem_limit_bytes=16 * 2**20),
        name="make_tables",
    )(skip, *args)


def conv_kernel(own, near, ch_count, parts, *rest):
    got_refs = rest[:parts]
    outer_ref, back_ref, ahead, rear, turns_ref, out_ref, x_all, r_all, z_all = rest[parts:]
    blocks = parts * near
    length = blocks * W
    me = lax.axis_index("ctx")
    order = partner_order(parts)
    for d, got_ref in zip(order, got_refs):
        here = pl.ds(pl.multiple_of(jnp.bitwise_xor(me, d) * near, TILE), near)
        for c in range(own + 1):
            x_all[here, W * c : W * (c + 1)] = got_ref[c * near : (c + 1) * near, :]

    def dot(left, right):
        return jnp.dot(left, right, preferred_element_type=jnp.float32)

    for first in range(0, blocks, CHUNK):
        here = slice(first, first + CHUNK)
        there = slice(blocks + first, blocks + first + CHUNK)
        both = dot(jnp.concatenate([outer_ref[here, :], outer_ref[there, :]], 0), x_all[...])
        real, imag = both[0:CHUNK, :], both[CHUNK:, :]
        turn_cos, turn_sin = turns_ref[here, 0:W], turns_ref[here, W:]
        rows = []
        for c in range(own + 1):
            re, im = real[:, W * c : W * (c + 1)], imag[:, W * c : W * (c + 1)]
            pair = [re * turn_cos + im * turn_sin, im * turn_cos - re * turn_sin]
            rows.append(jnp.concatenate(pair, 1).astype(jnp.bfloat16))
        spectrum = dot(jnp.concatenate(rows, 0), ahead[...])
        filt_re = spectrum[CHUNK * own :, 0:W] * (1.0 / length)
        filt_im = spectrum[CHUNK * own :, W:] * (1.0 / length)
        rows = []
        for c in range(own):
            part = spectrum[CHUNK * c : CHUNK * (c + 1), :]
            re, im = part[:, 0:W], part[:, W:]
            pair = [re * filt_re - im * filt_im, re * filt_im + im * filt_re]
            rows.append(jnp.concatenate(pair, 1).astype(jnp.bfloat16))
        middle = dot(jnp.concatenate(rows, 0), rear[...])
        for c in range(own):
            part = middle[CHUNK * c : CHUNK * (c + 1), :]
            re, im = part[:, 0:W], part[:, W:]
            cols = slice(W * c, W * (c + 1))
            r_all[here, cols] = (re * turn_cos - im * turn_sin).astype(jnp.bfloat16)
            r_all[there, cols] = (re * turn_sin + im * turn_cos).astype(jnp.bfloat16)

    conv = dot(back_ref[...], r_all[...])
    for c in range(own):
        cols = slice(W * c, W * (c + 1))
        z_all[c] = conv[:, cols] + turns_ref[blocks + 8 * c : blocks + 8 * c + 1, 0:W] * x_all[:, cols].astype(jnp.float32)
    some = out_ref.shape[1] // own
    early = some * (ch_count - ch_count // 2)
    place = lax.axis_index("ch")
    for d, got_ref in zip(order, got_refs):
        k = jnp.bitwise_xor(me, d)
        gate = got_ref[(own + 1) * near :, :].astype(jnp.float32)
        mine = [z_all[c, pl.ds(pl.multiple_of(k * near, TILE), near), :] for c in range(own)]
        for m in range(ch_count):
            rows = [part[m * some : (m + 1) * some, :] for part in mine]
            for e in range(ch_count // 2, ch_count):
                at = (e - ch_count // 2) * some
                for c in range(own):
                    factor = jnp.where(jnp.bitwise_xor(place, e) == m, gate[c * early + at : c * early + at + some, :], 1.0)
                    rows[c] = rows[c] * factor
            out_ref[k * ch_count + m] = jnp.concatenate(rows, 0).astype(jnp.bfloat16)


def convolve(got, tables, own, near, ch_count):
    parts = len(got)
    blocks = parts * near
    owners = parts * ch_count
    return pl.pallas_call(
        functools.partial(conv_kernel, own, near, ch_count, parts),
        out_shape=jax.ShapeDtypeStruct((owners, own * blocks // owners, W), jnp.bfloat16),
        in_specs=[whole_vmem()] * (parts + len(tables)),
        out_specs=whole_vmem(),
        scratch_shapes=[
            pltpu.VMEM((blocks, W * (own + 1)), jnp.bfloat16),
            pltpu.VMEM((2 * blocks, W * own), jnp.bfloat16),
            pltpu.VMEM((own, blocks, W), jnp.float32),
        ],
        compiler_params=pltpu.CompilerParams(vmem_limit_bytes=32 * 2**20),
        cost_estimate=pl.CostEstimate(flops=blocks * W, bytes_accessed=4 * blocks * W, transcendentals=0),
        name="convolve",
    )(*got, *tables)


def unpack_kernel(own, got_ref, *rest):
    gate_refs, (out_ref, flat, gate_s, stage, sems) = rest[:-5], rest[-5:]
    sources, rows, _ = got_ref.shape
    some = rows // own
    place = lax.axis_index("ch")
    channels, width = gate_refs[0].shape
    ch_count = out_ref.shape[0] // channels
    for d in range(ch_count):
        here = pl.ds(pl.multiple_of(jnp.bitwise_xor(place, d) * channels, TILE), channels)
        gate_s[here, :] = gate_refs[d][...] if d < len(gate_refs) else jnp.ones((channels, width), jnp.bfloat16)
    copies = []
    for m in range(ch_count):
        here = slice(m * channels, (m + 1) * channels)
        for k in range(sources // ch_count):
            part = got_ref[k * ch_count + m].astype(jnp.float32)
            first = m * channels * some + k * rows
            for h in range(W // LANES):
                flat[h, first : first + rows, :] = part[:, LANES * h : LANES * (h + 1)]
        for j in range(some):
            for h in range(W // LANES):
                part = flat[h, pl.ds(m * channels * some + j, channels, stride=some), :]
                first = W * j + LANES * h
                cols = slice(first, first + LANES)
                stage[here, cols] = (part * gate_s[here, cols].astype(jnp.float32)).astype(jnp.bfloat16)
        copies.append(pltpu.make_async_copy(stage.at[here], out_ref.at[here], sems.at[m]))
        copies[m].start()
    for copy in copies:
        copy.wait()


def unpack(got, gates, own, ch_count):
    sources, rows, _ = got.shape
    shape = (sources * own, rows // own * W)
    if rows % TILE:
        ones = [jnp.ones_like(gates[0])] * (ch_count - len(gates))
        order = jnp.bitwise_xor(lax.axis_index("ch"), jnp.arange(ch_count))
        gate = jnp.stack(gates + ones)[order].reshape(shape)
        got = got.reshape(-1, ch_count, rows, W).swapaxes(0, 1)
        return (got.reshape(shape).astype(jnp.float32) * gate.astype(jnp.float32)).astype(jnp.bfloat16)
    return pl.pallas_call(
        functools.partial(unpack_kernel, own),
        out_shape=jax.ShapeDtypeStruct(shape, jnp.bfloat16),
        in_specs=[whole_vmem()] * (1 + len(gates)),
        out_specs=in_hbm(),
        scratch_shapes=[
            pltpu.VMEM((W // LANES, sources * rows, LANES), jnp.float32),
            pltpu.VMEM(shape, jnp.bfloat16),
            pltpu.VMEM(shape, jnp.bfloat16),
            pltpu.SemaphoreType.DMA((ch_count,)),
        ],
        compiler_params=pltpu.CompilerParams(vmem_limit_bytes=24 * 2**20),
        name="unpack",
    )(got, *[pltpu.with_memory_space_constraint(gate, pltpu.VMEM) for gate in gates])


def body(pre_gate, value, post_gate, filter_taps, skip):
    ctx_count = lax.axis_size("ctx")
    ch_count = lax.axis_size("ch")
    own = value.shape[0] // ctx_count
    near = value.shape[1] // W
    got, gates = pack(pre_gate, value, post_gate, filter_taps, ctx_count, ch_count)
    tables, skip, _ = lax.optimization_barrier((dft_tables(near * ctx_count), skip, got[0]))
    got = [swap(got[d], "ctx", ctx_count, d) if d else got[d] for d in partner_order(ctx_count)]
    for d in range(1, ch_count // 2):
        gates[d] = swap(gates[d], "ch", ch_count, d)
    tables = list(make_tables(skip, *tables, own))
    mixed = convolve(got, tables, own, near, ch_count)
    mixed, gates = lax.optimization_barrier((mixed, gates))
    mixed = lax.all_to_all(mixed, ("ctx", "ch"), split_axis=0, concat_axis=0, tiled=True)
    return unpack(mixed, gates, own, ch_count)


def solution(mesh):
    placed = (P("ch", "ctx"), P("ch", "ctx"), P("ch", "ctx"), P("ch", "ctx"), P("ch"))
    return jax.shard_map(
        body, mesh=mesh, in_specs=placed, out_specs=P(None, ("ctx", "ch")), check_vma=False
    )
```

```python
import functools
import math

import jax
import jax.numpy as jnp
import numpy as np
from jax import lax
from jax.experimental import pallas as pl
from jax.experimental.pallas import tpu as pltpu
from jax.sharding import PartitionSpec as P

W = 256
LANES = 128
TILE = 16
CHUNK = 256


def whole_vmem():
    return pl.BlockSpec(memory_space=pltpu.VMEM)


def in_hbm():
    return pl.BlockSpec(memory_space=pltpu.HBM)


def dft_tables(blocks):
    length = blocks * W
    k = np.arange(blocks)[:, None]
    angle = 2 * np.pi * ((4 * k + 1) * np.arange(blocks)[None, :] % (4 * blocks)) / (4 * blocks)
    outer = np.concatenate([np.cos(angle), -np.sin(angle)], 0)
    turn = 2 * np.pi * ((4 * k + 1) * np.arange(W)[None, :]) / (4 * length)
    near = 2 * np.pi * (np.arange(W)[:, None] * np.arange(W)[None, :] % W) / W
    inner = np.concatenate([np.cos(near), np.sin(near)], 0)
    turns = np.concatenate([np.cos(turn), np.sin(turn)], 1)
    return [jnp.asarray(table, jnp.float32) for table in (outer, outer.T, inner, turns)]


def lay(natural, j, value):
    count = value.shape[0]
    for h in range(W // LANES):
        first = (j * (W // LANES) + h) * count
        natural[first : first + count, :] = value[:, LANES * h : LANES * (h + 1)]


def pick(natural, channel, count, blocks):
    halves = W // LANES
    rows = [natural[pl.ds(h * count + channel, blocks, stride=halves * count), :] for h in range(halves)]
    return jnp.concatenate(rows, 1)


def pack_kernel(own, blocks, group, ch_count, parts, pre_ref, val_ref, taps_ref, post_ref, *rest):
    out_refs, gate_refs = rest[:parts], rest[parts : parts + ch_count // 2]
    pre_s, val_s, taps_s, post_s, natural, natural_taps, natural_gate, stage, in_sems = rest[parts + ch_count // 2 :]
    channels = own * parts
    some = min(TILE, channels)
    rows = own * blocks
    main = rows + blocks
    loads = []
    for g in range(channels // some):
        here = pl.ds(g * some, some)
        loads.append(pltpu.make_async_copy(pre_ref.at[here], pre_s.at[here], in_sems.at[g, 0]))
        loads.append(pltpu.make_async_copy(val_ref.at[here], val_s.at[here], in_sems.at[g, 1]))
    taps_load = pltpu.make_async_copy(taps_ref, taps_s, in_sems.at[channels // some, 0])
    gate_load = pltpu.make_async_copy(post_ref, post_s, in_sems.at[channels // some, 1])
    for copy in loads[:2] + [taps_load] + loads[2:] + [gate_load]:
        copy.start()
    groups = taps_s.shape[0]
    taps_load.wait()
    for j in range(blocks):
        lay(natural_taps, j, taps_s[:, W * j : W * (j + 1)])
    for g in range(channels // some):
        loads[2 * g].wait()
        loads[2 * g + 1].wait()
        here = slice(g * some, (g + 1) * some)
        for j in range(blocks):
            cols = slice(W * j, W * (j + 1))
            product = pre_s[here, cols].astype(jnp.float32) * val_s[here, cols].astype(jnp.float32)
            lay(natural.at[g], j, product)
        for i in range(g * some // own, (g + 1) * some // own):
            for c in range(own):
                mine = pick(natural.at[g], own * i + c - g * some, some, blocks)
                stage[i, blocks * c : blocks * (c + 1), :] = mine.astype(jnp.bfloat16)
            taps = pick(natural_taps, own * i // group, groups, blocks)
            stage[i, rows:main, :] = taps.astype(jnp.bfloat16)
    gate_load.wait()
    place = lax.axis_index("ch")
    piece = blocks // ch_count
    for d in range(ch_count):
        first = jnp.bitwise_xor(place, d) * (piece * W)
        if d < ch_count // 2:
            gate_refs[d][...] = post_s[:, pl.ds(pl.multiple_of(first, LANES), piece * W)]
        else:
            for j in range(piece):
                cols = pl.ds(pl.multiple_of(first + W * j, LANES), W)
                lay(natural_gate, (d - ch_count // 2) * piece + j, post_s[:, cols].astype(jnp.float32))
    early = piece * (ch_count - ch_count // 2)
    for i in range(parts):
        gate = [pick(natural_gate, own * i + c, channels, early) for c in range(own)]
        stage[i, main:, :] = jnp.concatenate(gate, 0).astype(jnp.bfloat16)
    me = lax.axis_index("ctx")
    for d in range(parts):
        out_refs[d][...] = stage[jnp.bitwise_xor(me, d)]


def pack(pre_gate, value, post_gate, taps, parts, ch_count):
    channels, block = value.shape
    own = channels // parts
    group = channels // taps.shape[0]
    blocks = block // W
    piece = blocks // ch_count
    early = piece * (ch_count - ch_count // 2)
    local = (own + 1) * blocks + own * early
    halves = W // LANES
    some = min(TILE, channels)
    args = [pltpu.with_memory_space_constraint(arg, pltpu.HBM) for arg in (pre_gate, value, taps, post_gate)]
    out = pl.pallas_call(
        functools.partial(pack_kernel, own, blocks, group, ch_count, parts),
        out_shape=[jax.ShapeDtypeStruct((local, W), jnp.bfloat16)] * parts
        + [jax.ShapeDtypeStruct((channels, piece * W), jnp.bfloat16)] * (ch_count // 2),
        in_specs=[in_hbm()] * 4,
        out_specs=[whole_vmem()] * (parts + ch_count // 2),
        scratch_shapes=[
            pltpu.VMEM(pre_gate.shape, jnp.bfloat16),
            pltpu.VMEM(value.shape, jnp.bfloat16),
            pltpu.VMEM(taps.shape, jnp.float32),
            pltpu.VMEM(post_gate.shape, jnp.bfloat16),
            pltpu.VMEM((channels // some, blocks * halves * some, LANES), jnp.float32),
            pltpu.VMEM((blocks * halves * taps.shape[0], LANES), jnp.float32),
            pltpu.VMEM((early * halves * channels, LANES), jnp.float32),
            pltpu.VMEM((parts, local, W), jnp.bfloat16),
            pltpu.SemaphoreType.DMA((channels // some + 1, 2)),
        ],
        compiler_params=pltpu.CompilerParams(vmem_limit_bytes=16 * 2**20),
        name="pack",
    )(*args)
    return list(out[:parts]), list(out[parts:])


def partner_order(count):
    corners = [d for d in range(1, count) if bin(d >> 1).count("1") > 1]
    straight = [d for d in range(2, count, 2) if d not in corners]
    order = [0] + corners[:1] + straight + corners[1:]
    return order + [d for d in range(2, count) if d not in order] + [1]


def swap(piece, axis, count, d):
    return lax.ppermute(piece, axis, [(i, i ^ d) for i in range(count)])


def tables_kernel(own, skip_ref, *rest):
    outer_ref, back_ref, inner_ref, turns_ref, outer_out, back_out, ahead, rear, turns_out = rest[:9]
    outer_s, back_s, inner_s, sems = rest[9:]
    count, width = turns_ref.shape
    loads = [
        pltpu.make_async_copy(inner_ref, inner_s, sems.at[0]),
        pltpu.make_async_copy(outer_ref, outer_s, sems.at[1]),
        pltpu.make_async_copy(back_ref, back_s, sems.at[2]),
        pltpu.make_async_copy(turns_ref, turns_out.at[0:count, :], sems.at[3]),
    ]
    for copy in loads:
        copy.start()
    me = lax.axis_index("ctx")
    for c in range(own):
        turns_out[count + 8 * c : count + 8 * (c + 1), :] = jnp.full((8, width), skip_ref[own * me + c], jnp.float32)
    loads[0].wait()
    near_cos, near_sin = inner_s[0:W, :].astype(jnp.bfloat16), inner_s[W:, :].astype(jnp.bfloat16)
    for table, sign in ((ahead, -1), (rear, 1)):
        table[0:W, 0:W] = near_cos
        table[0:W, W:] = near_sin * sign
        table[W:, 0:W] = near_sin * -sign
        table[W:, W:] = near_cos
    loads[1].wait()
    outer_out[...] = outer_s[...].astype(jnp.bfloat16)
    loads[2].wait()
    back_out[...] = back_s[...].astype(jnp.bfloat16)
    loads[3].wait()


def make_tables(skip, outer, back, inner, turns, own):
    count, width = turns.shape
    args = [pltpu.with_memory_space_constraint(arg, pltpu.HBM) for arg in (outer, back, inner, turns)]
    narrow = (outer.shape, back.shape, (2 * W, 2 * W), (2 * W, 2 * W))
    return pl.pallas_call(
        functools.partial(tables_kernel, own),
        out_shape=[jax.ShapeDtypeStruct(shape, jnp.bfloat16) for shape in narrow]
        + [jax.ShapeDtypeStruct((count + 8 * own, width), jnp.float32)],
        in_specs=[pl.BlockSpec(memory_space=pltpu.SMEM)] + [in_hbm()] * 4,
        out_specs=[whole_vmem()] * 5,
        scratch_shapes=[
            pltpu.VMEM(outer.shape, jnp.float32),
            pltpu.VMEM(back.shape, jnp.float32),
            pltpu.VMEM(inner.shape, jnp.float32),
            pltpu.SemaphoreType.DMA((4,)),
        ],
        compiler_params=pltpu.CompilerParams(vmem_limit_bytes=16 * 2**20),
        name="make_tables",
    )(skip, *args)


def conv_kernel(own, near, ch_count, parts, *rest):
    got_refs = rest[:parts]
    outer_ref, back_ref, ahead, rear, turns_ref, out_ref, x_all, r_all, z_all = rest[parts:]
    blocks = parts * near
    length = blocks * W
    chunk = math.gcd(blocks, CHUNK)
    me = lax.axis_index("ctx")
    order = partner_order(parts)
    for d, got_ref in zip(order, got_refs):
        here = pl.ds(pl.multiple_of(jnp.bitwise_xor(me, d) * near, TILE), near)
        for c in range(own + 1):
            x_all[here, W * c : W * (c + 1)] = got_ref[c * near : (c + 1) * near, :]

    def dot(left, right):
        return jnp.dot(left, right, preferred_element_type=jnp.float32)

    for first in range(0, blocks, chunk):
        here = slice(first, first + chunk)
        there = slice(blocks + first, blocks + first + chunk)
        both = dot(jnp.concatenate([outer_ref[here, :], outer_ref[there, :]], 0), x_all[...])
        real, imag = both[0:chunk, :], both[chunk:, :]
        turn_cos, turn_sin = turns_ref[here, 0:W], turns_ref[here, W:]
        rows = []
        for c in range(own + 1):
            re, im = real[:, W * c : W * (c + 1)], imag[:, W * c : W * (c + 1)]
            pair = [re * turn_cos + im * turn_sin, im * turn_cos - re * turn_sin]
            rows.append(jnp.concatenate(pair, 1).astype(jnp.bfloat16))
        spectrum = dot(jnp.concatenate(rows, 0), ahead[...])
        filt_re = spectrum[chunk * own :, 0:W] * (1.0 / length)
        filt_im = spectrum[chunk * own :, W:] * (1.0 / length)
        rows = []
        for c in range(own):
            part = spectrum[chunk * c : chunk * (c + 1), :]
            re, im = part[:, 0:W], part[:, W:]
            pair = [re * filt_re - im * filt_im, re * filt_im + im * filt_re]
            rows.append(jnp.concatenate(pair, 1).astype(jnp.bfloat16))
        middle = dot(jnp.concatenate(rows, 0), rear[...])
        for c in range(own):
            part = middle[chunk * c : chunk * (c + 1), :]
            re, im = part[:, 0:W], part[:, W:]
            cols = slice(W * c, W * (c + 1))
            r_all[here, cols] = (re * turn_cos - im * turn_sin).astype(jnp.bfloat16)
            r_all[there, cols] = (re * turn_sin + im * turn_cos).astype(jnp.bfloat16)

    conv = dot(back_ref[...], r_all[...])
    for c in range(own):
        cols = slice(W * c, W * (c + 1))
        z_all[c] = conv[:, cols] + turns_ref[blocks + 8 * c : blocks + 8 * c + 1, 0:W] * x_all[:, cols].astype(jnp.float32)
    some = out_ref.shape[1] // own
    early = some * (ch_count - ch_count // 2)
    place = lax.axis_index("ch")
    for d, got_ref in zip(order, got_refs):
        k = jnp.bitwise_xor(me, d)
        gate = got_ref[(own + 1) * near :, :].astype(jnp.float32)
        mine = [z_all[c, pl.ds(pl.multiple_of(k * near, TILE), near), :] for c in range(own)]
        for m in range(ch_count):
            rows = [part[m * some : (m + 1) * some, :] for part in mine]
            for e in range(ch_count // 2, ch_count):
                at = (e - ch_count // 2) * some
                for c in range(own):
                    factor = jnp.where(jnp.bitwise_xor(place, e) == m, gate[c * early + at : c * early + at + some, :], 1.0)
                    rows[c] = rows[c] * factor
            out_ref[k * ch_count + m] = jnp.concatenate(rows, 0).astype(jnp.bfloat16)


def convolve(got, tables, own, near, ch_count):
    parts = len(got)
    blocks = parts * near
    owners = parts * ch_count
    return pl.pallas_call(
        functools.partial(conv_kernel, own, near, ch_count, parts),
        out_shape=jax.ShapeDtypeStruct((owners, own * blocks // owners, W), jnp.bfloat16),
        in_specs=[whole_vmem()] * (parts + len(tables)),
        out_specs=whole_vmem(),
        scratch_shapes=[
            pltpu.VMEM((blocks, W * (own + 1)), jnp.bfloat16),
            pltpu.VMEM((2 * blocks, W * own), jnp.bfloat16),
            pltpu.VMEM((own, blocks, W), jnp.float32),
        ],
        compiler_params=pltpu.CompilerParams(vmem_limit_bytes=32 * 2**20),
        cost_estimate=pl.CostEstimate(flops=blocks * W, bytes_accessed=4 * blocks * W, transcendentals=0),
        name="convolve",
    )(*got, *tables)


def unpack_kernel(own, got_ref, *rest):
    gate_refs, (out_ref, flat, gate_s, stage, sems) = rest[:-5], rest[-5:]
    sources, rows, _ = got_ref.shape
    some = rows // own
    place = lax.axis_index("ch")
    channels, width = gate_refs[0].shape
    ch_count = out_ref.shape[0] // channels
    for d in range(ch_count):
        here = pl.ds(pl.multiple_of(jnp.bitwise_xor(place, d) * channels, TILE), channels)
        gate_s[here, :] = gate_refs[d][...] if d < len(gate_refs) else jnp.ones((channels, width), jnp.bfloat16)
    copies = []
    for m in range(ch_count):
        here = slice(m * channels, (m + 1) * channels)
        for k in range(sources // ch_count):
            part = got_ref[k * ch_count + m].astype(jnp.float32)
            first = m * channels * some + k * rows
            for h in range(W // LANES):
                flat[h, first : first + rows, :] = part[:, LANES * h : LANES * (h + 1)]
        for j in range(some):
            for h in range(W // LANES):
                part = flat[h, pl.ds(m * channels * some + j, channels, stride=some), :]
                first = W * j + LANES * h
                cols = slice(first, first + LANES)
                stage[here, cols] = (part * gate_s[here, cols].astype(jnp.float32)).astype(jnp.bfloat16)
        copies.append(pltpu.make_async_copy(stage.at[here], out_ref.at[here], sems.at[m]))
        copies[m].start()
    for copy in copies:
        copy.wait()


def unpack(got, gates, own, ch_count):
    sources, rows, _ = got.shape
    shape = (sources * own, rows // own * W)
    if rows % TILE:
        ones = [jnp.ones_like(gates[0])] * (ch_count - len(gates))
        order = jnp.bitwise_xor(lax.axis_index("ch"), jnp.arange(ch_count))
        gate = jnp.stack(gates + ones)[order].reshape(shape)
        got = got.reshape(-1, ch_count, rows, W).swapaxes(0, 1)
        return (got.reshape(shape).astype(jnp.float32) * gate.astype(jnp.float32)).astype(jnp.bfloat16)
    return pl.pallas_call(
        functools.partial(unpack_kernel, own),
        out_shape=jax.ShapeDtypeStruct(shape, jnp.bfloat16),
        in_specs=[whole_vmem()] * (1 + len(gates)),
        out_specs=in_hbm(),
        scratch_shapes=[
            pltpu.VMEM((W // LANES, sources * rows, LANES), jnp.float32),
            pltpu.VMEM(shape, jnp.bfloat16),
            pltpu.VMEM(shape, jnp.bfloat16),
            pltpu.SemaphoreType.DMA((ch_count,)),
        ],
        compiler_params=pltpu.CompilerParams(vmem_limit_bytes=24 * 2**20),
        name="unpack",
    )(got, *[pltpu.with_memory_space_constraint(gate, pltpu.VMEM) for gate in gates])


def body(pre_gate, value, post_gate, filter_taps, skip):
    ctx_count = lax.axis_size("ctx")
    ch_count = lax.axis_size("ch")
    own = value.shape[0] // ctx_count
    near = value.shape[1] // W
    got, gates = pack(pre_gate, value, post_gate, filter_taps, ctx_count, ch_count)
    tables, skip, _ = lax.optimization_barrier((dft_tables(near * ctx_count), skip, got[0]))
    got = [swap(got[d], "ctx", ctx_count, d) if d else got[d] for d in partner_order(ctx_count)]
    for d in range(1, ch_count // 2):
        gates[d] = swap(gates[d], "ch", ch_count, d)
    tables = list(make_tables(skip, *tables, own))
    mixed = convolve(got, tables, own, near, ch_count)
    mixed, gates = lax.optimization_barrier((mixed, gates))
    mixed = lax.all_to_all(mixed, ("ctx", "ch"), split_axis=0, concat_axis=0, tiled=True)
    return unpack(mixed, gates, own, ch_count)


def solution(mesh):
    placed = (P("ch", "ctx"), P("ch", "ctx"), P("ch", "ctx"), P("ch", "ctx"), P("ch"))
    return jax.shard_map(
        body, mesh=mesh, in_specs=placed, out_specs=P(None, ("ctx", "ch")), check_vma=False
    )
```

```python
import functools
import math

import jax
import jax.numpy as jnp
import numpy as np
from jax import lax
from jax.experimental import pallas as pl
from jax.experimental.pallas import tpu as pltpu
from jax.sharding import PartitionSpec as P

W = 256
LANES = 128
TILE = 16
CHUNK = 256


def whole_vmem():
    return pl.BlockSpec(memory_space=pltpu.VMEM)


def in_hbm():
    return pl.BlockSpec(memory_space=pltpu.HBM)


def dft_tables(blocks):
    length = blocks * W
    k = np.arange(blocks)[:, None]
    angle = 2 * np.pi * ((4 * k + 1) * np.arange(blocks)[None, :] % (4 * blocks)) / (4 * blocks)
    outer = np.concatenate([np.cos(angle), -np.sin(angle)], 0)
    turn = 2 * np.pi * ((4 * k + 1) * np.arange(W)[None, :]) / (4 * length)
    near = 2 * np.pi * (np.arange(W)[:, None] * np.arange(W)[None, :] % W) / W
    inner = np.concatenate([np.cos(near), np.sin(near)], 0)
    turns = np.concatenate([np.cos(turn), np.sin(turn)], 1)
    return [jnp.asarray(table, jnp.float32) for table in (outer, outer.T, inner, turns)]


def lay(natural, j, value):
    count = value.shape[0]
    for h in range(W // LANES):
        first = (j * (W // LANES) + h) * count
        natural[first : first + count, :] = value[:, LANES * h : LANES * (h + 1)]


def pick(natural, channel, count, blocks):
    halves = W // LANES
    rows = [natural[pl.ds(h * count + channel, blocks, stride=halves * count), :] for h in range(halves)]
    return jnp.concatenate(rows, 1)


def pack_kernel(own, blocks, group, ch_count, parts, pre_ref, val_ref, taps_ref, post_ref, *rest):
    out_refs, gate_refs = rest[:parts], rest[parts : parts + ch_count // 2]
    pre_s, val_s, taps_s, post_s, natural, natural_taps, natural_gate, stage, in_sems = rest[parts + ch_count // 2 :]
    channels = own * parts
    some = min(TILE, channels)
    rows = own * blocks
    main = rows + blocks
    loads = []
    for g in range(channels // some):
        here = pl.ds(g * some, some)
        loads.append(pltpu.make_async_copy(pre_ref.at[here], pre_s.at[here], in_sems.at[g, 0]))
        loads.append(pltpu.make_async_copy(val_ref.at[here], val_s.at[here], in_sems.at[g, 1]))
    taps_load = pltpu.make_async_copy(taps_ref, taps_s, in_sems.at[channels // some, 0])
    gate_load = pltpu.make_async_copy(post_ref, post_s, in_sems.at[channels // some, 1])
    for copy in loads[:2] + [taps_load] + loads[2:] + [gate_load]:
        copy.start()
    groups = taps_s.shape[0]
    taps_load.wait()
    for j in range(blocks):
        lay(natural_taps, j, taps_s[:, W * j : W * (j + 1)])
    for g in range(channels // some):
        loads[2 * g].wait()
        loads[2 * g + 1].wait()
        here = slice(g * some, (g + 1) * some)
        for j in range(blocks):
            cols = slice(W * j, W * (j + 1))
            product = pre_s[here, cols].astype(jnp.float32) * val_s[here, cols].astype(jnp.float32)
            lay(natural.at[g], j, product)
        for i in range(g * some // own, (g + 1) * some // own):
            for c in range(own):
                mine = pick(natural.at[g], own * i + c - g * some, some, blocks)
                stage[i, blocks * c : blocks * (c + 1), :] = mine.astype(jnp.bfloat16)
            taps = pick(natural_taps, own * i // group, groups, blocks)
            stage[i, rows:main, :] = taps.astype(jnp.bfloat16)
    gate_load.wait()
    place = lax.axis_index("ch")
    piece = blocks // ch_count
    for d in range(ch_count):
        first = jnp.bitwise_xor(place, d) * (piece * W)
        if d < ch_count // 2:
            gate_refs[d][...] = post_s[:, pl.ds(pl.multiple_of(first, LANES), piece * W)]
        else:
            for j in range(piece):
                cols = pl.ds(pl.multiple_of(first + W * j, LANES), W)
                lay(natural_gate, (d - ch_count // 2) * piece + j, post_s[:, cols].astype(jnp.float32))
    early = piece * (ch_count - ch_count // 2)
    for i in range(parts):
        gate = [pick(natural_gate, own * i + c, channels, early) for c in range(own)]
        stage[i, main:, :] = jnp.concatenate(gate, 0).astype(jnp.bfloat16)
    me = lax.axis_index("ctx")
    for d in range(parts):
        out_refs[d][...] = stage[jnp.bitwise_xor(me, d)]


def pack(pre_gate, value, post_gate, taps, parts, ch_count):
    channels, block = value.shape
    own = channels // parts
    group = channels // taps.shape[0]
    blocks = block // W
    piece = blocks // ch_count
    early = piece * (ch_count - ch_count // 2)
    local = (own + 1) * blocks + own * early
    halves = W // LANES
    some = min(TILE, channels)
    args = [pltpu.with_memory_space_constraint(arg, pltpu.HBM) for arg in (pre_gate, value, taps, post_gate)]
    out = pl.pallas_call(
        functools.partial(pack_kernel, own, blocks, group, ch_count, parts),
        out_shape=[jax.ShapeDtypeStruct((local, W), jnp.bfloat16)] * parts
        + [jax.ShapeDtypeStruct((channels, piece * W), jnp.bfloat16)] * (ch_count // 2),
        in_specs=[in_hbm()] * 4,
        out_specs=[whole_vmem()] * (parts + ch_count // 2),
        scratch_shapes=[
            pltpu.VMEM(pre_gate.shape, jnp.bfloat16),
            pltpu.VMEM(value.shape, jnp.bfloat16),
            pltpu.VMEM(taps.shape, jnp.float32),
            pltpu.VMEM(post_gate.shape, jnp.bfloat16),
            pltpu.VMEM((channels // some, blocks * halves * some, LANES), jnp.float32),
            pltpu.VMEM((blocks * halves * taps.shape[0], LANES), jnp.float32),
            pltpu.VMEM((early * halves * channels, LANES), jnp.float32),
            pltpu.VMEM((parts, local, W), jnp.bfloat16),
            pltpu.SemaphoreType.DMA((channels // some + 1, 2)),
        ],
        compiler_params=pltpu.CompilerParams(vmem_limit_bytes=16 * 2**20),
        name="pack",
    )(*args)
    return list(out[:parts]), list(out[parts:])


def partner_order(count):
    corners = [d for d in range(1, count) if bin(d >> 1).count("1") > 1]
    straight = [d for d in range(2, count, 2) if d not in corners]
    order = [0] + corners[:1] + straight + corners[1:]
    return order + [d for d in range(2, count) if d not in order] + [1]


def swap(piece, axis, count, d):
    return lax.ppermute(piece, axis, [(i, i ^ d) for i in range(count)])


def tables_kernel(own, skip_ref, *rest):
    outer_ref, back_ref, inner_ref, turns_ref, outer_out, back_out, ahead, rear, turns_out = rest[:9]
    outer_s, back_s, inner_s, sems = rest[9:]
    count, width = turns_ref.shape
    loads = [
        pltpu.make_async_copy(inner_ref, inner_s, sems.at[0]),
        pltpu.make_async_copy(outer_ref, outer_s, sems.at[1]),
        pltpu.make_async_copy(back_ref, back_s, sems.at[2]),
        pltpu.make_async_copy(turns_ref, turns_out.at[0:count, :], sems.at[3]),
    ]
    for copy in loads:
        copy.start()
    me = lax.axis_index("ctx")
    for c in range(own):
        turns_out[count + 8 * c : count + 8 * (c + 1), :] = jnp.full((8, width), skip_ref[own * me + c], jnp.float32)
    loads[0].wait()
    near_cos, near_sin = inner_s[0:W, :].astype(jnp.bfloat16), inner_s[W:, :].astype(jnp.bfloat16)
    for table, sign in ((ahead, -1), (rear, 1)):
        table[0:W, 0:W] = near_cos
        table[0:W, W:] = near_sin * sign
        table[W:, 0:W] = near_sin * -sign
        table[W:, W:] = near_cos
    loads[1].wait()
    outer_out[...] = outer_s[...].astype(jnp.bfloat16)
    loads[2].wait()
    back_out[...] = back_s[...].astype(jnp.bfloat16)
    loads[3].wait()


def make_tables(skip, outer, back, inner, turns, own):
    count, width = turns.shape
    args = [pltpu.with_memory_space_constraint(arg, pltpu.HBM) for arg in (outer, back, inner, turns)]
    narrow = (outer.shape, back.shape, (2 * W, 2 * W), (2 * W, 2 * W))
    return pl.pallas_call(
        functools.partial(tables_kernel, own),
        out_shape=[jax.ShapeDtypeStruct(shape, jnp.bfloat16) for shape in narrow]
        + [jax.ShapeDtypeStruct((count + 8 * own, width), jnp.float32)],
        in_specs=[pl.BlockSpec(memory_space=pltpu.SMEM)] + [in_hbm()] * 4,
        out_specs=[whole_vmem()] * 5,
        scratch_shapes=[
            pltpu.VMEM(outer.shape, jnp.float32),
            pltpu.VMEM(back.shape, jnp.float32),
            pltpu.VMEM(inner.shape, jnp.float32),
            pltpu.SemaphoreType.DMA((4,)),
        ],
        compiler_params=pltpu.CompilerParams(vmem_limit_bytes=16 * 2**20),
        name="make_tables",
    )(skip, *args)


def conv_kernel(own, near, ch_count, parts, *rest):
    got_refs = rest[:parts]
    outer_ref, back_ref, ahead, rear, turns_ref, out_ref, x_all, r_all, z_all = rest[parts:]
    blocks = parts * near
    length = blocks * W
    chunk = math.gcd(blocks, CHUNK)
    me = lax.axis_index("ctx")
    order = partner_order(parts)
    for d, got_ref in zip(order, got_refs):
        here = pl.ds(pl.multiple_of(jnp.bitwise_xor(me, d) * near, TILE), near)
        for c in range(own + 1):
            x_all[here, W * c : W * (c + 1)] = got_ref[c * near : (c + 1) * near, :]

    def dot(left, right):
        return jnp.dot(left, right, preferred_element_type=jnp.float32)

    for first in range(0, blocks, chunk):
        here = slice(first, first + chunk)
        there = slice(blocks + first, blocks + first + chunk)
        both = dot(jnp.concatenate([outer_ref[here, :], outer_ref[there, :]], 0), x_all[...])
        real, imag = both[0:chunk, :], both[chunk:, :]
        turn_cos, turn_sin = turns_ref[here, 0:W], turns_ref[here, W:]
        rows = []
        for c in range(own + 1):
            re, im = real[:, W * c : W * (c + 1)], imag[:, W * c : W * (c + 1)]
            pair = [re * turn_cos + im * turn_sin, im * turn_cos - re * turn_sin]
            rows.append(jnp.concatenate(pair, 1).astype(jnp.bfloat16))
        spectrum = dot(jnp.concatenate(rows, 0), ahead[...])
        filt_re = spectrum[chunk * own :, 0:W] * (1.0 / length)
        filt_im = spectrum[chunk * own :, W:] * (1.0 / length)
        rows = []
        for c in range(own):
            part = spectrum[chunk * c : chunk * (c + 1), :]
            re, im = part[:, 0:W], part[:, W:]
            pair = [re * filt_re - im * filt_im, re * filt_im + im * filt_re]
            rows.append(jnp.concatenate(pair, 1).astype(jnp.bfloat16))
        middle = dot(jnp.concatenate(rows, 0), rear[...])
        for c in range(own):
            part = middle[chunk * c : chunk * (c + 1), :]
            re, im = part[:, 0:W], part[:, W:]
            cols = slice(W * c, W * (c + 1))
            r_all[here, cols] = (re * turn_cos - im * turn_sin).astype(jnp.bfloat16)
            r_all[there, cols] = (re * turn_sin + im * turn_cos).astype(jnp.bfloat16)

    conv = dot(back_ref[...], r_all[...])
    for c in range(own):
        cols = slice(W * c, W * (c + 1))
        z_all[c] = conv[:, cols] + turns_ref[blocks + 8 * c : blocks + 8 * c + 1, 0:W] * x_all[:, cols].astype(jnp.float32)
    some = out_ref.shape[1] // own
    early = some * (ch_count - ch_count // 2)
    place = lax.axis_index("ch")
    for d, got_ref in zip(order, got_refs):
        k = jnp.bitwise_xor(me, d)
        gate = got_ref[(own + 1) * near :, :].astype(jnp.float32)
        mine = [z_all[c, pl.ds(pl.multiple_of(k * near, TILE), near), :] for c in range(own)]
        for m in range(ch_count):
            rows = [part[m * some : (m + 1) * some, :] for part in mine]
            for e in range(ch_count // 2, ch_count):
                at = (e - ch_count // 2) * some
                for c in range(own):
                    factor = jnp.where(jnp.bitwise_xor(place, e) == m, gate[c * early + at : c * early + at + some, :], 1.0)
                    rows[c] = rows[c] * factor
            out_ref[k * ch_count + m] = jnp.concatenate(rows, 0).astype(jnp.bfloat16)


def convolve(got, tables, own, near, ch_count):
    parts = len(got)
    blocks = parts * near
    owners = parts * ch_count
    return pl.pallas_call(
        functools.partial(conv_kernel, own, near, ch_count, parts),
        out_shape=jax.ShapeDtypeStruct((owners, own * blocks // owners, W), jnp.bfloat16),
        in_specs=[whole_vmem()] * (parts + len(tables)),
        out_specs=whole_vmem(),
        scratch_shapes=[
            pltpu.VMEM((blocks, W * (own + 1)), jnp.bfloat16),
            pltpu.VMEM((2 * blocks, W * own), jnp.bfloat16),
            pltpu.VMEM((own, blocks, W), jnp.float32),
        ],
        compiler_params=pltpu.CompilerParams(vmem_limit_bytes=32 * 2**20),
        cost_estimate=pl.CostEstimate(flops=blocks * W, bytes_accessed=4 * blocks * W, transcendentals=0),
        name="convolve",
    )(*got, *tables)


def unpack_kernel(own, got_ref, *rest):
    gate_refs, (out_ref, flat, gate_s, stage, sems) = rest[:-5], rest[-5:]
    sources, rows, _ = got_ref.shape
    some = rows // own
    place = lax.axis_index("ch")
    channels, width = gate_refs[0].shape
    ch_count = out_ref.shape[0] // channels
    for d in range(ch_count):
        here = pl.ds(pl.multiple_of(jnp.bitwise_xor(place, d) * channels, TILE), channels)
        gate_s[here, :] = gate_refs[d][...] if d < len(gate_refs) else jnp.ones((channels, width), jnp.bfloat16)
    copies = []
    for m in range(ch_count):
        here = slice(m * channels, (m + 1) * channels)
        for k in range(sources // ch_count):
            part = got_ref[k * ch_count + m].astype(jnp.float32)
            first = m * channels * some + k * rows
            for h in range(W // LANES):
                flat[h, first : first + rows, :] = part[:, LANES * h : LANES * (h + 1)]
        for j in range(some):
            for h in range(W // LANES):
                part = flat[h, pl.ds(m * channels * some + j, channels, stride=some), :]
                first = W * j + LANES * h
                cols = slice(first, first + LANES)
                stage[here, cols] = (part * gate_s[here, cols].astype(jnp.float32)).astype(jnp.bfloat16)
        copies.append(pltpu.make_async_copy(stage.at[here], out_ref.at[here], sems.at[m]))
        copies[m].start()
    for copy in copies:
        copy.wait()


def unpack(got, gates, own, ch_count):
    sources, rows, _ = got.shape
    shape = (sources * own, rows // own * W)
    if rows % TILE:
        ones = [jnp.ones_like(gates[0])] * (ch_count - len(gates))
        order = jnp.bitwise_xor(lax.axis_index("ch"), jnp.arange(ch_count))
        gate = jnp.stack(gates + ones)[order].reshape(shape)
        got = got.reshape(-1, ch_count, rows, W).swapaxes(0, 1)
        return (got.reshape(shape).astype(jnp.float32) * gate.astype(jnp.float32)).astype(jnp.bfloat16)
    return pl.pallas_call(
        functools.partial(unpack_kernel, own),
        out_shape=jax.ShapeDtypeStruct(shape, jnp.bfloat16),
        in_specs=[whole_vmem()] * (1 + len(gates)),
        out_specs=in_hbm(),
        scratch_shapes=[
            pltpu.VMEM((W // LANES, sources * rows, LANES), jnp.float32),
            pltpu.VMEM(shape, jnp.bfloat16),
            pltpu.VMEM(shape, jnp.bfloat16),
            pltpu.SemaphoreType.DMA((ch_count,)),
        ],
        compiler_params=pltpu.CompilerParams(vmem_limit_bytes=24 * 2**20),
        name="unpack",
    )(got, *[pltpu.with_memory_space_constraint(gate, pltpu.VMEM) for gate in gates])


def body(pre_gate, value, post_gate, filter_taps, skip):
    ctx_count = lax.axis_size("ctx")
    ch_count = lax.axis_size("ch")
    own = value.shape[0] // ctx_count
    near = value.shape[1] // W
    got, gates = pack(pre_gate, value, post_gate, filter_taps, ctx_count, ch_count)
    order = partner_order(ctx_count)
    got = [got[d] for d in order]
    tables, skip, _ = lax.optimization_barrier((dft_tables(near * ctx_count), skip, got[0]))
    tables = list(make_tables(skip, *tables, own))
    half = ctx_count // 2 + 1
    tables, got[half:] = lax.optimization_barrier((tables, got[half:]))
    got = [swap(piece, "ctx", ctx_count, d) if d else piece for piece, d in zip(got, order)]
    for d in range(1, ch_count // 2):
        gates[d] = swap(gates[d], "ch", ch_count, d)
    mixed = convolve(got, tables, own, near, ch_count)
    mixed, gates = lax.optimization_barrier((mixed, gates))
    mixed = lax.all_to_all(mixed, ("ctx", "ch"), split_axis=0, concat_axis=0, tiled=True)
    return unpack(mixed, gates, own, ch_count)


def solution(mesh):
    placed = (P("ch", "ctx"), P("ch", "ctx"), P("ch", "ctx"), P("ch", "ctx"), P("ch"))
    return jax.shard_map(
        body, mesh=mesh, in_specs=placed, out_specs=P(None, ("ctx", "ch")), check_vma=False
    )
```

```python
import functools
import math

import jax
import jax.numpy as jnp
import numpy as np
from jax import lax
from jax.experimental import pallas as pl
from jax.experimental.pallas import tpu as pltpu
from jax.sharding import PartitionSpec as P

W = 256
LANES = 128
TILE = 16
CHUNK = 256


def whole_vmem():
    return pl.BlockSpec(memory_space=pltpu.VMEM)


def in_hbm():
    return pl.BlockSpec(memory_space=pltpu.HBM)


def dft_tables(blocks):
    length = blocks * W
    k = np.arange(blocks)[:, None]
    angle = 2 * np.pi * ((4 * k + 1) * np.arange(blocks)[None, :] % (4 * blocks)) / (4 * blocks)
    outer = np.concatenate([np.cos(angle), -np.sin(angle)], 0)
    turn = 2 * np.pi * ((4 * k + 1) * np.arange(W)[None, :]) / (4 * length)
    near = 2 * np.pi * (np.arange(W)[:, None] * np.arange(W)[None, :] % W) / W
    inner = np.concatenate([np.cos(near), np.sin(near)], 0)
    turns = np.concatenate([np.cos(turn), np.sin(turn)], 1)
    return [jnp.asarray(table, jnp.float32) for table in (outer, outer.T, inner, turns)]


def lay(natural, j, value):
    count = value.shape[0]
    for h in range(W // LANES):
        first = (j * (W // LANES) + h) * count
        natural[first : first + count, :] = value[:, LANES * h : LANES * (h + 1)]


def pick(natural, channel, count, blocks):
    halves = W // LANES
    rows = [natural[pl.ds(h * count + channel, blocks, stride=halves * count), :] for h in range(halves)]
    return jnp.concatenate(rows, 1)


def pack_kernel(own, blocks, group, ch_count, parts, pre_ref, val_ref, taps_ref, post_ref, *rest):
    even_refs, odd_ref, gate_refs = rest[: parts // 2], rest[parts // 2], rest[parts // 2 + 1 : parts // 2 + 1 + ch_count]
    pre_s, val_s, taps_s, natural, natural_taps, stage, in_sems, gate_sems = rest[parts // 2 + 1 + ch_count :]
    channels = own * parts
    some = min(TILE, channels)
    rows = own * blocks
    main = rows + blocks
    loads = []
    for g in range(channels // some):
        here = pl.ds(g * some, some)
        loads.append(pltpu.make_async_copy(pre_ref.at[here], pre_s.at[here], in_sems.at[g, 0]))
        loads.append(pltpu.make_async_copy(val_ref.at[here], val_s.at[here], in_sems.at[g, 1]))
    taps_load = pltpu.make_async_copy(taps_ref, taps_s, in_sems.at[channels // some, 0])
    place = lax.axis_index("ch")
    piece = blocks // ch_count * W
    gates = []
    for d in range(ch_count):
        cols = pl.ds(pl.multiple_of(jnp.bitwise_xor(place, d) * piece, LANES), piece)
        gates.append(pltpu.make_async_copy(post_ref.at[:, cols], gate_refs[d], gate_sems.at[d]))
    for copy in loads[:2] + [taps_load] + loads[2:] + gates[::-1]:
        copy.start()
    groups = taps_s.shape[0]
    taps_load.wait()
    for j in range(blocks):
        lay(natural_taps, j, taps_s[:, W * j : W * (j + 1)])
    for g in range(channels // some):
        loads[2 * g].wait()
        loads[2 * g + 1].wait()
        here = slice(g * some, (g + 1) * some)
        for j in range(blocks):
            cols = slice(W * j, W * (j + 1))
            product = pre_s[here, cols].astype(jnp.float32) * val_s[here, cols].astype(jnp.float32)
            lay(natural.at[g], j, product)
        for i in range(g * some // own, (g + 1) * some // own):
            for c in range(own):
                mine = pick(natural.at[g], own * i + c - g * some, some, blocks)
                stage[i, blocks * c : blocks * (c + 1), :] = mine.astype(jnp.bfloat16)
            taps = pick(natural_taps, own * i // group, groups, blocks)
            stage[i, rows:main, :] = taps.astype(jnp.bfloat16)
    me = lax.axis_index("ctx")
    for d in range(parts):
        if d % 2:
            odd_ref[d // 2] = stage[jnp.bitwise_xor(me, d)]
        else:
            even_refs[d // 2][...] = stage[jnp.bitwise_xor(me, d)]
    for copy in gates:
        copy.wait()


def pack(pre_gate, value, post_gate, taps, parts, ch_count):
    channels, block = value.shape
    own = channels // parts
    group = channels // taps.shape[0]
    blocks = block // W
    local = (own + 1) * blocks
    halves = W // LANES
    some = min(TILE, channels)
    args = [pltpu.with_memory_space_constraint(arg, pltpu.HBM) for arg in (pre_gate, value, taps, post_gate)]
    out = pl.pallas_call(
        functools.partial(pack_kernel, own, blocks, group, ch_count, parts),
        out_shape=[jax.ShapeDtypeStruct((local, W), jnp.bfloat16)] * (parts // 2)
        + [jax.ShapeDtypeStruct((parts // 2, local, W), jnp.bfloat16)]
        + [jax.ShapeDtypeStruct((channels, block // ch_count), jnp.bfloat16)] * ch_count,
        in_specs=[in_hbm()] * 4,
        out_specs=[whole_vmem()] * (parts // 2 + 1 + ch_count),
        scratch_shapes=[
            pltpu.VMEM(pre_gate.shape, jnp.bfloat16),
            pltpu.VMEM(value.shape, jnp.bfloat16),
            pltpu.VMEM(taps.shape, jnp.float32),
            pltpu.VMEM((channels // some, blocks * halves * some, LANES), jnp.float32),
            pltpu.VMEM((blocks * halves * taps.shape[0], LANES), jnp.float32),
            pltpu.VMEM((parts, local, W), jnp.bfloat16),
            pltpu.SemaphoreType.DMA((channels // some + 1, 2)),
            pltpu.SemaphoreType.DMA((ch_count,)),
        ],
        compiler_params=pltpu.CompilerParams(vmem_limit_bytes=16 * 2**20),
        name="pack",
    )(*args)
    return list(out[: parts // 2]), out[parts // 2], list(out[parts // 2 + 1 :])


def chip_order(chips):
    corners = [n for n in range(1, chips) if bin(n).count("1") > 1]
    return corners + [n for n in range(1, chips) if n not in corners]


def merge_kernel(order, other_ref, *refs):
    count = len(refs) // 2
    rows = other_ref.shape[1]
    for n in range(count):
        refs[count + n][0:rows, :] = refs[n][...]
        refs[count + n][rows:, :] = other_ref[order[n]]


def merge(even, other, order):
    local, width = even[0].shape
    count = len(even) - 1
    return pl.pallas_call(
        functools.partial(merge_kernel, order),
        out_shape=[jax.ShapeDtypeStruct((2 * local, width), jnp.bfloat16)] * count,
        in_specs=[whole_vmem()] * (1 + count),
        out_specs=[whole_vmem()] * count,
        compiler_params=pltpu.CompilerParams(vmem_limit_bytes=8 * 2**20),
        name="merge",
    )(other, *even[1:])


def swap(piece, axis, count, d):
    return lax.ppermute(piece, axis, [(i, i ^ d) for i in range(count)])


def tables_kernel(own, skip_ref, *rest):
    outer_ref, back_ref, inner_ref, turns_ref, outer_out, back_out, ahead, rear, turns_out = rest[:9]
    outer_s, back_s, inner_s, sems = rest[9:]
    count, width = turns_ref.shape
    loads = [
        pltpu.make_async_copy(inner_ref, inner_s, sems.at[0]),
        pltpu.make_async_copy(outer_ref, outer_s, sems.at[1]),
        pltpu.make_async_copy(back_ref, back_s, sems.at[2]),
        pltpu.make_async_copy(turns_ref, turns_out.at[0:count, :], sems.at[3]),
    ]
    for copy in loads:
        copy.start()
    me = lax.axis_index("ctx")
    for c in range(own):
        turns_out[count + 8 * c : count + 8 * (c + 1), :] = jnp.full((8, width), skip_ref[own * me + c], jnp.float32)
    loads[0].wait()
    near_cos, near_sin = inner_s[0:W, :].astype(jnp.bfloat16), inner_s[W:, :].astype(jnp.bfloat16)
    for table, sign in ((ahead, -1), (rear, 1)):
        table[0:W, 0:W] = near_cos
        table[0:W, W:] = near_sin * sign
        table[W:, 0:W] = near_sin * -sign
        table[W:, W:] = near_cos
    loads[1].wait()
    outer_out[...] = outer_s[...].astype(jnp.bfloat16)
    loads[2].wait()
    back_out[...] = back_s[...].astype(jnp.bfloat16)
    loads[3].wait()


def make_tables(skip, outer, back, inner, turns, own):
    count, width = turns.shape
    args = [pltpu.with_memory_space_constraint(arg, pltpu.HBM) for arg in (outer, back, inner, turns)]
    narrow = (outer.shape, back.shape, (2 * W, 2 * W), (2 * W, 2 * W))
    return pl.pallas_call(
        functools.partial(tables_kernel, own),
        out_shape=[jax.ShapeDtypeStruct(shape, jnp.bfloat16) for shape in narrow]
        + [jax.ShapeDtypeStruct((count + 8 * own, width), jnp.float32)],
        in_specs=[pl.BlockSpec(memory_space=pltpu.SMEM)] + [in_hbm()] * 4,
        out_specs=[whole_vmem()] * 5,
        scratch_shapes=[
            pltpu.VMEM(outer.shape, jnp.float32),
            pltpu.VMEM(back.shape, jnp.float32),
            pltpu.VMEM(inner.shape, jnp.float32),
            pltpu.SemaphoreType.DMA((4,)),
        ],
        compiler_params=pltpu.CompilerParams(vmem_limit_bytes=16 * 2**20),
        name="make_tables",
    )(skip, *args)


def conv_kernel(own, near, parts, mine_ref, other_ref, *rest):
    pair_refs = rest[: parts // 2 - 1]
    outer_ref, back_ref, ahead, rear, turns_ref, out_ref, x_all, r_all, z_all = rest[parts // 2 - 1 :]
    blocks = parts * near
    length = blocks * W
    chunk = math.gcd(blocks, CHUNK)
    local = mine_ref.shape[0]
    me = lax.axis_index("ctx")
    order = chip_order(parts // 2)
    for d in range(parts):
        here = pl.ds(pl.multiple_of(jnp.bitwise_xor(me, d) * near, TILE), near)
        for c in range(own + 1):
            first = c * near
            if d == 0:
                part = mine_ref[first : first + near, :]
            elif d == 1:
                part = other_ref[0, first : first + near, :]
            else:
                first += d % 2 * local
                part = pair_refs[order.index(d // 2)][first : first + near, :]
            x_all[here, W * c : W * (c + 1)] = part

    def dot(left, right):
        return jnp.dot(left, right, preferred_element_type=jnp.float32)

    for first in range(0, blocks, chunk):
        here = slice(first, first + chunk)
        there = slice(blocks + first, blocks + first + chunk)
        both = dot(jnp.concatenate([outer_ref[here, :], outer_ref[there, :]], 0), x_all[...])
        real, imag = both[0:chunk, :], both[chunk:, :]
        turn_cos, turn_sin = turns_ref[here, 0:W], turns_ref[here, W:]
        rows = []
        for c in range(own + 1):
            re, im = real[:, W * c : W * (c + 1)], imag[:, W * c : W * (c + 1)]
            pair = [re * turn_cos + im * turn_sin, im * turn_cos - re * turn_sin]
            rows.append(jnp.concatenate(pair, 1).astype(jnp.bfloat16))
        spectrum = dot(jnp.concatenate(rows, 0), ahead[...])
        filt_re = spectrum[chunk * own :, 0:W] * (1.0 / length)
        filt_im = spectrum[chunk * own :, W:] * (1.0 / length)
        rows = []
        for c in range(own):
            part = spectrum[chunk * c : chunk * (c + 1), :]
            re, im = part[:, 0:W], part[:, W:]
            pair = [re * filt_re - im * filt_im, re * filt_im + im * filt_re]
            rows.append(jnp.concatenate(pair, 1).astype(jnp.bfloat16))
        middle = dot(jnp.concatenate(rows, 0), rear[...])
        for c in range(own):
            part = middle[chunk * c : chunk * (c + 1), :]
            re, im = part[:, 0:W], part[:, W:]
            cols = slice(W * c, W * (c + 1))
            r_all[here, cols] = (re * turn_cos - im * turn_sin).astype(jnp.bfloat16)
            r_all[there, cols] = (re * turn_sin + im * turn_cos).astype(jnp.bfloat16)

    conv = dot(back_ref[...], r_all[...])
    for c in range(own):
        cols = slice(W * c, W * (c + 1))
        z_all[c] = conv[:, cols] + turns_ref[blocks + 8 * c : blocks + 8 * c + 1, 0:W] * x_all[:, cols].astype(jnp.float32)
    some = out_ref.shape[1] // own
    for n in range(out_ref.shape[0]):
        rows = [z_all[c, n * some : (n + 1) * some, :] for c in range(own)]
        out_ref[n] = jnp.concatenate(rows, 0).astype(jnp.bfloat16)


def convolve(mine, other, pairs, tables, own, near, ch_count):
    parts = 2 * len(pairs) + 2
    blocks = parts * near
    owners = parts * ch_count
    return pl.pallas_call(
        functools.partial(conv_kernel, own, near, parts),
        out_shape=jax.ShapeDtypeStruct((owners, own * blocks // owners, W), jnp.bfloat16),
        in_specs=[whole_vmem()] * (2 + len(pairs) + len(tables)),
        out_specs=whole_vmem(),
        scratch_shapes=[
            pltpu.VMEM((blocks, W * (own + 1)), jnp.bfloat16),
            pltpu.VMEM((2 * blocks, W * own), jnp.bfloat16),
            pltpu.VMEM((own, blocks, W), jnp.float32),
        ],
        compiler_params=pltpu.CompilerParams(vmem_limit_bytes=32 * 2**20),
        cost_estimate=pl.CostEstimate(flops=blocks * W, bytes_accessed=4 * blocks * W, transcendentals=0),
        name="convolve",
    )(mine, other, *pairs, *tables)


def unpack_kernel(own, got_ref, *rest):
    gate_refs, (out_ref, flat, gate_s, stage, sems) = rest[:-5], rest[-5:]
    sources, rows, _ = got_ref.shape
    some = rows // own
    place = lax.axis_index("ch")
    channels = gate_refs[0].shape[0]
    ch_count = out_ref.shape[0] // channels
    for d in range(ch_count):
        here = pl.ds(pl.multiple_of(jnp.bitwise_xor(place, d) * channels, TILE), channels)
        gate_s[here, :] = gate_refs[d][...]
    copies = []
    for m in range(ch_count):
        here = slice(m * channels, (m + 1) * channels)
        for k in range(sources // ch_count):
            part = got_ref[k * ch_count + m].astype(jnp.float32)
            first = m * channels * some + k * rows
            for h in range(W // LANES):
                flat[h, first : first + rows, :] = part[:, LANES * h : LANES * (h + 1)]
        for j in range(some):
            for h in range(W // LANES):
                part = flat[h, pl.ds(m * channels * some + j, channels, stride=some), :]
                first = W * j + LANES * h
                cols = slice(first, first + LANES)
                stage[here, cols] = (part * gate_s[here, cols].astype(jnp.float32)).astype(jnp.bfloat16)
        copies.append(pltpu.make_async_copy(stage.at[here], out_ref.at[here], sems.at[m]))
        copies[m].start()
    for copy in copies:
        copy.wait()


def unpack(got, gates, own, ch_count):
    sources, rows, _ = got.shape
    shape = (sources * own, rows // own * W)
    if rows % TILE:
        order = jnp.bitwise_xor(lax.axis_index("ch"), jnp.arange(ch_count))
        gate = jnp.stack(gates)[order].reshape(shape)
        got = got.reshape(-1, ch_count, rows, W).swapaxes(0, 1)
        return (got.reshape(shape).astype(jnp.float32) * gate.astype(jnp.float32)).astype(jnp.bfloat16)
    return pl.pallas_call(
        functools.partial(unpack_kernel, own),
        out_shape=jax.ShapeDtypeStruct(shape, jnp.bfloat16),
        in_specs=[whole_vmem()] * (1 + len(gates)),
        out_specs=in_hbm(),
        scratch_shapes=[
            pltpu.VMEM((W // LANES, sources * rows, LANES), jnp.float32),
            pltpu.VMEM(shape, jnp.bfloat16),
            pltpu.VMEM(shape, jnp.bfloat16),
            pltpu.SemaphoreType.DMA((ch_count,)),
        ],
        compiler_params=pltpu.CompilerParams(vmem_limit_bytes=24 * 2**20),
        name="unpack",
    )(got, *[pltpu.with_memory_space_constraint(gate, pltpu.VMEM) for gate in gates])


def body(pre_gate, value, post_gate, filter_taps, skip):
    ctx_count = lax.axis_size("ctx")
    ch_count = lax.axis_size("ch")
    own = value.shape[0] // ctx_count
    near = value.shape[1] // W
    even, odd, gates = pack(pre_gate, value, post_gate, filter_taps, ctx_count, ch_count)
    other = swap(odd, "ctx", ctx_count, 1)
    for d in reversed(range(1, ch_count)):
        gates[d] = swap(gates[d], "ch", ch_count, d)
    order = chip_order(ctx_count // 2)
    pairs = merge([even[n] for n in [0] + order], other, order)
    pairs = [swap(pair, "ctx", ctx_count, 2 * n) for n, pair in zip(order, pairs)]
    tables, skip, _ = lax.optimization_barrier((dft_tables(near * ctx_count), skip, odd))
    tables = list(make_tables(skip, *tables, own))
    gates[-1], pairs = lax.optimization_barrier((gates[-1], pairs))
    mixed = convolve(even[0], other, pairs, tables, own, near, ch_count)
    mixed, gates = lax.optimization_barrier((mixed, gates[::-1]))
    gates = gates[::-1]
    mixed = lax.all_to_all(mixed, ("ctx", "ch"), split_axis=0, concat_axis=0, tiled=True)
    return unpack(mixed, gates, own, ch_count)


def solution(mesh):
    placed = (P("ch", "ctx"), P("ch", "ctx"), P("ch", "ctx"), P("ch", "ctx"), P("ch"))
    return jax.shard_map(
        body, mesh=mesh, in_specs=placed, out_specs=P(None, ("ctx", "ch")), check_vma=False
    )
```

```python
import functools
import math

import jax
import jax.numpy as jnp
import numpy as np
from jax import lax
from jax.experimental import pallas as pl
from jax.experimental.pallas import tpu as pltpu
from jax.sharding import PartitionSpec as P

W = 256
LANES = 128
TILE = 16
CHUNK = 256


def whole_vmem():
    return pl.BlockSpec(memory_space=pltpu.VMEM)


def in_hbm():
    return pl.BlockSpec(memory_space=pltpu.HBM)


def dft_tables(blocks):
    length = blocks * W
    k = np.arange(blocks)[:, None]
    angle = 2 * np.pi * ((4 * k + 1) * np.arange(blocks)[None, :] % (4 * blocks)) / (4 * blocks)
    outer = np.concatenate([np.cos(angle), -np.sin(angle)], 0)
    turn = 2 * np.pi * ((4 * k + 1) * np.arange(W)[None, :]) / (4 * length)
    near = 2 * np.pi * (np.arange(W)[:, None] * np.arange(W)[None, :] % W) / W
    inner = np.concatenate([np.cos(near), np.sin(near)], 0)
    turns = np.concatenate([np.cos(turn), np.sin(turn)], 1)
    return [jnp.asarray(table, jnp.float32) for table in (outer, outer.T, inner, turns)]


def lay(natural, j, value):
    count = value.shape[0]
    for h in range(W // LANES):
        first = (j * (W // LANES) + h) * count
        natural[first : first + count, :] = value[:, LANES * h : LANES * (h + 1)]


def pick(natural, channel, count, blocks):
    halves = W // LANES
    rows = [natural[pl.ds(h * count + channel, blocks, stride=halves * count), :] for h in range(halves)]
    return jnp.concatenate(rows, 1)


def pack_kernel(own, blocks, group, ch_count, parts, pre_ref, val_ref, taps_ref, post_ref, *rest):
    out_refs, gate_refs = rest[:parts], rest[parts : parts + ch_count // 2]
    pre_s, val_s, taps_s, far_s, natural, natural_taps, natural_gate, stage, in_sems, gate_sems = rest[
        parts + ch_count // 2 :
    ]
    channels = own * parts
    some = min(TILE, channels)
    rows = own * blocks
    piece = blocks // ch_count
    early = piece * (ch_count // 2)
    main = rows + own * early
    place = lax.axis_index("ch")
    loads = []
    for g in range(channels // some):
        here = pl.ds(g * some, some)
        loads.append(pltpu.make_async_copy(pre_ref.at[here], pre_s.at[here], in_sems.at[g, 0]))
        loads.append(pltpu.make_async_copy(val_ref.at[here], val_s.at[here], in_sems.at[g, 1]))
    taps_load = pltpu.make_async_copy(taps_ref, taps_s, in_sems.at[channels // some, 0])
    other_half = (1 - place // (ch_count // 2)) * (early * W)
    cols = pl.ds(pl.multiple_of(other_half, LANES), early * W)
    far_load = pltpu.make_async_copy(post_ref.at[:, cols], far_s, in_sems.at[channels // some, 1])
    gates = []
    for d in range(ch_count // 2):
        cols = pl.ds(pl.multiple_of(jnp.bitwise_xor(place, d) * (piece * W), LANES), piece * W)
        gates.append(pltpu.make_async_copy(post_ref.at[:, cols], gate_refs[d], gate_sems.at[d]))
    for copy in loads[:2] + [taps_load, far_load] + loads[2:] + gates[::-1]:
        copy.start()
    groups = taps_s.shape[0]
    for g in range(channels // some):
        loads[2 * g].wait()
        loads[2 * g + 1].wait()
        here = slice(g * some, (g + 1) * some)
        for j in range(blocks):
            cols = slice(W * j, W * (j + 1))
            product = pre_s[here, cols].astype(jnp.float32) * val_s[here, cols].astype(jnp.float32)
            lay(natural.at[g], j, product)
        for i in range(g * some // own, (g + 1) * some // own):
            for c in range(own):
                mine = pick(natural.at[g], own * i + c - g * some, some, blocks)
                stage[i, blocks * c : blocks * (c + 1), :] = mine.astype(jnp.bfloat16)
        if g == 0:
            taps_load.wait()
            for j in range(blocks):
                lay(natural_taps, j, taps_s[:, W * j : W * (j + 1)])
            for i in range(parts):
                stage[i, main:, :] = pick(natural_taps, own * i // group, groups, blocks).astype(jnp.bfloat16)
            far_load.wait()
            for d in range(ch_count // 2, ch_count):
                first = jnp.bitwise_xor(place, d) % (ch_count // 2) * (piece * W)
                for j in range(piece):
                    cols = pl.ds(pl.multiple_of(first + W * j, LANES), W)
                    lay(natural_gate, (d - ch_count // 2) * piece + j, far_s[:, cols].astype(jnp.float32))
            for i in range(parts):
                gate = [pick(natural_gate, own * i + c, channels, early) for c in range(own)]
                stage[i, rows:main, :] = jnp.concatenate(gate, 0).astype(jnp.bfloat16)
    me = lax.axis_index("ctx")
    for d in range(parts):
        out_refs[d][...] = stage[jnp.bitwise_xor(me, d)]
    for copy in gates:
        copy.wait()


def pack(pre_gate, value, post_gate, taps, parts, ch_count):
    channels, block = value.shape
    own = channels // parts
    group = channels // taps.shape[0]
    blocks = block // W
    piece = blocks // ch_count
    early = piece * (ch_count // 2)
    local = own * (blocks + early) + blocks
    halves = W // LANES
    some = min(TILE, channels)
    args = [pltpu.with_memory_space_constraint(arg, pltpu.HBM) for arg in (pre_gate, value, taps, post_gate)]
    out = pl.pallas_call(
        functools.partial(pack_kernel, own, blocks, group, ch_count, parts),
        out_shape=[jax.ShapeDtypeStruct((local, W), jnp.bfloat16)] * parts
        + [jax.ShapeDtypeStruct((channels, piece * W), jnp.bfloat16)] * (ch_count // 2),
        in_specs=[in_hbm()] * 4,
        out_specs=[whole_vmem()] * (parts + ch_count // 2),
        scratch_shapes=[
            pltpu.VMEM(pre_gate.shape, jnp.bfloat16),
            pltpu.VMEM(value.shape, jnp.bfloat16),
            pltpu.VMEM(taps.shape, jnp.float32),
            pltpu.VMEM((channels, early * W), jnp.bfloat16),
            pltpu.VMEM((channels // some, blocks * halves * some, LANES), jnp.float32),
            pltpu.VMEM((blocks * halves * taps.shape[0], LANES), jnp.float32),
            pltpu.VMEM((early * halves * channels, LANES), jnp.float32),
            pltpu.VMEM((parts, local, W), jnp.bfloat16),
            pltpu.SemaphoreType.DMA((channels // some + 1, 2)),
            pltpu.SemaphoreType.DMA((ch_count // 2,)),
        ],
        compiler_params=pltpu.CompilerParams(vmem_limit_bytes=16 * 2**20),
        name="pack",
    )(*args)
    return list(out[:parts]), list(out[parts:])


def partner_order(count):
    corners = [d for d in range(1, count) if bin(d >> 1).count("1") > 1]
    straight = [d for d in range(2, count, 2) if d not in corners]
    order = [0] + corners[:1] + straight + corners[1:]
    return order + [d for d in range(2, count) if d not in order] + [1]


def swap(piece, axis, count, d):
    return lax.ppermute(piece, axis, [(i, i ^ d) for i in range(count)])


def tables_kernel(own, skip_ref, *rest):
    outer_ref, back_ref, inner_ref, turns_ref, outer_out, back_out, ahead, rear, turns_out = rest[:9]
    outer_s, back_s, inner_s, sems = rest[9:]
    count, width = turns_ref.shape
    loads = [
        pltpu.make_async_copy(inner_ref, inner_s, sems.at[0]),
        pltpu.make_async_copy(outer_ref, outer_s, sems.at[1]),
        pltpu.make_async_copy(back_ref, back_s, sems.at[2]),
        pltpu.make_async_copy(turns_ref, turns_out.at[0:count, :], sems.at[3]),
    ]
    for copy in loads:
        copy.start()
    me = lax.axis_index("ctx")
    for c in range(own):
        turns_out[count + 8 * c : count + 8 * (c + 1), :] = jnp.full((8, width), skip_ref[own * me + c], jnp.float32)
    loads[0].wait()
    near_cos, near_sin = inner_s[0:W, :].astype(jnp.bfloat16), inner_s[W:, :].astype(jnp.bfloat16)
    for table, sign in ((ahead, -1), (rear, 1)):
        table[0:W, 0:W] = near_cos
        table[0:W, W:] = near_sin * sign
        table[W:, 0:W] = near_sin * -sign
        table[W:, W:] = near_cos
    loads[1].wait()
    outer_out[...] = outer_s[...].astype(jnp.bfloat16)
    loads[2].wait()
    back_out[...] = back_s[...].astype(jnp.bfloat16)
    loads[3].wait()


def make_tables(skip, outer, back, inner, turns, own):
    count, width = turns.shape
    args = [pltpu.with_memory_space_constraint(arg, pltpu.HBM) for arg in (outer, back, inner, turns)]
    narrow = (outer.shape, back.shape, (2 * W, 2 * W), (2 * W, 2 * W))
    return pl.pallas_call(
        functools.partial(tables_kernel, own),
        out_shape=[jax.ShapeDtypeStruct(shape, jnp.bfloat16) for shape in narrow]
        + [jax.ShapeDtypeStruct((count + 8 * own, width), jnp.float32)],
        in_specs=[pl.BlockSpec(memory_space=pltpu.SMEM)] + [in_hbm()] * 4,
        out_specs=[whole_vmem()] * 5,
        scratch_shapes=[
            pltpu.VMEM(outer.shape, jnp.float32),
            pltpu.VMEM(back.shape, jnp.float32),
            pltpu.VMEM(inner.shape, jnp.float32),
            pltpu.SemaphoreType.DMA((4,)),
        ],
        compiler_params=pltpu.CompilerParams(vmem_limit_bytes=16 * 2**20),
        name="make_tables",
    )(skip, *args)


def conv_kernel(own, near, ch_count, parts, *rest):
    got_refs = rest[:parts]
    outer_ref, back_ref, ahead, rear, turns_ref, out_ref, x_all, r_all, z_all = rest[parts:]
    blocks = parts * near
    length = blocks * W
    chunk = math.gcd(blocks, CHUNK)
    me = lax.axis_index("ctx")
    order = partner_order(parts)
    some = out_ref.shape[1] // own
    early = some * (ch_count // 2)
    main = own * (near + early)
    for d, got_ref in zip(order, got_refs):
        here = pl.ds(pl.multiple_of(jnp.bitwise_xor(me, d) * near, TILE), near)
        for c in range(own):
            x_all[here, W * c : W * (c + 1)] = got_ref[c * near : (c + 1) * near, :]
        x_all[here, W * own :] = got_ref[main:, :]

    def dot(left, right):
        return jnp.dot(left, right, preferred_element_type=jnp.float32)

    for first in range(0, blocks, chunk):
        here = slice(first, first + chunk)
        there = slice(blocks + first, blocks + first + chunk)
        both = dot(jnp.concatenate([outer_ref[here, :], outer_ref[there, :]], 0), x_all[...])
        real, imag = both[0:chunk, :], both[chunk:, :]
        turn_cos, turn_sin = turns_ref[here, 0:W], turns_ref[here, W:]
        rows = []
        for c in range(own + 1):
            re, im = real[:, W * c : W * (c + 1)], imag[:, W * c : W * (c + 1)]
            pair = [re * turn_cos + im * turn_sin, im * turn_cos - re * turn_sin]
            rows.append(jnp.concatenate(pair, 1).astype(jnp.bfloat16))
        spectrum = dot(jnp.concatenate(rows, 0), ahead[...])
        filt_re = spectrum[chunk * own :, 0:W] * (1.0 / length)
        filt_im = spectrum[chunk * own :, W:] * (1.0 / length)
        rows = []
        for c in range(own):
            part = spectrum[chunk * c : chunk * (c + 1), :]
            re, im = part[:, 0:W], part[:, W:]
            pair = [re * filt_re - im * filt_im, re * filt_im + im * filt_re]
            rows.append(jnp.concatenate(pair, 1).astype(jnp.bfloat16))
        middle = dot(jnp.concatenate(rows, 0), rear[...])
        for c in range(own):
            part = middle[chunk * c : chunk * (c + 1), :]
            re, im = part[:, 0:W], part[:, W:]
            cols = slice(W * c, W * (c + 1))
            r_all[here, cols] = (re * turn_cos - im * turn_sin).astype(jnp.bfloat16)
            r_all[there, cols] = (re * turn_sin + im * turn_cos).astype(jnp.bfloat16)

    conv = dot(back_ref[...], r_all[...])
    for c in range(own):
        cols = slice(W * c, W * (c + 1))
        z_all[c] = conv[:, cols] + turns_ref[blocks + 8 * c : blocks + 8 * c + 1, 0:W] * x_all[:, cols].astype(jnp.float32)
    place = lax.axis_index("ch")
    for d, got_ref in zip(order, got_refs):
        k = jnp.bitwise_xor(me, d)
        gate = got_ref[own * near : main, :].astype(jnp.float32)
        mine = [z_all[c, pl.ds(pl.multiple_of(k * near, TILE), near), :] for c in range(own)]
        for m in range(ch_count):
            rows = [part[m * some : (m + 1) * some, :] for part in mine]
            for e in range(ch_count // 2, ch_count):
                at = (e - ch_count // 2) * some
                for c in range(own):
                    factor = jnp.where(jnp.bitwise_xor(place, e) == m, gate[c * early + at : c * early + at + some, :], 1.0)
                    rows[c] = rows[c] * factor
            out_ref[k * ch_count + m] = jnp.concatenate(rows, 0).astype(jnp.bfloat16)


def convolve(got, tables, own, near, ch_count):
    parts = len(got)
    blocks = parts * near
    owners = parts * ch_count
    return pl.pallas_call(
        functools.partial(conv_kernel, own, near, ch_count, parts),
        out_shape=jax.ShapeDtypeStruct((owners, own * blocks // owners, W), jnp.bfloat16),
        in_specs=[whole_vmem()] * (parts + len(tables)),
        out_specs=whole_vmem(),
        scratch_shapes=[
            pltpu.VMEM((blocks, W * (own + 1)), jnp.bfloat16),
            pltpu.VMEM((2 * blocks, W * own), jnp.bfloat16),
            pltpu.VMEM((own, blocks, W), jnp.float32),
        ],
        compiler_params=pltpu.CompilerParams(vmem_limit_bytes=32 * 2**20),
        cost_estimate=pl.CostEstimate(flops=blocks * W, bytes_accessed=4 * blocks * W, transcendentals=0),
        name="convolve",
    )(*got, *tables)


def unpack_kernel(own, got_ref, *rest):
    gate_refs, (out_ref, flat, gate_s, stage, sems) = rest[:-5], rest[-5:]
    sources, rows, _ = got_ref.shape
    some = rows // own
    place = lax.axis_index("ch")
    channels, width = gate_refs[0].shape
    ch_count = out_ref.shape[0] // channels
    for d in range(ch_count):
        here = pl.ds(pl.multiple_of(jnp.bitwise_xor(place, d) * channels, TILE), channels)
        gate_s[here, :] = gate_refs[d][...] if d < len(gate_refs) else jnp.ones((channels, width), jnp.bfloat16)
    copies = []
    for m in range(ch_count):
        here = slice(m * channels, (m + 1) * channels)
        for k in range(sources // ch_count):
            part = got_ref[k * ch_count + m].astype(jnp.float32)
            first = m * channels * some + k * rows
            for h in range(W // LANES):
                flat[h, first : first + rows, :] = part[:, LANES * h : LANES * (h + 1)]
        for j in range(some):
            for h in range(W // LANES):
                part = flat[h, pl.ds(m * channels * some + j, channels, stride=some), :]
                first = W * j + LANES * h
                cols = slice(first, first + LANES)
                stage[here, cols] = (part * gate_s[here, cols].astype(jnp.float32)).astype(jnp.bfloat16)
        copies.append(pltpu.make_async_copy(stage.at[here], out_ref.at[here], sems.at[m]))
        copies[m].start()
    for copy in copies:
        copy.wait()


def unpack(got, gates, own, ch_count):
    sources, rows, _ = got.shape
    shape = (sources * own, rows // own * W)
    if rows % TILE:
        ones = [jnp.ones_like(gates[0])] * (ch_count - len(gates))
        order = jnp.bitwise_xor(lax.axis_index("ch"), jnp.arange(ch_count))
        gate = jnp.stack(gates + ones)[order].reshape(shape)
        got = got.reshape(-1, ch_count, rows, W).swapaxes(0, 1)
        return (got.reshape(shape).astype(jnp.float32) * gate.astype(jnp.float32)).astype(jnp.bfloat16)
    return pl.pallas_call(
        functools.partial(unpack_kernel, own),
        out_shape=jax.ShapeDtypeStruct(shape, jnp.bfloat16),
        in_specs=[whole_vmem()] * (1 + len(gates)),
        out_specs=in_hbm(),
        scratch_shapes=[
            pltpu.VMEM((W // LANES, sources * rows, LANES), jnp.float32),
            pltpu.VMEM(shape, jnp.bfloat16),
            pltpu.VMEM(shape, jnp.bfloat16),
            pltpu.SemaphoreType.DMA((ch_count,)),
        ],
        compiler_params=pltpu.CompilerParams(vmem_limit_bytes=24 * 2**20),
        name="unpack",
    )(got, *[pltpu.with_memory_space_constraint(gate, pltpu.VMEM) for gate in gates])


def body(pre_gate, value, post_gate, filter_taps, skip):
    ctx_count = lax.axis_size("ctx")
    ch_count = lax.axis_size("ch")
    own = value.shape[0] // ctx_count
    near = value.shape[1] // W
    got, gates = pack(pre_gate, value, post_gate, filter_taps, ctx_count, ch_count)
    order = partner_order(ctx_count)
    got = [got[d] for d in order]
    tables, skip, _ = lax.optimization_barrier((dft_tables(near * ctx_count), skip, got[0]))
    tables = list(make_tables(skip, *tables, own))
    half = ctx_count // 2 + 1
    tables, got[half:] = lax.optimization_barrier((tables, got[half:]))
    got = [swap(piece, "ctx", ctx_count, d) if d else piece for piece, d in zip(got, order)]
    for d in range(1, ch_count // 2):
        gates[d] = swap(gates[d], "ch", ch_count, d)
    mixed = convolve(got, tables, own, near, ch_count)
    mixed, gates = lax.optimization_barrier((mixed, gates))
    mixed = lax.all_to_all(mixed, ("ctx", "ch"), split_axis=0, concat_axis=0, tiled=True)
    return unpack(mixed, gates, own, ch_count)


def solution(mesh):
    placed = (P("ch", "ctx"), P("ch", "ctx"), P("ch", "ctx"), P("ch", "ctx"), P("ch"))
    return jax.shard_map(
        body, mesh=mesh, in_specs=placed, out_specs=P(None, ("ctx", "ch")), check_vma=False
    )
```

```python
import functools
import math

import jax
import jax.numpy as jnp
import numpy as np
from jax import lax
from jax.experimental import pallas as pl
from jax.experimental.pallas import tpu as pltpu
from jax.sharding import PartitionSpec as P

W = 256
LANES = 128
TILE = 16
CHUNK = 256


def whole_vmem():
    return pl.BlockSpec(memory_space=pltpu.VMEM)


def in_hbm():
    return pl.BlockSpec(memory_space=pltpu.HBM)


def dft_tables(blocks):
    length = blocks * W
    k = np.arange(blocks)[:, None]
    angle = 2 * np.pi * ((4 * k + 1) * np.arange(blocks)[None, :] % (4 * blocks)) / (4 * blocks)
    outer = np.concatenate([np.cos(angle), -np.sin(angle)], 0)
    turn = 2 * np.pi * ((4 * k + 1) * np.arange(W)[None, :]) / (4 * length)
    near = 2 * np.pi * (np.arange(W)[:, None] * np.arange(W)[None, :] % W) / W
    inner = np.concatenate([np.cos(near), np.sin(near)], 0)
    turns = np.concatenate([np.cos(turn), np.sin(turn)], 1)
    return [jnp.asarray(table, jnp.float32) for table in (outer, outer.T, inner, turns)]


def lay(natural, j, value):
    count = value.shape[0]
    for h in range(W // LANES):
        first = (j * (W // LANES) + h) * count
        natural[first : first + count, :] = value[:, LANES * h : LANES * (h + 1)]


def pick(natural, channel, count, blocks):
    halves = W // LANES
    rows = [natural[pl.ds(h * count + channel, blocks, stride=halves * count), :] for h in range(halves)]
    return jnp.concatenate(rows, 1)


def pack_kernel(own, blocks, group, ch_count, parts, pre_ref, val_ref, taps_ref, post_ref, *rest):
    out_refs, gate_refs = rest[:parts], rest[parts : parts + ch_count // 2]
    pre_s, val_s, taps_s, post_s, natural, natural_taps, natural_gate, stage, in_sems = rest[parts + ch_count // 2 :]
    channels = own * parts
    some = min(TILE, channels)
    rows = own * blocks
    main = rows + blocks
    loads = []
    for g in range(channels // some):
        here = pl.ds(g * some, some)
        loads.append(pltpu.make_async_copy(pre_ref.at[here], pre_s.at[here], in_sems.at[g, 0]))
        loads.append(pltpu.make_async_copy(val_ref.at[here], val_s.at[here], in_sems.at[g, 1]))
    taps_load = pltpu.make_async_copy(taps_ref, taps_s, in_sems.at[channels // some, 0])
    gate_load = pltpu.make_async_copy(post_ref, post_s, in_sems.at[channels // some, 1])
    for copy in loads[:2] + [taps_load] + loads[2:] + [gate_load]:
        copy.start()
    groups = taps_s.shape[0]
    taps_load.wait()
    for j in range(blocks):
        lay(natural_taps, j, taps_s[:, W * j : W * (j + 1)])
    for g in range(channels // some):
        loads[2 * g].wait()
        loads[2 * g + 1].wait()
        here = slice(g * some, (g + 1) * some)
        for j in range(blocks):
            cols = slice(W * j, W * (j + 1))
            product = pre_s[here, cols].astype(jnp.float32) * val_s[here, cols].astype(jnp.float32)
            lay(natural.at[g], j, product)
        for i in range(g * some // own, (g + 1) * some // own):
            for c in range(own):
                mine = pick(natural.at[g], own * i + c - g * some, some, blocks)
                stage[i, blocks * c : blocks * (c + 1), :] = mine.astype(jnp.bfloat16)
            taps = pick(natural_taps, own * i // group, groups, blocks)
            stage[i, rows:main, :] = taps.astype(jnp.bfloat16)
    gate_load.wait()
    place = lax.axis_index("ch")
    piece = blocks // ch_count
    for d in range(ch_count):
        first = jnp.bitwise_xor(place, d) * (piece * W)
        if d < ch_count // 2:
            gate_refs[d][...] = post_s[:, pl.ds(pl.multiple_of(first, LANES), piece * W)]
        else:
            for j in range(piece):
                cols = pl.ds(pl.multiple_of(first + W * j, LANES), W)
                lay(natural_gate, (d - ch_count // 2) * piece + j, post_s[:, cols].astype(jnp.float32))
    early = piece * (ch_count - ch_count // 2)
    for i in range(parts):
        gate = [pick(natural_gate, own * i + c, channels, early) for c in range(own)]
        stage[i, main:, :] = jnp.concatenate(gate, 0).astype(jnp.bfloat16)
    me = lax.axis_index("ctx")
    for d in range(parts):
        out_refs[d][...] = stage[jnp.bitwise_xor(me, d)]


def pack(pre_gate, value, post_gate, taps, parts, ch_count):
    channels, block = value.shape
    own = channels // parts
    group = channels // taps.shape[0]
    blocks = block // W
    piece = blocks // ch_count
    early = piece * (ch_count - ch_count // 2)
    local = (own + 1) * blocks + own * early
    halves = W // LANES
    some = min(TILE, channels)
    args = [pltpu.with_memory_space_constraint(arg, pltpu.HBM) for arg in (pre_gate, value, taps, post_gate)]
    out = pl.pallas_call(
        functools.partial(pack_kernel, own, blocks, group, ch_count, parts),
        out_shape=[jax.ShapeDtypeStruct((local, W), jnp.bfloat16)] * parts
        + [jax.ShapeDtypeStruct((channels, piece * W), jnp.bfloat16)] * (ch_count // 2),
        in_specs=[in_hbm()] * 4,
        out_specs=[whole_vmem()] * (parts + ch_count // 2),
        scratch_shapes=[
            pltpu.VMEM(pre_gate.shape, jnp.bfloat16),
            pltpu.VMEM(value.shape, jnp.bfloat16),
            pltpu.VMEM(taps.shape, jnp.float32),
            pltpu.VMEM(post_gate.shape, jnp.bfloat16),
            pltpu.VMEM((channels // some, blocks * halves * some, LANES), jnp.float32),
            pltpu.VMEM((blocks * halves * taps.shape[0], LANES), jnp.float32),
            pltpu.VMEM((early * halves * channels, LANES), jnp.float32),
            pltpu.VMEM((parts, local, W), jnp.bfloat16),
            pltpu.SemaphoreType.DMA((channels // some + 1, 2)),
        ],
        compiler_params=pltpu.CompilerParams(vmem_limit_bytes=16 * 2**20),
        name="pack",
    )(*args)
    return list(out[:parts]), list(out[parts:])


def partner_order(count):
    corners = [d for d in range(1, count) if bin(d >> 1).count("1") > 1]
    straight = [d for d in range(2, count, 2) if d not in corners]
    order = [0] + corners[:1] + straight + corners[1:]
    return order + [d for d in range(2, count) if d not in order] + [1]


def swap(piece, axis, count, d):
    return lax.ppermute(piece, axis, [(i, i ^ d) for i in range(count)])


def tables_kernel(own, skip_ref, *rest):
    outer_ref, back_ref, inner_ref, turns_ref, outer_out, back_out, ahead, rear, turns_out = rest[:9]
    outer_s, back_s, inner_s, sems = rest[9:]
    count, width = turns_ref.shape
    loads = [
        pltpu.make_async_copy(inner_ref, inner_s, sems.at[0]),
        pltpu.make_async_copy(outer_ref, outer_s, sems.at[1]),
        pltpu.make_async_copy(back_ref, back_s, sems.at[2]),
        pltpu.make_async_copy(turns_ref, turns_out.at[0:count, :], sems.at[3]),
    ]
    for copy in loads:
        copy.start()
    me = lax.axis_index("ctx")
    for c in range(own):
        turns_out[count + 8 * c : count + 8 * (c + 1), :] = jnp.full((8, width), skip_ref[own * me + c], jnp.float32)
    loads[0].wait()
    near_cos, near_sin = inner_s[0:W, :].astype(jnp.bfloat16), inner_s[W:, :].astype(jnp.bfloat16)
    for table, sign in ((ahead, -1), (rear, 1)):
        table[0:W, 0:W] = near_cos
        table[0:W, W:] = near_sin * sign
        table[W:, 0:W] = near_sin * -sign
        table[W:, W:] = near_cos
    loads[1].wait()
    outer_out[...] = outer_s[...].astype(jnp.bfloat16)
    loads[2].wait()
    back_out[...] = back_s[...].astype(jnp.bfloat16)
    loads[3].wait()


def make_tables(skip, outer, back, inner, turns, own):
    count, width = turns.shape
    args = [pltpu.with_memory_space_constraint(arg, pltpu.HBM) for arg in (outer, back, inner, turns)]
    narrow = (outer.shape, back.shape, (2 * W, 2 * W), (2 * W, 2 * W))
    return pl.pallas_call(
        functools.partial(tables_kernel, own),
        out_shape=[jax.ShapeDtypeStruct(shape, jnp.bfloat16) for shape in narrow]
        + [jax.ShapeDtypeStruct((count + 8 * own, width), jnp.float32)],
        in_specs=[pl.BlockSpec(memory_space=pltpu.SMEM)] + [in_hbm()] * 4,
        out_specs=[whole_vmem()] * 5,
        scratch_shapes=[
            pltpu.VMEM(outer.shape, jnp.float32),
            pltpu.VMEM(back.shape, jnp.float32),
            pltpu.VMEM(inner.shape, jnp.float32),
            pltpu.SemaphoreType.DMA((4,)),
        ],
        compiler_params=pltpu.CompilerParams(vmem_limit_bytes=16 * 2**20),
        name="make_tables",
    )(skip, *args)


def conv_kernel(own, near, ch_count, parts, *rest):
    got_refs = rest[:parts]
    outer_ref, back_ref, ahead, rear, turns_ref, out_ref, x_all, r_all, z_all = rest[parts:]
    blocks = parts * near
    length = blocks * W
    chunk = math.gcd(blocks, CHUNK)
    me = lax.axis_index("ctx")
    order = partner_order(parts)
    for d, got_ref in zip(order, got_refs):
        here = pl.ds(pl.multiple_of(jnp.bitwise_xor(me, d) * near, TILE), near)
        for c in range(own + 1):
            x_all[here, W * c : W * (c + 1)] = got_ref[c * near : (c + 1) * near, :]

    def dot(left, right):
        return jnp.dot(left, right, preferred_element_type=jnp.float32)

    for first in range(0, blocks, chunk):
        here = slice(first, first + chunk)
        there = slice(blocks + first, blocks + first + chunk)
        both = dot(jnp.concatenate([outer_ref[here, :], outer_ref[there, :]], 0), x_all[...])
        real, imag = both[0:chunk, :], both[chunk:, :]
        turn_cos, turn_sin = turns_ref[here, 0:W], turns_ref[here, W:]
        rows = []
        for c in range(own + 1):
            re, im = real[:, W * c : W * (c + 1)], imag[:, W * c : W * (c + 1)]
            pair = [re * turn_cos + im * turn_sin, im * turn_cos - re * turn_sin]
            rows.append(jnp.concatenate(pair, 1).astype(jnp.bfloat16))
        spectrum = dot(jnp.concatenate(rows, 0), ahead[...])
        filt_re = spectrum[chunk * own :, 0:W] * (1.0 / length)
        filt_im = spectrum[chunk * own :, W:] * (1.0 / length)
        rows = []
        for c in range(own):
            part = spectrum[chunk * c : chunk * (c + 1), :]
            re, im = part[:, 0:W], part[:, W:]
            pair = [re * filt_re - im * filt_im, re * filt_im + im * filt_re]
            rows.append(jnp.concatenate(pair, 1).astype(jnp.bfloat16))
        middle = dot(jnp.concatenate(rows, 0), rear[...])
        for c in range(own):
            part = middle[chunk * c : chunk * (c + 1), :]
            re, im = part[:, 0:W], part[:, W:]
            cols = slice(W * c, W * (c + 1))
            r_all[here, cols] = (re * turn_cos - im * turn_sin).astype(jnp.bfloat16)
            r_all[there, cols] = (re * turn_sin + im * turn_cos).astype(jnp.bfloat16)

    conv = dot(back_ref[...], r_all[...])
    for c in range(own):
        cols = slice(W * c, W * (c + 1))
        z_all[c] = conv[:, cols] + turns_ref[blocks + 8 * c : blocks + 8 * c + 1, 0:W] * x_all[:, cols].astype(jnp.float32)
    some = out_ref.shape[1] // own
    early = some * (ch_count - ch_count // 2)
    place = lax.axis_index("ch")
    for d, got_ref in zip(order, got_refs):
        k = jnp.bitwise_xor(me, d)
        gate = got_ref[(own + 1) * near :, :].astype(jnp.float32)
        mine = [z_all[c, pl.ds(pl.multiple_of(k * near, TILE), near), :] for c in range(own)]
        for m in range(ch_count):
            rows = [part[m * some : (m + 1) * some, :] for part in mine]
            for e in range(ch_count // 2, ch_count):
                at = (e - ch_count // 2) * some
                for c in range(own):
                    factor = jnp.where(jnp.bitwise_xor(place, e) == m, gate[c * early + at : c * early + at + some, :], 1.0)
                    rows[c] = rows[c] * factor
            out_ref[parts * ch_count - 1 - (k * ch_count + m)] = jnp.concatenate(rows, 0).astype(jnp.bfloat16)


def convolve(got, tables, own, near, ch_count):
    parts = len(got)
    blocks = parts * near
    owners = parts * ch_count
    return pl.pallas_call(
        functools.partial(conv_kernel, own, near, ch_count, parts),
        out_shape=jax.ShapeDtypeStruct((owners, own * blocks // owners, W), jnp.bfloat16),
        in_specs=[whole_vmem()] * (parts + len(tables)),
        out_specs=whole_vmem(),
        scratch_shapes=[
            pltpu.VMEM((blocks, W * (own + 1)), jnp.bfloat16),
            pltpu.VMEM((2 * blocks, W * own), jnp.bfloat16),
            pltpu.VMEM((own, blocks, W), jnp.float32),
        ],
        compiler_params=pltpu.CompilerParams(vmem_limit_bytes=32 * 2**20),
        cost_estimate=pl.CostEstimate(flops=blocks * W, bytes_accessed=4 * blocks * W, transcendentals=0),
        name="convolve",
    )(*got, *tables)


def unpack_kernel(own, got_ref, *rest):
    gate_refs, (out_ref, flat, gate_s, stage, sems) = rest[:-5], rest[-5:]
    sources, rows, _ = got_ref.shape
    some = rows // own
    place = lax.axis_index("ch")
    channels, width = gate_refs[0].shape
    ch_count = out_ref.shape[0] // channels
    for d in range(ch_count):
        here = pl.ds(pl.multiple_of(jnp.bitwise_xor(place, d) * channels, TILE), channels)
        gate_s[here, :] = gate_refs[d][...] if d < len(gate_refs) else jnp.ones((channels, width), jnp.bfloat16)
    copies = []
    for m in range(ch_count):
        here = slice(m * channels, (m + 1) * channels)
        for k in range(sources // ch_count):
            part = got_ref[sources - 1 - (k * ch_count + m)].astype(jnp.float32)
            first = m * channels * some + k * rows
            for h in range(W // LANES):
                flat[h, first : first + rows, :] = part[:, LANES * h : LANES * (h + 1)]
        for j in range(some):
            for h in range(W // LANES):
                part = flat[h, pl.ds(m * channels * some + j, channels, stride=some), :]
                first = W * j + LANES * h
                cols = slice(first, first + LANES)
                stage[here, cols] = (part * gate_s[here, cols].astype(jnp.float32)).astype(jnp.bfloat16)
        copies.append(pltpu.make_async_copy(stage.at[here], out_ref.at[here], sems.at[m]))
        copies[m].start()
    for copy in copies:
        copy.wait()


def unpack(got, gates, own, ch_count):
    sources, rows, _ = got.shape
    shape = (sources * own, rows // own * W)
    if rows % TILE:
        ones = [jnp.ones_like(gates[0])] * (ch_count - len(gates))
        order = jnp.bitwise_xor(lax.axis_index("ch"), jnp.arange(ch_count))
        gate = jnp.stack(gates + ones)[order].reshape(shape)
        got = got[::-1].reshape(-1, ch_count, rows, W).swapaxes(0, 1)
        return (got.reshape(shape).astype(jnp.float32) * gate.astype(jnp.float32)).astype(jnp.bfloat16)
    return pl.pallas_call(
        functools.partial(unpack_kernel, own),
        out_shape=jax.ShapeDtypeStruct(shape, jnp.bfloat16),
        in_specs=[whole_vmem()] * (1 + len(gates)),
        out_specs=in_hbm(),
        scratch_shapes=[
            pltpu.VMEM((W // LANES, sources * rows, LANES), jnp.float32),
            pltpu.VMEM(shape, jnp.bfloat16),
            pltpu.VMEM(shape, jnp.bfloat16),
            pltpu.SemaphoreType.DMA((ch_count,)),
        ],
        compiler_params=pltpu.CompilerParams(vmem_limit_bytes=24 * 2**20),
        name="unpack",
    )(got, *[pltpu.with_memory_space_constraint(gate, pltpu.VMEM) for gate in gates])


def body(pre_gate, value, post_gate, filter_taps, skip):
    ctx_count = lax.axis_size("ctx")
    ch_count = lax.axis_size("ch")
    own = value.shape[0] // ctx_count
    near = value.shape[1] // W
    got, gates = pack(pre_gate, value, post_gate, filter_taps, ctx_count, ch_count)
    order = partner_order(ctx_count)
    got = [got[d] for d in order]
    tables, skip, _ = lax.optimization_barrier((dft_tables(near * ctx_count), skip, got[0]))
    tables = list(make_tables(skip, *tables, own))
    half = ctx_count // 2 + 1
    tables, got[half:] = lax.optimization_barrier((tables, got[half:]))
    got = [swap(piece, "ctx", ctx_count, d) if d else piece for piece, d in zip(got, order)]
    for d in range(1, ch_count // 2):
        gates[d] = swap(gates[d], "ch", ch_count, d)
    mixed = convolve(got, tables, own, near, ch_count)
    mixed, gates = lax.optimization_barrier((mixed, gates))
    places = list(range(ctx_count * ch_count))[::-1]
    mixed = lax.all_to_all(mixed, ("ctx", "ch"), split_axis=0, concat_axis=0, tiled=True, axis_index_groups=[places])
    return unpack(mixed, gates, own, ch_count)


def solution(mesh):
    placed = (P("ch", "ctx"), P("ch", "ctx"), P("ch", "ctx"), P("ch", "ctx"), P("ch"))
    return jax.shard_map(
        body, mesh=mesh, in_specs=placed, out_specs=P(None, ("ctx", "ch")), check_vma=False
    )
```

```python
import functools
import math

import jax
import jax.numpy as jnp
import numpy as np
from jax import lax
from jax.experimental import pallas as pl
from jax.experimental.pallas import tpu as pltpu
from jax.sharding import PartitionSpec as P

W = 256
LANES = 128
TILE = 16
CHUNK = 256


def whole_vmem():
    return pl.BlockSpec(memory_space=pltpu.VMEM)


def in_hbm():
    return pl.BlockSpec(memory_space=pltpu.HBM)


def dft_tables(blocks):
    length = blocks * W
    k = np.arange(blocks)[:, None]
    angle = 2 * np.pi * ((4 * k + 1) * np.arange(blocks)[None, :] % (4 * blocks)) / (4 * blocks)
    outer = np.concatenate([np.cos(angle), -np.sin(angle)], 0)
    turn = 2 * np.pi * ((4 * k + 1) * np.arange(W)[None, :]) / (4 * length)
    near = 2 * np.pi * (np.arange(W)[:, None] * np.arange(W)[None, :] % W) / W
    inner = np.concatenate([np.cos(near), np.sin(near)], 0)
    turns = np.concatenate([np.cos(turn), np.sin(turn)], 1)
    return [jnp.asarray(table, jnp.float32) for table in (outer, outer.T, inner, turns)]


def lay(natural, j, value):
    count = value.shape[0]
    for h in range(W // LANES):
        first = (j * (W // LANES) + h) * count
        natural[first : first + count, :] = value[:, LANES * h : LANES * (h + 1)]


def pick(natural, channel, count, blocks):
    halves = W // LANES
    rows = [natural[pl.ds(h * count + channel, blocks, stride=halves * count), :] for h in range(halves)]
    return jnp.concatenate(rows, 1)


def late_pieces(own, piece, ch_count):
    early = max(1, ch_count // 4)
    if own * piece * early % TILE:
        early = ch_count // 2
    return ch_count - early


def pack_kernel(own, blocks, group, ch_count, parts, pre_ref, val_ref, taps_ref, post_ref, *rest):
    piece = blocks // ch_count
    late = late_pieces(own, piece, ch_count)
    out_refs, gate_refs = rest[:parts], rest[parts : parts + late]
    pre_s, val_s, taps_s, post_s, natural, natural_taps, natural_gate, stage, in_sems = rest[parts + late :]
    channels = own * parts
    some = min(TILE, channels)
    rows = own * blocks
    main = rows + blocks
    loads = []
    for g in range(channels // some):
        here = pl.ds(g * some, some)
        loads.append(pltpu.make_async_copy(pre_ref.at[here], pre_s.at[here], in_sems.at[g, 0]))
        loads.append(pltpu.make_async_copy(val_ref.at[here], val_s.at[here], in_sems.at[g, 1]))
    taps_load = pltpu.make_async_copy(taps_ref, taps_s, in_sems.at[channels // some, 0])
    gate_load = pltpu.make_async_copy(post_ref, post_s, in_sems.at[channels // some, 1])
    for copy in loads[:2] + [taps_load] + loads[2:] + [gate_load]:
        copy.start()
    groups = taps_s.shape[0]
    taps_load.wait()
    for j in range(blocks):
        lay(natural_taps, j, taps_s[:, W * j : W * (j + 1)])
    for g in range(channels // some):
        loads[2 * g].wait()
        loads[2 * g + 1].wait()
        here = slice(g * some, (g + 1) * some)
        for j in range(blocks):
            cols = slice(W * j, W * (j + 1))
            product = pre_s[here, cols].astype(jnp.float32) * val_s[here, cols].astype(jnp.float32)
            lay(natural.at[g], j, product)
        for i in range(g * some // own, (g + 1) * some // own):
            for c in range(own):
                mine = pick(natural.at[g], own * i + c - g * some, some, blocks)
                stage[i, blocks * c : blocks * (c + 1), :] = mine.astype(jnp.bfloat16)
            taps = pick(natural_taps, own * i // group, groups, blocks)
            stage[i, rows:main, :] = taps.astype(jnp.bfloat16)
    gate_load.wait()
    place = lax.axis_index("ch")
    for d in range(ch_count):
        first = jnp.bitwise_xor(place, d) * (piece * W)
        if d < late:
            gate_refs[d][...] = post_s[:, pl.ds(pl.multiple_of(first, LANES), piece * W)]
        else:
            for j in range(piece):
                cols = pl.ds(pl.multiple_of(first + W * j, LANES), W)
                lay(natural_gate, (d - late) * piece + j, post_s[:, cols].astype(jnp.float32))
    early = piece * (ch_count - late)
    for i in range(parts):
        gate = [pick(natural_gate, own * i + c, channels, early) for c in range(own)]
        stage[i, main:, :] = jnp.concatenate(gate, 0).astype(jnp.bfloat16)
    me = lax.axis_index("ctx")
    for d in range(parts):
        out_refs[d][...] = stage[jnp.bitwise_xor(me, d)]


def pack(pre_gate, value, post_gate, taps, parts, ch_count):
    channels, block = value.shape
    own = channels // parts
    group = channels // taps.shape[0]
    blocks = block // W
    piece = blocks // ch_count
    late = late_pieces(own, piece, ch_count)
    early = piece * (ch_count - late)
    local = (own + 1) * blocks + own * early
    halves = W // LANES
    some = min(TILE, channels)
    args = [pltpu.with_memory_space_constraint(arg, pltpu.HBM) for arg in (pre_gate, value, taps, post_gate)]
    out = pl.pallas_call(
        functools.partial(pack_kernel, own, blocks, group, ch_count, parts),
        out_shape=[jax.ShapeDtypeStruct((local, W), jnp.bfloat16)] * parts
        + [jax.ShapeDtypeStruct((channels, piece * W), jnp.bfloat16)] * late,
        in_specs=[in_hbm()] * 4,
        out_specs=[whole_vmem()] * (parts + late),
        scratch_shapes=[
            pltpu.VMEM(pre_gate.shape, jnp.bfloat16),
            pltpu.VMEM(value.shape, jnp.bfloat16),
            pltpu.VMEM(taps.shape, jnp.float32),
            pltpu.VMEM(post_gate.shape, jnp.bfloat16),
            pltpu.VMEM((channels // some, blocks * halves * some, LANES), jnp.float32),
            pltpu.VMEM((blocks * halves * taps.shape[0], LANES), jnp.float32),
            pltpu.VMEM((early * halves * channels, LANES), jnp.float32),
            pltpu.VMEM((parts, local, W), jnp.bfloat16),
            pltpu.SemaphoreType.DMA((channels // some + 1, 2)),
        ],
        compiler_params=pltpu.CompilerParams(vmem_limit_bytes=16 * 2**20),
        name="pack",
    )(*args)
    return list(out[:parts]), list(out[parts:])


def partner_order(count):
    corners = [d for d in range(1, count) if bin(d >> 1).count("1") > 1]
    straight = [d for d in range(2, count, 2) if d not in corners]
    order = [0] + corners[:1] + straight + corners[1:]
    return order + [d for d in range(2, count) if d not in order] + [1]


def swap(piece, axis, count, d):
    return lax.ppermute(piece, axis, [(i, i ^ d) for i in range(count)])


def tables_kernel(own, skip_ref, *rest):
    outer_ref, back_ref, inner_ref, turns_ref, outer_out, back_out, ahead, rear, turns_out = rest[:9]
    outer_s, back_s, inner_s, sems = rest[9:]
    count, width = turns_ref.shape
    loads = [
        pltpu.make_async_copy(inner_ref, inner_s, sems.at[0]),
        pltpu.make_async_copy(outer_ref, outer_s, sems.at[1]),
        pltpu.make_async_copy(back_ref, back_s, sems.at[2]),
        pltpu.make_async_copy(turns_ref, turns_out.at[0:count, :], sems.at[3]),
    ]
    for copy in loads:
        copy.start()
    me = lax.axis_index("ctx")
    for c in range(own):
        turns_out[count + 8 * c : count + 8 * (c + 1), :] = jnp.full((8, width), skip_ref[own * me + c], jnp.float32)
    loads[0].wait()
    near_cos, near_sin = inner_s[0:W, :].astype(jnp.bfloat16), inner_s[W:, :].astype(jnp.bfloat16)
    for table, sign in ((ahead, -1), (rear, 1)):
        table[0:W, 0:W] = near_cos
        table[0:W, W:] = near_sin * sign
        table[W:, 0:W] = near_sin * -sign
        table[W:, W:] = near_cos
    loads[1].wait()
    outer_out[...] = outer_s[...].astype(jnp.bfloat16)
    loads[2].wait()
    back_out[...] = back_s[...].astype(jnp.bfloat16)
    loads[3].wait()


def make_tables(skip, outer, back, inner, turns, own):
    count, width = turns.shape
    args = [pltpu.with_memory_space_constraint(arg, pltpu.HBM) for arg in (outer, back, inner, turns)]
    narrow = (outer.shape, back.shape, (2 * W, 2 * W), (2 * W, 2 * W))
    return pl.pallas_call(
        functools.partial(tables_kernel, own),
        out_shape=[jax.ShapeDtypeStruct(shape, jnp.bfloat16) for shape in narrow]
        + [jax.ShapeDtypeStruct((count + 8 * own, width), jnp.float32)],
        in_specs=[pl.BlockSpec(memory_space=pltpu.SMEM)] + [in_hbm()] * 4,
        out_specs=[whole_vmem()] * 5,
        scratch_shapes=[
            pltpu.VMEM(outer.shape, jnp.float32),
            pltpu.VMEM(back.shape, jnp.float32),
            pltpu.VMEM(inner.shape, jnp.float32),
            pltpu.SemaphoreType.DMA((4,)),
        ],
        compiler_params=pltpu.CompilerParams(vmem_limit_bytes=16 * 2**20),
        name="make_tables",
    )(skip, *args)


def conv_kernel(own, near, ch_count, parts, *rest):
    got_refs = rest[:parts]
    outer_ref, back_ref, ahead, rear, turns_ref, out_ref, x_all, r_all, z_all = rest[parts:]
    blocks = parts * near
    length = blocks * W
    chunk = math.gcd(blocks, CHUNK)
    me = lax.axis_index("ctx")
    order = partner_order(parts)
    for d, got_ref in zip(order, got_refs):
        here = pl.ds(pl.multiple_of(jnp.bitwise_xor(me, d) * near, TILE), near)
        for c in range(own + 1):
            x_all[here, W * c : W * (c + 1)] = got_ref[c * near : (c + 1) * near, :]

    def dot(left, right):
        return jnp.dot(left, right, preferred_element_type=jnp.float32)

    for first in range(0, blocks, chunk):
        here = slice(first, first + chunk)
        there = slice(blocks + first, blocks + first + chunk)
        both = dot(jnp.concatenate([outer_ref[here, :], outer_ref[there, :]], 0), x_all[...])
        real, imag = both[0:chunk, :], both[chunk:, :]
        turn_cos, turn_sin = turns_ref[here, 0:W], turns_ref[here, W:]
        rows = []
        for c in range(own + 1):
            re, im = real[:, W * c : W * (c + 1)], imag[:, W * c : W * (c + 1)]
            pair = [re * turn_cos + im * turn_sin, im * turn_cos - re * turn_sin]
            rows.append(jnp.concatenate(pair, 1).astype(jnp.bfloat16))
        spectrum = dot(jnp.concatenate(rows, 0), ahead[...])
        filt_re = spectrum[chunk * own :, 0:W] * (1.0 / length)
        filt_im = spectrum[chunk * own :, W:] * (1.0 / length)
        rows = []
        for c in range(own):
            part = spectrum[chunk * c : chunk * (c + 1), :]
            re, im = part[:, 0:W], part[:, W:]
            pair = [re * filt_re - im * filt_im, re * filt_im + im * filt_re]
            rows.append(jnp.concatenate(pair, 1).astype(jnp.bfloat16))
        middle = dot(jnp.concatenate(rows, 0), rear[...])
        for c in range(own):
            part = middle[chunk * c : chunk * (c + 1), :]
            re, im = part[:, 0:W], part[:, W:]
            cols = slice(W * c, W * (c + 1))
            r_all[here, cols] = (re * turn_cos - im * turn_sin).astype(jnp.bfloat16)
            r_all[there, cols] = (re * turn_sin + im * turn_cos).astype(jnp.bfloat16)

    conv = dot(back_ref[...], r_all[...])
    for c in range(own):
        cols = slice(W * c, W * (c + 1))
        z_all[c] = conv[:, cols] + turns_ref[blocks + 8 * c : blocks + 8 * c + 1, 0:W] * x_all[:, cols].astype(jnp.float32)
    some = out_ref.shape[1] // own
    late = late_pieces(own, some, ch_count)
    early = some * (ch_count - late)
    place = lax.axis_index("ch")
    for d, got_ref in zip(order, got_refs):
        k = jnp.bitwise_xor(me, d)
        gate = got_ref[(own + 1) * near :, :].astype(jnp.float32)
        mine = [z_all[c, pl.ds(pl.multiple_of(k * near, TILE), near), :] for c in range(own)]
        for m in range(ch_count):
            rows = [part[m * some : (m + 1) * some, :] for part in mine]
            for e in range(late, ch_count):
                at = (e - late) * some
                for c in range(own):
                    factor = jnp.where(jnp.bitwise_xor(place, e) == m, gate[c * early + at : c * early + at + some, :], 1.0)
                    rows[c] = rows[c] * factor
            out_ref[k * ch_count + m] = jnp.concatenate(rows, 0).astype(jnp.bfloat16)


def convolve(got, tables, own, near, ch_count):
    parts = len(got)
    blocks = parts * near
    owners = parts * ch_count
    return pl.pallas_call(
        functools.partial(conv_kernel, own, near, ch_count, parts),
        out_shape=jax.ShapeDtypeStruct((owners, own * blocks // owners, W), jnp.bfloat16),
        in_specs=[whole_vmem()] * (parts + len(tables)),
        out_specs=whole_vmem(),
        scratch_shapes=[
            pltpu.VMEM((blocks, W * (own + 1)), jnp.bfloat16),
            pltpu.VMEM((2 * blocks, W * own), jnp.bfloat16),
            pltpu.VMEM((own, blocks, W), jnp.float32),
        ],
        compiler_params=pltpu.CompilerParams(vmem_limit_bytes=32 * 2**20),
        cost_estimate=pl.CostEstimate(flops=blocks * W, bytes_accessed=4 * blocks * W, transcendentals=0),
        name="convolve",
    )(*got, *tables)


def unpack_kernel(own, got_ref, *rest):
    gate_refs, (out_ref, flat, gate_s, stage, sems) = rest[:-5], rest[-5:]
    sources, rows, _ = got_ref.shape
    some = rows // own
    place = lax.axis_index("ch")
    channels, width = gate_refs[0].shape
    ch_count = out_ref.shape[0] // channels
    for d in range(ch_count):
        here = pl.ds(pl.multiple_of(jnp.bitwise_xor(place, d) * channels, TILE), channels)
        gate_s[here, :] = gate_refs[d][...] if d < len(gate_refs) else jnp.ones((channels, width), jnp.bfloat16)
    copies = []
    for m in range(ch_count):
        here = slice(m * channels, (m + 1) * channels)
        for k in range(sources // ch_count):
            part = got_ref[k * ch_count + m].astype(jnp.float32)
            first = m * channels * some + k * rows
            for h in range(W // LANES):
                flat[h, first : first + rows, :] = part[:, LANES * h : LANES * (h + 1)]
        for j in range(some):
            for h in range(W // LANES):
                part = flat[h, pl.ds(m * channels * some + j, channels, stride=some), :]
                first = W * j + LANES * h
                cols = slice(first, first + LANES)
                stage[here, cols] = (part * gate_s[here, cols].astype(jnp.float32)).astype(jnp.bfloat16)
        copies.append(pltpu.make_async_copy(stage.at[here], out_ref.at[here], sems.at[m]))
        copies[m].start()
    for copy in copies:
        copy.wait()


def unpack(got, gates, own, ch_count):
    sources, rows, _ = got.shape
    shape = (sources * own, rows // own * W)
    if rows % TILE:
        ones = [jnp.ones_like(gates[0])] * (ch_count - len(gates))
        order = jnp.bitwise_xor(lax.axis_index("ch"), jnp.arange(ch_count))
        gate = jnp.stack(gates + ones)[order].reshape(shape)
        got = got.reshape(-1, ch_count, rows, W).swapaxes(0, 1)
        return (got.reshape(shape).astype(jnp.float32) * gate.astype(jnp.float32)).astype(jnp.bfloat16)
    return pl.pallas_call(
        functools.partial(unpack_kernel, own),
        out_shape=jax.ShapeDtypeStruct(shape, jnp.bfloat16),
        in_specs=[whole_vmem()] * (1 + len(gates)),
        out_specs=in_hbm(),
        scratch_shapes=[
            pltpu.VMEM((W // LANES, sources * rows, LANES), jnp.float32),
            pltpu.VMEM(shape, jnp.bfloat16),
            pltpu.VMEM(shape, jnp.bfloat16),
            pltpu.SemaphoreType.DMA((ch_count,)),
        ],
        compiler_params=pltpu.CompilerParams(vmem_limit_bytes=24 * 2**20),
        name="unpack",
    )(got, *[pltpu.with_memory_space_constraint(gate, pltpu.VMEM) for gate in gates])


def body(pre_gate, value, post_gate, filter_taps, skip):
    ctx_count = lax.axis_size("ctx")
    ch_count = lax.axis_size("ch")
    own = value.shape[0] // ctx_count
    near = value.shape[1] // W
    got, gates = pack(pre_gate, value, post_gate, filter_taps, ctx_count, ch_count)
    order = partner_order(ctx_count)
    got = [got[d] for d in order]
    tables, skip, _ = lax.optimization_barrier((dft_tables(near * ctx_count), skip, got[0]))
    tables = list(make_tables(skip, *tables, own))
    got = [swap(piece, "ctx", ctx_count, d) if d else piece for piece, d in zip(got, order)]
    for d in range(1, len(gates)):
        gates[d] = swap(gates[d], "ch", ch_count, d)
    mixed = convolve(got, tables, own, near, ch_count)
    mixed, gates = lax.optimization_barrier((mixed, gates[::-1]))
    gates = gates[::-1]
    mixed = lax.all_to_all(mixed, ("ctx", "ch"), split_axis=0, concat_axis=0, tiled=True)
    return unpack(mixed, gates, own, ch_count)


def solution(mesh):
    placed = (P("ch", "ctx"), P("ch", "ctx"), P("ch", "ctx"), P("ch", "ctx"), P("ch"))
    return jax.shard_map(
        body, mesh=mesh, in_specs=placed, out_specs=P(None, ("ctx", "ch")), check_vma=False
    )
```

```python
import functools
import math

import jax
import jax.numpy as jnp
import numpy as np
from jax import lax
from jax.experimental import pallas as pl
from jax.experimental.pallas import tpu as pltpu
from jax.sharding import PartitionSpec as P

W = 256
LANES = 128
TILE = 16
CHUNK = 256


def whole_vmem():
    return pl.BlockSpec(memory_space=pltpu.VMEM)


def in_hbm():
    return pl.BlockSpec(memory_space=pltpu.HBM)


def dft_tables(blocks):
    length = blocks * W
    k = np.arange(blocks)[:, None]
    angle = 2 * np.pi * ((4 * k + 1) * np.arange(blocks)[None, :] % (4 * blocks)) / (4 * blocks)
    outer = np.concatenate([np.cos(angle), -np.sin(angle)], 0)
    turn = 2 * np.pi * ((4 * k + 1) * np.arange(W)[None, :]) / (4 * length)
    near = 2 * np.pi * (np.arange(W)[:, None] * np.arange(W)[None, :] % W) / W
    inner = np.concatenate([np.cos(near), np.sin(near)], 0)
    turns = np.concatenate([np.cos(turn), np.sin(turn)], 1)
    return [jnp.asarray(table, jnp.float32) for table in (outer, outer.T, inner, turns)]


def lay(natural, j, value):
    count = value.shape[0]
    for h in range(W // LANES):
        first = (j * (W // LANES) + h) * count
        natural[first : first + count, :] = value[:, LANES * h : LANES * (h + 1)]


def pick(natural, channel, count, blocks):
    halves = W // LANES
    rows = [natural[pl.ds(h * count + channel, blocks, stride=halves * count), :] for h in range(halves)]
    return jnp.concatenate(rows, 1)


def late_pieces(own, piece, ch_count):
    early = max(1, ch_count // 4)
    if own * piece * early % TILE:
        early = ch_count // 2
    return ch_count - early


def pack_kernel(own, blocks, group, ch_count, parts, pre_ref, val_ref, taps_ref, post_ref, *rest):
    piece = blocks // ch_count
    late = late_pieces(own, piece, ch_count)
    out_refs, gate_refs = rest[:parts], rest[parts : parts + late]
    pre_s, val_s, taps_s, post_s, natural, natural_taps, natural_gate, stage, in_sems = rest[parts + late :]
    channels = own * parts
    some = min(TILE, channels)
    rows = own * blocks
    main = rows + blocks
    loads = []
    for g in range(channels // some):
        here = pl.ds(g * some, some)
        loads.append(pltpu.make_async_copy(pre_ref.at[here], pre_s.at[here], in_sems.at[g, 0]))
        loads.append(pltpu.make_async_copy(val_ref.at[here], val_s.at[here], in_sems.at[g, 1]))
    taps_load = pltpu.make_async_copy(taps_ref, taps_s, in_sems.at[channels // some, 0])
    gate_load = pltpu.make_async_copy(post_ref, post_s, in_sems.at[channels // some, 1])
    for copy in loads[:2] + [taps_load] + loads[2:] + [gate_load]:
        copy.start()
    groups = taps_s.shape[0]
    taps_load.wait()
    for j in range(blocks):
        lay(natural_taps, j, taps_s[:, W * j : W * (j + 1)])
    for g in range(channels // some):
        loads[2 * g].wait()
        loads[2 * g + 1].wait()
        here = slice(g * some, (g + 1) * some)
        for j in range(blocks):
            cols = slice(W * j, W * (j + 1))
            product = pre_s[here, cols].astype(jnp.float32) * val_s[here, cols].astype(jnp.float32)
            lay(natural.at[g], j, product)
        for i in range(g * some // own, (g + 1) * some // own):
            for c in range(own):
                mine = pick(natural.at[g], own * i + c - g * some, some, blocks)
                stage[i, blocks * c : blocks * (c + 1), :] = mine.astype(jnp.bfloat16)
            taps = pick(natural_taps, own * i // group, groups, blocks)
            stage[i, rows:main, :] = taps.astype(jnp.bfloat16)
    gate_load.wait()
    place = lax.axis_index("ch")
    for d in range(ch_count):
        first = jnp.bitwise_xor(place, d) * (piece * W)
        if d < late:
            gate_refs[d][...] = post_s[:, pl.ds(pl.multiple_of(first, LANES), piece * W)]
        else:
            for j in range(piece):
                cols = pl.ds(pl.multiple_of(first + W * j, LANES), W)
                lay(natural_gate, (d - late) * piece + j, post_s[:, cols].astype(jnp.float32))
    early = piece * (ch_count - late)
    for i in range(parts):
        gate = [pick(natural_gate, own * i + c, channels, early) for c in range(own)]
        stage[i, main:, :] = jnp.concatenate(gate, 0).astype(jnp.bfloat16)
    me = lax.axis_index("ctx")
    for d in range(parts):
        out_refs[d][...] = stage[jnp.bitwise_xor(me, d)]


def pack(pre_gate, value, post_gate, taps, parts, ch_count):
    channels, block = value.shape
    own = channels // parts
    group = channels // taps.shape[0]
    blocks = block // W
    piece = blocks // ch_count
    late = late_pieces(own, piece, ch_count)
    early = piece * (ch_count - late)
    local = (own + 1) * blocks + own * early
    halves = W // LANES
    some = min(TILE, channels)
    args = [pltpu.with_memory_space_constraint(arg, pltpu.HBM) for arg in (pre_gate, value, taps, post_gate)]
    out = pl.pallas_call(
        functools.partial(pack_kernel, own, blocks, group, ch_count, parts),
        out_shape=[jax.ShapeDtypeStruct((local, W), jnp.bfloat16)] * parts
        + [jax.ShapeDtypeStruct((channels, piece * W), jnp.bfloat16)] * late,
        in_specs=[in_hbm()] * 4,
        out_specs=[whole_vmem()] * (parts + late),
        scratch_shapes=[
            pltpu.VMEM(pre_gate.shape, jnp.bfloat16),
            pltpu.VMEM(value.shape, jnp.bfloat16),
            pltpu.VMEM(taps.shape, jnp.float32),
            pltpu.VMEM(post_gate.shape, jnp.bfloat16),
            pltpu.VMEM((channels // some, blocks * halves * some, LANES), jnp.float32),
            pltpu.VMEM((blocks * halves * taps.shape[0], LANES), jnp.float32),
            pltpu.VMEM((early * halves * channels, LANES), jnp.float32),
            pltpu.VMEM((parts, local, W), jnp.bfloat16),
            pltpu.SemaphoreType.DMA((channels // some + 1, 2)),
        ],
        compiler_params=pltpu.CompilerParams(vmem_limit_bytes=16 * 2**20),
        name="pack",
    )(*args)
    return list(out[:parts]), list(out[parts:])


def partner_order(count):
    corners = [d for d in range(1, count) if bin(d >> 1).count("1") > 1]
    straight = [d for d in range(2, count, 2) if d not in corners]
    order = [0] + corners[:1] + straight + corners[1:]
    return order + [d for d in range(2, count) if d not in order] + [1]


def swap(piece, axis, count, d):
    return lax.ppermute(piece, axis, [(i, i ^ d) for i in range(count)])


def tables_kernel(own, skip_ref, *rest):
    outer_ref, back_ref, inner_ref, turns_ref, outer_out, back_out, ahead, rear, turns_out = rest[:9]
    outer_s, back_s, inner_s, sems = rest[9:]
    count, width = turns_ref.shape
    loads = [
        pltpu.make_async_copy(inner_ref, inner_s, sems.at[0]),
        pltpu.make_async_copy(outer_ref, outer_s, sems.at[1]),
        pltpu.make_async_copy(back_ref, back_s, sems.at[2]),
        pltpu.make_async_copy(turns_ref, turns_out.at[0:count, :], sems.at[3]),
    ]
    for copy in loads:
        copy.start()
    me = lax.axis_index("ctx")
    for c in range(own):
        turns_out[count + 8 * c : count + 8 * (c + 1), :] = jnp.full((8, width), skip_ref[own * me + c], jnp.float32)
    loads[0].wait()
    near_cos, near_sin = inner_s[0:W, :].astype(jnp.bfloat16), inner_s[W:, :].astype(jnp.bfloat16)
    for table, sign in ((ahead, -1), (rear, 1)):
        table[0:W, 0:W] = near_cos
        table[0:W, W:] = near_sin * sign
        table[W:, 0:W] = near_sin * -sign
        table[W:, W:] = near_cos
    loads[1].wait()
    outer_out[...] = outer_s[...].astype(jnp.bfloat16)
    loads[2].wait()
    back_out[...] = back_s[...].astype(jnp.bfloat16)
    loads[3].wait()


def make_tables(skip, outer, back, inner, turns, own):
    count, width = turns.shape
    args = [pltpu.with_memory_space_constraint(arg, pltpu.HBM) for arg in (outer, back, inner, turns)]
    narrow = (outer.shape, back.shape, (2 * W, 2 * W), (2 * W, 2 * W))
    return pl.pallas_call(
        functools.partial(tables_kernel, own),
        out_shape=[jax.ShapeDtypeStruct(shape, jnp.bfloat16) for shape in narrow]
        + [jax.ShapeDtypeStruct((count + 8 * own, width), jnp.float32)],
        in_specs=[pl.BlockSpec(memory_space=pltpu.SMEM)] + [in_hbm()] * 4,
        out_specs=[whole_vmem()] * 5,
        scratch_shapes=[
            pltpu.VMEM(outer.shape, jnp.float32),
            pltpu.VMEM(back.shape, jnp.float32),
            pltpu.VMEM(inner.shape, jnp.float32),
            pltpu.SemaphoreType.DMA((4,)),
        ],
        compiler_params=pltpu.CompilerParams(vmem_limit_bytes=16 * 2**20),
        name="make_tables",
    )(skip, *args)


def conv_kernel(own, near, ch_count, parts, *rest):
    got_refs = rest[:parts]
    outer_ref, back_ref, ahead, rear, turns_ref, out_ref, x_all, r_all, z_all = rest[parts:]
    blocks = parts * near
    length = blocks * W
    chunk = math.gcd(blocks, CHUNK)
    me = lax.axis_index("ctx")
    order = partner_order(parts)
    for d, got_ref in zip(order, got_refs):
        here = pl.ds(pl.multiple_of(jnp.bitwise_xor(me, d) * near, TILE), near)
        for c in range(own + 1):
            x_all[here, W * c : W * (c + 1)] = got_ref[c * near : (c + 1) * near, :]

    def dot(left, right):
        return jnp.dot(left, right, preferred_element_type=jnp.float32)

    for first in range(0, blocks, chunk):
        here = slice(first, first + chunk)
        there = slice(blocks + first, blocks + first + chunk)
        both = dot(jnp.concatenate([outer_ref[here, :], outer_ref[there, :]], 0), x_all[...])
        real, imag = both[0:chunk, :], both[chunk:, :]
        turn_cos, turn_sin = turns_ref[here, 0:W], turns_ref[here, W:]
        rows = []
        for c in range(own + 1):
            re, im = real[:, W * c : W * (c + 1)], imag[:, W * c : W * (c + 1)]
            pair = [re * turn_cos + im * turn_sin, im * turn_cos - re * turn_sin]
            rows.append(jnp.concatenate(pair, 1).astype(jnp.bfloat16))
        spectrum = dot(jnp.concatenate(rows, 0), ahead[...])
        filt_re = spectrum[chunk * own :, 0:W] * (1.0 / length)
        filt_im = spectrum[chunk * own :, W:] * (1.0 / length)
        rows = []
        for c in range(own):
            part = spectrum[chunk * c : chunk * (c + 1), :]
            re, im = part[:, 0:W], part[:, W:]
            pair = [re * filt_re - im * filt_im, re * filt_im + im * filt_re]
            rows.append(jnp.concatenate(pair, 1).astype(jnp.bfloat16))
        middle = dot(jnp.concatenate(rows, 0), rear[...])
        for c in range(own):
            part = middle[chunk * c : chunk * (c + 1), :]
            re, im = part[:, 0:W], part[:, W:]
            cols = slice(W * c, W * (c + 1))
            r_all[here, cols] = (re * turn_cos - im * turn_sin).astype(jnp.bfloat16)
            r_all[there, cols] = (re * turn_sin + im * turn_cos).astype(jnp.bfloat16)

    conv = dot(back_ref[...], r_all[...])
    for c in range(own):
        cols = slice(W * c, W * (c + 1))
        z_all[c] = conv[:, cols] + turns_ref[blocks + 8 * c : blocks + 8 * c + 1, 0:W] * x_all[:, cols].astype(jnp.float32)
    some = out_ref.shape[1] // own
    late = late_pieces(own, some, ch_count)
    early = some * (ch_count - late)
    place = lax.axis_index("ch")
    for d, got_ref in zip(order, got_refs):
        k = jnp.bitwise_xor(me, d)
        gate = got_ref[(own + 1) * near :, :].astype(jnp.float32)
        mine = [z_all[c, pl.ds(pl.multiple_of(k * near, TILE), near), :] for c in range(own)]
        for m in range(ch_count):
            rows = [part[m * some : (m + 1) * some, :] for part in mine]
            for e in range(late, ch_count):
                at = (e - late) * some
                for c in range(own):
                    factor = jnp.where(jnp.bitwise_xor(place, e) == m, gate[c * early + at : c * early + at + some, :], 1.0)
                    rows[c] = rows[c] * factor
            out_ref[k * ch_count + m] = jnp.concatenate(rows, 0).astype(jnp.bfloat16)


def convolve(got, tables, own, near, ch_count):
    parts = len(got)
    blocks = parts * near
    owners = parts * ch_count
    return pl.pallas_call(
        functools.partial(conv_kernel, own, near, ch_count, parts),
        out_shape=jax.ShapeDtypeStruct((owners, own * blocks // owners, W), jnp.bfloat16),
        in_specs=[whole_vmem()] * (parts + len(tables)),
        out_specs=whole_vmem(),
        scratch_shapes=[
            pltpu.VMEM((blocks, W * (own + 1)), jnp.bfloat16),
            pltpu.VMEM((2 * blocks, W * own), jnp.bfloat16),
            pltpu.VMEM((own, blocks, W), jnp.float32),
        ],
        compiler_params=pltpu.CompilerParams(vmem_limit_bytes=32 * 2**20),
        cost_estimate=pl.CostEstimate(flops=16000 * blocks * W, bytes_accessed=4 * blocks * W, transcendentals=0),
        name="convolve",
    )(*got, *tables)


def unpack_kernel(own, got_ref, *rest):
    gate_refs, (out_ref, flat, gate_s, stage, sems) = rest[:-5], rest[-5:]
    sources, rows, _ = got_ref.shape
    some = rows // own
    place = lax.axis_index("ch")
    channels, width = gate_refs[0].shape
    ch_count = out_ref.shape[0] // channels
    for d in range(ch_count):
        here = pl.ds(pl.multiple_of(jnp.bitwise_xor(place, d) * channels, TILE), channels)
        gate_s[here, :] = gate_refs[d][...] if d < len(gate_refs) else jnp.ones((channels, width), jnp.bfloat16)
    copies = []
    for m in range(ch_count):
        here = slice(m * channels, (m + 1) * channels)
        for k in range(sources // ch_count):
            part = got_ref[k * ch_count + m].astype(jnp.float32)
            first = m * channels * some + k * rows
            for h in range(W // LANES):
                flat[h, first : first + rows, :] = part[:, LANES * h : LANES * (h + 1)]
        for j in range(some):
            for h in range(W // LANES):
                part = flat[h, pl.ds(m * channels * some + j, channels, stride=some), :]
                first = W * j + LANES * h
                cols = slice(first, first + LANES)
                stage[here, cols] = (part * gate_s[here, cols].astype(jnp.float32)).astype(jnp.bfloat16)
        copies.append(pltpu.make_async_copy(stage.at[here], out_ref.at[here], sems.at[m]))
        copies[m].start()
    for copy in copies:
        copy.wait()


def unpack(got, gates, own, ch_count):
    sources, rows, _ = got.shape
    shape = (sources * own, rows // own * W)
    if rows % TILE:
        ones = [jnp.ones_like(gates[0])] * (ch_count - len(gates))
        order = jnp.bitwise_xor(lax.axis_index("ch"), jnp.arange(ch_count))
        gate = jnp.stack(gates + ones)[order].reshape(shape)
        got = got.reshape(-1, ch_count, rows, W).swapaxes(0, 1)
        return (got.reshape(shape).astype(jnp.float32) * gate.astype(jnp.float32)).astype(jnp.bfloat16)
    return pl.pallas_call(
        functools.partial(unpack_kernel, own),
        out_shape=jax.ShapeDtypeStruct(shape, jnp.bfloat16),
        in_specs=[whole_vmem()] * (1 + len(gates)),
        out_specs=in_hbm(),
        scratch_shapes=[
            pltpu.VMEM((W // LANES, sources * rows, LANES), jnp.float32),
            pltpu.VMEM(shape, jnp.bfloat16),
            pltpu.VMEM(shape, jnp.bfloat16),
            pltpu.SemaphoreType.DMA((ch_count,)),
        ],
        compiler_params=pltpu.CompilerParams(vmem_limit_bytes=24 * 2**20),
        name="unpack",
    )(got, *[pltpu.with_memory_space_constraint(gate, pltpu.VMEM) for gate in gates])


def body(pre_gate, value, post_gate, filter_taps, skip):
    ctx_count = lax.axis_size("ctx")
    ch_count = lax.axis_size("ch")
    own = value.shape[0] // ctx_count
    near = value.shape[1] // W
    got, gates = pack(pre_gate, value, post_gate, filter_taps, ctx_count, ch_count)
    order = partner_order(ctx_count)
    got = [got[d] for d in order]
    tables, skip, _ = lax.optimization_barrier((dft_tables(near * ctx_count), skip, got[0]))
    tables = list(make_tables(skip, *tables, own))
    got = [swap(piece, "ctx", ctx_count, d) if d else piece for piece, d in zip(got, order)]
    for d in range(1, len(gates)):
        gates[d] = swap(gates[d], "ch", ch_count, d)
    got[1:], gates[2:] = lax.optimization_barrier((got[1:], gates[2:]))
    mixed = convolve(got, tables, own, near, ch_count)
    mixed, gates = lax.optimization_barrier((mixed, gates[::-1]))
    gates = gates[::-1]
    mixed = lax.all_to_all(mixed, ("ctx", "ch"), split_axis=0, concat_axis=0, tiled=True)
    return unpack(mixed, gates, own, ch_count)


def solution(mesh):
    placed = (P("ch", "ctx"), P("ch", "ctx"), P("ch", "ctx"), P("ch", "ctx"), P("ch"))
    return jax.shard_map(
        body, mesh=mesh, in_specs=placed, out_specs=P(None, ("ctx", "ch")), check_vma=False
    )
```

```python
import functools
import math

import jax
import jax.numpy as jnp
import numpy as np
from jax import lax
from jax.experimental import pallas as pl
from jax.experimental.pallas import tpu as pltpu
from jax.sharding import PartitionSpec as P

W = 256
LANES = 128
TILE = 16
CHUNK = 256


def whole_vmem():
    return pl.BlockSpec(memory_space=pltpu.VMEM)


def in_hbm():
    return pl.BlockSpec(memory_space=pltpu.HBM)


def dft_tables(blocks):
    length = blocks * W
    k = np.arange(blocks)[:, None]
    angle = 2 * np.pi * ((4 * k + 1) * np.arange(blocks)[None, :] % (4 * blocks)) / (4 * blocks)
    outer = np.concatenate([np.cos(angle), -np.sin(angle)], 0)
    turn = 2 * np.pi * ((4 * k + 1) * np.arange(W)[None, :]) / (4 * length)
    near = 2 * np.pi * (np.arange(W)[:, None] * np.arange(W)[None, :] % W) / W
    inner = np.concatenate([np.cos(near), np.sin(near)], 0)
    turns = np.concatenate([np.cos(turn), np.sin(turn)], 1)
    return [jnp.asarray(table, jnp.float32) for table in (outer, outer.T, inner, turns)]


def lay(natural, j, value):
    count = value.shape[0]
    for h in range(W // LANES):
        first = (j * (W // LANES) + h) * count
        natural[first : first + count, :] = value[:, LANES * h : LANES * (h + 1)]


def pick(natural, channel, count, blocks):
    halves = W // LANES
    rows = [natural[pl.ds(h * count + channel, blocks, stride=halves * count), :] for h in range(halves)]
    return jnp.concatenate(rows, 1)


def late_pieces(own, piece, ch_count):
    early = max(1, ch_count // 4)
    if own * piece * early % TILE:
        early = ch_count // 2
    return ch_count - early


def pack_kernel(own, blocks, group, ch_count, parts, pre_ref, val_ref, taps_ref, post_ref, *rest):
    piece = blocks // ch_count
    late = late_pieces(own, piece, ch_count)
    out_refs, gate_refs = rest[:parts], rest[parts : parts + late]
    pre_s, val_s, taps_s, post_s, natural, natural_taps, natural_gate, stage, in_sems = rest[parts + late :]
    channels = own * parts
    some = min(TILE, channels)
    rows = own * blocks
    main = rows + blocks
    loads = []
    for g in range(channels // some):
        here = pl.ds(g * some, some)
        loads.append(pltpu.make_async_copy(pre_ref.at[here], pre_s.at[here], in_sems.at[g, 0]))
        loads.append(pltpu.make_async_copy(val_ref.at[here], val_s.at[here], in_sems.at[g, 1]))
    taps_load = pltpu.make_async_copy(taps_ref, taps_s, in_sems.at[channels // some, 0])
    gate_load = pltpu.make_async_copy(post_ref, post_s, in_sems.at[channels // some, 1])
    for copy in loads[:2] + [taps_load] + loads[2:] + [gate_load]:
        copy.start()
    groups = taps_s.shape[0]
    taps_load.wait()
    for j in range(blocks):
        lay(natural_taps, j, taps_s[:, W * j : W * (j + 1)])
    for g in range(channels // some):
        loads[2 * g].wait()
        loads[2 * g + 1].wait()
        here = slice(g * some, (g + 1) * some)
        for j in range(blocks):
            cols = slice(W * j, W * (j + 1))
            product = pre_s[here, cols].astype(jnp.float32) * val_s[here, cols].astype(jnp.float32)
            lay(natural.at[g], j, product)
        for i in range(g * some // own, (g + 1) * some // own):
            for c in range(own):
                mine = pick(natural.at[g], own * i + c - g * some, some, blocks)
                stage[i, blocks * c : blocks * (c + 1), :] = mine.astype(jnp.bfloat16)
            taps = pick(natural_taps, own * i // group, groups, blocks)
            stage[i, rows:main, :] = taps.astype(jnp.bfloat16)
    gate_load.wait()
    place = lax.axis_index("ch")
    for d in range(ch_count):
        first = jnp.bitwise_xor(place, d) * (piece * W)
        if d < late:
            gate_refs[d][...] = post_s[:, pl.ds(pl.multiple_of(first, LANES), piece * W)]
        else:
            for j in range(piece):
                cols = pl.ds(pl.multiple_of(first + W * j, LANES), W)
                lay(natural_gate, (d - late) * piece + j, post_s[:, cols].astype(jnp.float32))
    early = piece * (ch_count - late)
    for i in range(parts):
        gate = [pick(natural_gate, own * i + c, channels, early) for c in range(own)]
        stage[i, main:, :] = jnp.concatenate(gate, 0).astype(jnp.bfloat16)
    me = lax.axis_index("ctx")
    for d in range(parts):
        out_refs[d][...] = stage[jnp.bitwise_xor(me, d)]


def pack(pre_gate, value, post_gate, taps, parts, ch_count):
    channels, block = value.shape
    own = channels // parts
    group = channels // taps.shape[0]
    blocks = block // W
    piece = blocks // ch_count
    late = late_pieces(own, piece, ch_count)
    early = piece * (ch_count - late)
    local = (own + 1) * blocks + own * early
    halves = W // LANES
    some = min(TILE, channels)
    args = [pltpu.with_memory_space_constraint(arg, pltpu.HBM) for arg in (pre_gate, value, taps, post_gate)]
    out = pl.pallas_call(
        functools.partial(pack_kernel, own, blocks, group, ch_count, parts),
        out_shape=[jax.ShapeDtypeStruct((local, W), jnp.bfloat16)] * parts
        + [jax.ShapeDtypeStruct((channels, piece * W), jnp.bfloat16)] * late,
        in_specs=[in_hbm()] * 4,
        out_specs=[whole_vmem()] * (parts + late),
        scratch_shapes=[
            pltpu.VMEM(pre_gate.shape, jnp.bfloat16),
            pltpu.VMEM(value.shape, jnp.bfloat16),
            pltpu.VMEM(taps.shape, jnp.float32),
            pltpu.VMEM(post_gate.shape, jnp.bfloat16),
            pltpu.VMEM((channels // some, blocks * halves * some, LANES), jnp.float32),
            pltpu.VMEM((blocks * halves * taps.shape[0], LANES), jnp.float32),
            pltpu.VMEM((early * halves * channels, LANES), jnp.float32),
            pltpu.VMEM((parts, local, W), jnp.bfloat16),
            pltpu.SemaphoreType.DMA((channels // some + 1, 2)),
        ],
        compiler_params=pltpu.CompilerParams(vmem_limit_bytes=16 * 2**20),
        name="pack",
    )(*args)
    return list(out[:parts]), list(out[parts:])


def partner_order(count):
    corners = [d for d in range(1, count) if bin(d >> 1).count("1") > 1]
    straight = [d for d in range(2, count, 2) if d not in corners]
    order = [0] + corners[:1] + straight + corners[1:]
    return order + [d for d in range(2, count) if d not in order] + [1]


def swap(piece, axis, count, d):
    return lax.ppermute(piece, axis, [(i, i ^ d) for i in range(count)])


def tables_kernel(own, skip_ref, *rest):
    outer_ref, back_ref, inner_ref, turns_ref, outer_out, back_out, ahead, rear, turns_out = rest[:9]
    outer_s, back_s, inner_s, sems = rest[9:]
    count, width = turns_ref.shape
    loads = [
        pltpu.make_async_copy(inner_ref, inner_s, sems.at[0]),
        pltpu.make_async_copy(outer_ref, outer_s, sems.at[1]),
        pltpu.make_async_copy(back_ref, back_s, sems.at[2]),
        pltpu.make_async_copy(turns_ref, turns_out.at[0:count, :], sems.at[3]),
    ]
    for copy in loads:
        copy.start()
    me = lax.axis_index("ctx")
    for c in range(own):
        turns_out[count + 8 * c : count + 8 * (c + 1), :] = jnp.full((8, width), skip_ref[own * me + c], jnp.float32)
    loads[0].wait()
    near_cos, near_sin = inner_s[0:W, :].astype(jnp.bfloat16), inner_s[W:, :].astype(jnp.bfloat16)
    for table, sign in ((ahead, -1), (rear, 1)):
        table[0:W, 0:W] = near_cos
        table[0:W, W:] = near_sin * sign
        table[W:, 0:W] = near_sin * -sign
        table[W:, W:] = near_cos
    loads[1].wait()
    outer_out[...] = outer_s[...].astype(jnp.bfloat16)
    loads[2].wait()
    back_out[...] = back_s[...].astype(jnp.bfloat16)
    loads[3].wait()


def make_tables(skip, outer, back, inner, turns, own):
    count, width = turns.shape
    args = [pltpu.with_memory_space_constraint(arg, pltpu.HBM) for arg in (outer, back, inner, turns)]
    narrow = (outer.shape, back.shape, (2 * W, 2 * W), (2 * W, 2 * W))
    return pl.pallas_call(
        functools.partial(tables_kernel, own),
        out_shape=[jax.ShapeDtypeStruct(shape, jnp.bfloat16) for shape in narrow]
        + [jax.ShapeDtypeStruct((count + 8 * own, width), jnp.float32)],
        in_specs=[pl.BlockSpec(memory_space=pltpu.SMEM)] + [in_hbm()] * 4,
        out_specs=[whole_vmem()] * 5,
        scratch_shapes=[
            pltpu.VMEM(outer.shape, jnp.float32),
            pltpu.VMEM(back.shape, jnp.float32),
            pltpu.VMEM(inner.shape, jnp.float32),
            pltpu.SemaphoreType.DMA((4,)),
        ],
        compiler_params=pltpu.CompilerParams(vmem_limit_bytes=16 * 2**20),
        name="make_tables",
    )(skip, *args)


def conv_kernel(own, near, ch_count, parts, *rest):
    got_refs = rest[:parts]
    outer_ref, back_ref, ahead, rear, turns_ref, out_ref, x_all, r_all, z_all = rest[parts:]
    blocks = parts * near
    length = blocks * W
    chunk = math.gcd(blocks, CHUNK)
    me = lax.axis_index("ctx")
    order = partner_order(parts)
    for d, got_ref in zip(order, got_refs):
        here = pl.ds(pl.multiple_of(jnp.bitwise_xor(me, d) * near, TILE), near)
        for c in range(own + 1):
            x_all[here, W * c : W * (c + 1)] = got_ref[c * near : (c + 1) * near, :]

    def dot(left, right):
        return jnp.dot(left, right, preferred_element_type=jnp.float32)

    for first in range(0, blocks, chunk):
        here = slice(first, first + chunk)
        there = slice(blocks + first, blocks + first + chunk)
        both = dot(jnp.concatenate([outer_ref[here, :], outer_ref[there, :]], 0), x_all[...])
        real, imag = both[0:chunk, :], both[chunk:, :]
        turn_cos, turn_sin = turns_ref[here, 0:W], turns_ref[here, W:]
        rows = []
        for c in range(own + 1):
            re, im = real[:, W * c : W * (c + 1)], imag[:, W * c : W * (c + 1)]
            pair = [re * turn_cos + im * turn_sin, im * turn_cos - re * turn_sin]
            rows.append(jnp.concatenate(pair, 1).astype(jnp.bfloat16))
        spectrum = dot(jnp.concatenate(rows, 0), ahead[...])
        filt_re = spectrum[chunk * own :, 0:W] * (1.0 / length)
        filt_im = spectrum[chunk * own :, W:] * (1.0 / length)
        rows = []
        for c in range(own):
            part = spectrum[chunk * c : chunk * (c + 1), :]
            re, im = part[:, 0:W], part[:, W:]
            pair = [re * filt_re - im * filt_im, re * filt_im + im * filt_re]
            rows.append(jnp.concatenate(pair, 1).astype(jnp.bfloat16))
        middle = dot(jnp.concatenate(rows, 0), rear[...])
        for c in range(own):
            part = middle[chunk * c : chunk * (c + 1), :]
            re, im = part[:, 0:W], part[:, W:]
            cols = slice(W * c, W * (c + 1))
            r_all[here, cols] = (re * turn_cos - im * turn_sin).astype(jnp.bfloat16)
            r_all[there, cols] = (re * turn_sin + im * turn_cos).astype(jnp.bfloat16)

    conv = dot(back_ref[...], r_all[...])
    for c in range(own):
        cols = slice(W * c, W * (c + 1))
        z_all[c] = conv[:, cols] + turns_ref[blocks + 8 * c : blocks + 8 * c + 1, 0:W] * x_all[:, cols].astype(jnp.float32)
    some = out_ref.shape[1] // own
    late = late_pieces(own, some, ch_count)
    early = some * (ch_count - late)
    place = lax.axis_index("ch")
    for d, got_ref in zip(order, got_refs):
        k = jnp.bitwise_xor(me, d)
        gate = got_ref[(own + 1) * near :, :].astype(jnp.float32)
        mine = [z_all[c, pl.ds(pl.multiple_of(k * near, TILE), near), :] for c in range(own)]
        for m in range(ch_count):
            rows = [part[m * some : (m + 1) * some, :] for part in mine]
            for e in range(late, ch_count):
                at = (e - late) * some
                for c in range(own):
                    factor = jnp.where(jnp.bitwise_xor(place, e) == m, gate[c * early + at : c * early + at + some, :], 1.0)
                    rows[c] = rows[c] * factor
            out_ref[k * ch_count + m] = jnp.concatenate(rows, 0).astype(jnp.bfloat16)


def convolve(got, tables, own, near, ch_count):
    parts = len(got)
    blocks = parts * near
    owners = parts * ch_count
    return pl.pallas_call(
        functools.partial(conv_kernel, own, near, ch_count, parts),
        out_shape=jax.ShapeDtypeStruct((owners, own * blocks // owners, W), jnp.bfloat16),
        in_specs=[whole_vmem()] * (parts + len(tables)),
        out_specs=whole_vmem(),
        scratch_shapes=[
            pltpu.VMEM((blocks, W * (own + 1)), jnp.bfloat16),
            pltpu.VMEM((2 * blocks, W * own), jnp.bfloat16),
            pltpu.VMEM((own, blocks, W), jnp.float32),
        ],
        compiler_params=pltpu.CompilerParams(vmem_limit_bytes=32 * 2**20),
        cost_estimate=pl.CostEstimate(flops=16000 * blocks * W, bytes_accessed=4 * blocks * W, transcendentals=0),
        name="convolve",
    )(*got, *tables)


def unpack_kernel(own, got_ref, *rest):
    gate_refs, (out_ref, flat, gate_s, stage, sems) = rest[:-5], rest[-5:]
    sources, rows, _ = got_ref.shape
    some = rows // own
    place = lax.axis_index("ch")
    channels, width = gate_refs[0].shape
    ch_count = out_ref.shape[0] // channels
    for d in range(ch_count):
        here = pl.ds(pl.multiple_of(jnp.bitwise_xor(place, d) * channels, TILE), channels)
        gate_s[here, :] = gate_refs[d][...] if d < len(gate_refs) else jnp.ones((channels, width), jnp.bfloat16)
    copies = []
    for m in range(ch_count):
        here = slice(m * channels, (m + 1) * channels)
        for k in range(sources // ch_count):
            part = got_ref[k * ch_count + m].astype(jnp.float32)
            first = m * channels * some + k * rows
            for h in range(W // LANES):
                flat[h, first : first + rows, :] = part[:, LANES * h : LANES * (h + 1)]
        for j in range(some):
            for h in range(W // LANES):
                part = flat[h, pl.ds(m * channels * some + j, channels, stride=some), :]
                first = W * j + LANES * h
                cols = slice(first, first + LANES)
                stage[here, cols] = (part * gate_s[here, cols].astype(jnp.float32)).astype(jnp.bfloat16)
        copies.append(pltpu.make_async_copy(stage.at[here], out_ref.at[here], sems.at[m]))
        copies[m].start()
    for copy in copies:
        copy.wait()


def unpack(got, gates, own, ch_count):
    sources, rows, _ = got.shape
    shape = (sources * own, rows // own * W)
    if rows % TILE:
        ones = [jnp.ones_like(gates[0])] * (ch_count - len(gates))
        order = jnp.bitwise_xor(lax.axis_index("ch"), jnp.arange(ch_count))
        gate = jnp.stack(gates + ones)[order].reshape(shape)
        got = got.reshape(-1, ch_count, rows, W).swapaxes(0, 1)
        return (got.reshape(shape).astype(jnp.float32) * gate.astype(jnp.float32)).astype(jnp.bfloat16)
    return pl.pallas_call(
        functools.partial(unpack_kernel, own),
        out_shape=jax.ShapeDtypeStruct(shape, jnp.bfloat16),
        in_specs=[whole_vmem()] * (1 + len(gates)),
        out_specs=in_hbm(),
        scratch_shapes=[
            pltpu.VMEM((W // LANES, sources * rows, LANES), jnp.float32),
            pltpu.VMEM(shape, jnp.bfloat16),
            pltpu.VMEM(shape, jnp.bfloat16),
            pltpu.SemaphoreType.DMA((ch_count,)),
        ],
        compiler_params=pltpu.CompilerParams(vmem_limit_bytes=24 * 2**20),
        name="unpack",
    )(got, *[pltpu.with_memory_space_constraint(gate, pltpu.VMEM) for gate in gates])


def body(pre_gate, value, post_gate, filter_taps, skip):
    ctx_count = lax.axis_size("ctx")
    ch_count = lax.axis_size("ch")
    own = value.shape[0] // ctx_count
    near = value.shape[1] // W
    got, gates = pack(pre_gate, value, post_gate, filter_taps, ctx_count, ch_count)
    order = partner_order(ctx_count)
    got = [got[d] for d in order]
    tables, skip, _ = lax.optimization_barrier((dft_tables(near * ctx_count), skip, got[0]))
    tables = list(make_tables(skip, *tables, own))
    half = ctx_count // 2 + 1
    tables, got[half:] = lax.optimization_barrier((tables, got[half:]))
    got = [swap(piece, "ctx", ctx_count, d) if d else piece for piece, d in zip(got, order)]
    for d in range(1, len(gates)):
        gates[d] = swap(gates[d], "ch", ch_count, d)
    got[1:], gates[2:] = lax.optimization_barrier((got[1:], gates[2:]))
    mixed = convolve(got, tables, own, near, ch_count)
    mixed, gates = lax.optimization_barrier((mixed, gates[::-1]))
    gates = gates[::-1]
    mixed = lax.all_to_all(mixed, ("ctx", "ch"), split_axis=0, concat_axis=0, tiled=True)
    return unpack(mixed, gates, own, ch_count)


def solution(mesh):
    placed = (P("ch", "ctx"), P("ch", "ctx"), P("ch", "ctx"), P("ch", "ctx"), P("ch"))
    return jax.shard_map(
        body, mesh=mesh, in_specs=placed, out_specs=P(None, ("ctx", "ch")), check_vma=False
    )
```

```python
import functools
import math

import jax
import jax.numpy as jnp
import numpy as np
from jax import lax
from jax.experimental import pallas as pl
from jax.experimental.pallas import tpu as pltpu
from jax.sharding import PartitionSpec as P

W = 256
LANES = 128
TILE = 16
CHUNK = 256


def whole_vmem():
    return pl.BlockSpec(memory_space=pltpu.VMEM)


def in_hbm():
    return pl.BlockSpec(memory_space=pltpu.HBM)


def dft_tables(blocks):
    length = blocks * W
    k = np.arange(blocks)[:, None]
    angle = 2 * np.pi * ((4 * k + 1) * np.arange(blocks)[None, :] % (4 * blocks)) / (4 * blocks)
    outer = np.concatenate([np.cos(angle), -np.sin(angle)], 0)
    turn = 2 * np.pi * ((4 * k + 1) * np.arange(W)[None, :]) / (4 * length)
    near = 2 * np.pi * (np.arange(W)[:, None] * np.arange(W)[None, :] % W) / W
    inner = np.concatenate([np.cos(near), np.sin(near)], 0)
    turns = np.concatenate([np.cos(turn), np.sin(turn)], 1)
    return [jnp.asarray(table, jnp.float32) for table in (outer, inner, turns)]


def lay(natural, j, value):
    count = value.shape[0]
    for h in range(W // LANES):
        first = (j * (W // LANES) + h) * count
        natural[first : first + count, :] = value[:, LANES * h : LANES * (h + 1)]


def pick(natural, channel, count, blocks):
    halves = W // LANES
    rows = [natural[pl.ds(h * count + channel, blocks, stride=halves * count), :] for h in range(halves)]
    return jnp.concatenate(rows, 1)


def late_pieces(own, piece, ch_count):
    early = max(1, ch_count // 4)
    if own * piece * early % TILE:
        early = ch_count // 2
    return ch_count - early


def pack_kernel(own, blocks, group, ch_count, parts, pre_ref, val_ref, taps_ref, post_ref, *rest):
    piece = blocks // ch_count
    late = late_pieces(own, piece, ch_count)
    out_refs, gate_refs = rest[:parts], rest[parts : parts + late]
    pre_s, val_s, taps_s, post_s, natural, natural_taps, natural_gate, stage, in_sems = rest[parts + late :]
    channels = own * parts
    some = min(TILE, channels)
    rows = own * blocks
    main = rows + blocks
    loads = []
    for g in range(channels // some):
        here = pl.ds(g * some, some)
        loads.append(pltpu.make_async_copy(pre_ref.at[here], pre_s.at[here], in_sems.at[g, 0]))
        loads.append(pltpu.make_async_copy(val_ref.at[here], val_s.at[here], in_sems.at[g, 1]))
    taps_load = pltpu.make_async_copy(taps_ref, taps_s, in_sems.at[channels // some, 0])
    gate_load = pltpu.make_async_copy(post_ref, post_s, in_sems.at[channels // some, 1])
    for copy in loads[:2] + [taps_load] + loads[2:] + [gate_load]:
        copy.start()
    groups = taps_s.shape[0]
    taps_load.wait()
    for j in range(blocks):
        lay(natural_taps, j, taps_s[:, W * j : W * (j + 1)])
    for g in range(channels // some):
        loads[2 * g].wait()
        loads[2 * g + 1].wait()
        here = slice(g * some, (g + 1) * some)
        for j in range(blocks):
            cols = slice(W * j, W * (j + 1))
            product = pre_s[here, cols].astype(jnp.float32) * val_s[here, cols].astype(jnp.float32)
            lay(natural.at[g], j, product)
        for i in range(g * some // own, (g + 1) * some // own):
            for c in range(own):
                mine = pick(natural.at[g], own * i + c - g * some, some, blocks)
                stage[i, blocks * c : blocks * (c + 1), :] = mine.astype(jnp.bfloat16)
            taps = pick(natural_taps, own * i // group, groups, blocks)
            stage[i, rows:main, :] = taps.astype(jnp.bfloat16)
    gate_load.wait()
    place = lax.axis_index("ch")
    for d in range(ch_count):
        first = jnp.bitwise_xor(place, d) * (piece * W)
        if d < late:
            gate_refs[d][...] = post_s[:, pl.ds(pl.multiple_of(first, LANES), piece * W)]
        else:
            for j in range(piece):
                cols = pl.ds(pl.multiple_of(first + W * j, LANES), W)
                lay(natural_gate, (d - late) * piece + j, post_s[:, cols].astype(jnp.float32))
    early = piece * (ch_count - late)
    for i in range(parts):
        gate = [pick(natural_gate, own * i + c, channels, early) for c in range(own)]
        stage[i, main:, :] = jnp.concatenate(gate, 0).astype(jnp.bfloat16)
    me = lax.axis_index("ctx")
    for d in range(parts):
        out_refs[d][...] = stage[jnp.bitwise_xor(me, d)]


def pack(pre_gate, value, post_gate, taps, parts, ch_count):
    channels, block = value.shape
    own = channels // parts
    group = channels // taps.shape[0]
    blocks = block // W
    piece = blocks // ch_count
    late = late_pieces(own, piece, ch_count)
    early = piece * (ch_count - late)
    local = (own + 1) * blocks + own * early
    halves = W // LANES
    some = min(TILE, channels)
    args = [pltpu.with_memory_space_constraint(arg, pltpu.HBM) for arg in (pre_gate, value, taps, post_gate)]
    out = pl.pallas_call(
        functools.partial(pack_kernel, own, blocks, group, ch_count, parts),
        out_shape=[jax.ShapeDtypeStruct((local, W), jnp.bfloat16)] * parts
        + [jax.ShapeDtypeStruct((channels, piece * W), jnp.bfloat16)] * late,
        in_specs=[in_hbm()] * 4,
        out_specs=[whole_vmem()] * (parts + late),
        scratch_shapes=[
            pltpu.VMEM(pre_gate.shape, jnp.bfloat16),
            pltpu.VMEM(value.shape, jnp.bfloat16),
            pltpu.VMEM(taps.shape, jnp.float32),
            pltpu.VMEM(post_gate.shape, jnp.bfloat16),
            pltpu.VMEM((channels // some, blocks * halves * some, LANES), jnp.float32),
            pltpu.VMEM((blocks * halves * taps.shape[0], LANES), jnp.float32),
            pltpu.VMEM((early * halves * channels, LANES), jnp.float32),
            pltpu.VMEM((parts, local, W), jnp.bfloat16),
            pltpu.SemaphoreType.DMA((channels // some + 1, 2)),
        ],
        compiler_params=pltpu.CompilerParams(vmem_limit_bytes=16 * 2**20),
        name="pack",
    )(*args)
    return list(out[:parts]), list(out[parts:])


def partner_order(count):
    corners = [d for d in range(1, count) if bin(d >> 1).count("1") > 1]
    straight = [d for d in range(2, count, 2) if d not in corners]
    order = [0] + corners[:1] + straight + corners[1:]
    return order + [d for d in range(2, count) if d not in order] + [1]


def swap(piece, axis, count, d):
    return lax.ppermute(piece, axis, [(i, i ^ d) for i in range(count)])


def tables_kernel(own, skip_ref, outer_ref, inner_ref, turns_ref, outer_out, back_out, ahead, rear, turns_out, *rest):
    outer_s, inner_s, sems = rest
    count, width = turns_ref.shape
    loads = [
        pltpu.make_async_copy(outer_ref, outer_s, sems.at[0]),
        pltpu.make_async_copy(inner_ref, inner_s, sems.at[1]),
        pltpu.make_async_copy(turns_ref, turns_out.at[0:count, :], sems.at[2]),
    ]
    for copy in loads:
        copy.start()
    me = lax.axis_index("ctx")
    for c in range(own):
        turns_out[count + 8 * c : count + 8 * (c + 1), :] = jnp.full((8, width), skip_ref[own * me + c], jnp.float32)
    loads[0].wait()
    outer_out[...] = outer_s[...].astype(jnp.bfloat16)
    back_out[...] = outer_s[...].T.astype(jnp.bfloat16)
    loads[1].wait()
    near_cos, near_sin = inner_s[0:W, :].astype(jnp.bfloat16), inner_s[W:, :].astype(jnp.bfloat16)
    for table, sign in ((ahead, -1), (rear, 1)):
        table[0:W, 0:W] = near_cos
        table[0:W, W:] = near_sin * sign
        table[W:, 0:W] = near_sin * -sign
        table[W:, W:] = near_cos
    loads[2].wait()


def make_tables(skip, outer, inner, turns, own):
    count, width = turns.shape
    args = [pltpu.with_memory_space_constraint(arg, pltpu.HBM) for arg in (outer, inner, turns)]
    narrow = (outer.shape, outer.shape[::-1], (2 * W, 2 * W), (2 * W, 2 * W))
    return pl.pallas_call(
        functools.partial(tables_kernel, own),
        out_shape=[jax.ShapeDtypeStruct(shape, jnp.bfloat16) for shape in narrow]
        + [jax.ShapeDtypeStruct((count + 8 * own, width), jnp.float32)],
        in_specs=[pl.BlockSpec(memory_space=pltpu.SMEM)] + [in_hbm()] * 3,
        out_specs=[whole_vmem()] * 5,
        scratch_shapes=[
            pltpu.VMEM(outer.shape, jnp.float32),
            pltpu.VMEM(inner.shape, jnp.float32),
            pltpu.SemaphoreType.DMA((3,)),
        ],
        compiler_params=pltpu.CompilerParams(vmem_limit_bytes=16 * 2**20),
        name="make_tables",
    )(skip, *args)


def conv_kernel(own, near, ch_count, parts, *rest):
    got_refs = rest[:parts]
    outer_ref, back_ref, ahead, rear, turns_ref, out_ref, x_all, r_all, z_all = rest[parts:]
    blocks = parts * near
    length = blocks * W
    chunk = math.gcd(blocks, CHUNK)
    me = lax.axis_index("ctx")
    order = partner_order(parts)
    for d, got_ref in zip(order, got_refs):
        here = pl.ds(pl.multiple_of(jnp.bitwise_xor(me, d) * near, TILE), near)
        for c in range(own + 1):
            x_all[here, W * c : W * (c + 1)] = got_ref[c * near : (c + 1) * near, :]

    def dot(left, right):
        return jnp.dot(left, right, preferred_element_type=jnp.float32)

    for first in range(0, blocks, chunk):
        here = slice(first, first + chunk)
        there = slice(blocks + first, blocks + first + chunk)
        both = dot(jnp.concatenate([outer_ref[here, :], outer_ref[there, :]], 0), x_all[...])
        real, imag = both[0:chunk, :], both[chunk:, :]
        turn_cos, turn_sin = turns_ref[here, 0:W], turns_ref[here, W:]
        rows = []
        for c in range(own + 1):
            re, im = real[:, W * c : W * (c + 1)], imag[:, W * c : W * (c + 1)]
            pair = [re * turn_cos + im * turn_sin, im * turn_cos - re * turn_sin]
            rows.append(jnp.concatenate(pair, 1).astype(jnp.bfloat16))
        spectrum = dot(jnp.concatenate(rows, 0), ahead[...])
        filt_re = spectrum[chunk * own :, 0:W] * (1.0 / length)
        filt_im = spectrum[chunk * own :, W:] * (1.0 / length)
        rows = []
        for c in range(own):
            part = spectrum[chunk * c : chunk * (c + 1), :]
            re, im = part[:, 0:W], part[:, W:]
            pair = [re * filt_re - im * filt_im, re * filt_im + im * filt_re]
            rows.append(jnp.concatenate(pair, 1).astype(jnp.bfloat16))
        middle = dot(jnp.concatenate(rows, 0), rear[...])
        for c in range(own):
            part = middle[chunk * c : chunk * (c + 1), :]
            re, im = part[:, 0:W], part[:, W:]
            cols = slice(W * c, W * (c + 1))
            r_all[here, cols] = (re * turn_cos - im * turn_sin).astype(jnp.bfloat16)
            r_all[there, cols] = (re * turn_sin + im * turn_cos).astype(jnp.bfloat16)

    conv = dot(back_ref[...], r_all[...])
    for c in range(own):
        cols = slice(W * c, W * (c + 1))
        z_all[c] = conv[:, cols] + turns_ref[blocks + 8 * c : blocks + 8 * c + 1, 0:W] * x_all[:, cols].astype(jnp.float32)
    some = out_ref.shape[1] // own
    late = late_pieces(own, some, ch_count)
    early = some * (ch_count - late)
    place = lax.axis_index("ch")
    for d, got_ref in zip(order, got_refs):
        k = jnp.bitwise_xor(me, d)
        gate = got_ref[(own + 1) * near :, :].astype(jnp.float32)
        mine = [z_all[c, pl.ds(pl.multiple_of(k * near, TILE), near), :] for c in range(own)]
        for m in range(ch_count):
            rows = [part[m * some : (m + 1) * some, :] for part in mine]
            for e in range(late, ch_count):
                at = (e - late) * some
                for c in range(own):
                    factor = jnp.where(jnp.bitwise_xor(place, e) == m, gate[c * early + at : c * early + at + some, :], 1.0)
                    rows[c] = rows[c] * factor
            out_ref[k * ch_count + m] = jnp.concatenate(rows, 0).astype(jnp.bfloat16)


def convolve(got, tables, own, near, ch_count):
    parts = len(got)
    blocks = parts * near
    owners = parts * ch_count
    return pl.pallas_call(
        functools.partial(conv_kernel, own, near, ch_count, parts),
        out_shape=jax.ShapeDtypeStruct((owners, own * blocks // owners, W), jnp.bfloat16),
        in_specs=[whole_vmem()] * (parts + len(tables)),
        out_specs=whole_vmem(),
        scratch_shapes=[
            pltpu.VMEM((blocks, W * (own + 1)), jnp.bfloat16),
            pltpu.VMEM((2 * blocks, W * own), jnp.bfloat16),
            pltpu.VMEM((own, blocks, W), jnp.float32),
        ],
        compiler_params=pltpu.CompilerParams(vmem_limit_bytes=32 * 2**20),
        cost_estimate=pl.CostEstimate(flops=16000 * blocks * W, bytes_accessed=4 * blocks * W, transcendentals=0),
        name="convolve",
    )(*got, *tables)


def unpack_kernel(own, got_ref, *rest):
    gate_refs, (out_ref, flat, gate_s, stage, sems) = rest[:-5], rest[-5:]
    sources, rows, _ = got_ref.shape
    some = rows // own
    place = lax.axis_index("ch")
    channels, width = gate_refs[0].shape
    ch_count = out_ref.shape[0] // channels
    for d in range(ch_count):
        here = pl.ds(pl.multiple_of(jnp.bitwise_xor(place, d) * channels, TILE), channels)
        gate_s[here, :] = gate_refs[d][...] if d < len(gate_refs) else jnp.ones((channels, width), jnp.bfloat16)
    copies = []
    for m in range(ch_count):
        here = slice(m * channels, (m + 1) * channels)
        for k in range(sources // ch_count):
            part = got_ref[k * ch_count + m].astype(jnp.float32)
            first = m * channels * some + k * rows
            for h in range(W // LANES):
                flat[h, first : first + rows, :] = part[:, LANES * h : LANES * (h + 1)]
        for j in range(some):
            for h in range(W // LANES):
                part = flat[h, pl.ds(m * channels * some + j, channels, stride=some), :]
                first = W * j + LANES * h
                cols = slice(first, first + LANES)
                stage[here, cols] = (part * gate_s[here, cols].astype(jnp.float32)).astype(jnp.bfloat16)
        copies.append(pltpu.make_async_copy(stage.at[here], out_ref.at[here], sems.at[m]))
        copies[m].start()
    for copy in copies:
        copy.wait()


def unpack(got, gates, own, ch_count):
    sources, rows, _ = got.shape
    shape = (sources * own, rows // own * W)
    if rows % TILE:
        ones = [jnp.ones_like(gates[0])] * (ch_count - len(gates))
        order = jnp.bitwise_xor(lax.axis_index("ch"), jnp.arange(ch_count))
        gate = jnp.stack(gates + ones)[order].reshape(shape)
        got = got.reshape(-1, ch_count, rows, W).swapaxes(0, 1)
        return (got.reshape(shape).astype(jnp.float32) * gate.astype(jnp.float32)).astype(jnp.bfloat16)
    return pl.pallas_call(
        functools.partial(unpack_kernel, own),
        out_shape=jax.ShapeDtypeStruct(shape, jnp.bfloat16),
        in_specs=[whole_vmem()] * (1 + len(gates)),
        out_specs=in_hbm(),
        scratch_shapes=[
            pltpu.VMEM((W // LANES, sources * rows, LANES), jnp.float32),
            pltpu.VMEM(shape, jnp.bfloat16),
            pltpu.VMEM(shape, jnp.bfloat16),
            pltpu.SemaphoreType.DMA((ch_count,)),
        ],
        compiler_params=pltpu.CompilerParams(vmem_limit_bytes=24 * 2**20),
        name="unpack",
    )(got, *[pltpu.with_memory_space_constraint(gate, pltpu.VMEM) for gate in gates])


def body(pre_gate, value, post_gate, filter_taps, skip):
    ctx_count = lax.axis_size("ctx")
    ch_count = lax.axis_size("ch")
    own = value.shape[0] // ctx_count
    near = value.shape[1] // W
    got, gates = pack(pre_gate, value, post_gate, filter_taps, ctx_count, ch_count)
    order = partner_order(ctx_count)
    got = [got[d] for d in order]
    tables, skip, _ = lax.optimization_barrier((dft_tables(near * ctx_count), skip, got[0]))
    tables = list(make_tables(skip, *tables, own))
    got = [swap(piece, "ctx", ctx_count, d) if d else piece for piece, d in zip(got, order)]
    for d in range(1, len(gates)):
        gates[d] = swap(gates[d], "ch", ch_count, d)
    got[1:], gates[2:] = lax.optimization_barrier((got[1:], gates[2:]))
    mixed = convolve(got, tables, own, near, ch_count)
    mixed, gates = lax.optimization_barrier((mixed, gates[::-1]))
    gates = gates[::-1]
    mixed = lax.all_to_all(mixed, ("ctx", "ch"), split_axis=0, concat_axis=0, tiled=True)
    return unpack(mixed, gates, own, ch_count)


def solution(mesh):
    placed = (P("ch", "ctx"), P("ch", "ctx"), P("ch", "ctx"), P("ch", "ctx"), P("ch"))
    return jax.shard_map(
        body, mesh=mesh, in_specs=placed, out_specs=P(None, ("ctx", "ch")), check_vma=False
    )
```

```python
import functools
import math

import jax
import jax.numpy as jnp
import numpy as np
from jax import lax
from jax.experimental import pallas as pl
from jax.experimental.pallas import tpu as pltpu
from jax.sharding import PartitionSpec as P

W = 256
LANES = 128
TILE = 16
CHUNK = 256


def whole_vmem():
    return pl.BlockSpec(memory_space=pltpu.VMEM)


def in_hbm():
    return pl.BlockSpec(memory_space=pltpu.HBM)


def dft_tables(blocks):
    length = blocks * W
    k = np.arange(blocks)[:, None]
    angle = 2 * np.pi * ((4 * k + 1) * np.arange(blocks)[None, :] % (4 * blocks)) / (4 * blocks)
    outer = np.concatenate([np.cos(angle), -np.sin(angle)], 0)
    turn = 2 * np.pi * ((4 * k + 1) * np.arange(W)[None, :]) / (4 * length)
    near = 2 * np.pi * (np.arange(W)[:, None] * np.arange(W)[None, :] % W) / W
    inner = np.concatenate([np.cos(near), np.sin(near)], 0)
    turns = np.concatenate([np.cos(turn), np.sin(turn)], 1)
    return [jnp.asarray(table, jnp.float32) for table in (outer, inner, turns)]


def lay(natural, j, value):
    count = value.shape[0]
    for h in range(W // LANES):
        first = (j * (W // LANES) + h) * count
        natural[first : first + count, :] = value[:, LANES * h : LANES * (h + 1)]


def pick(natural, channel, count, blocks):
    halves = W // LANES
    rows = [natural[pl.ds(h * count + channel, blocks, stride=halves * count), :] for h in range(halves)]
    return jnp.concatenate(rows, 1)


def late_pieces(own, piece, ch_count):
    early = max(1, ch_count // 4)
    if own * piece * early % TILE:
        early = ch_count // 2
    return ch_count - early


def pack_kernel(own, blocks, group, ch_count, parts, pre_ref, val_ref, taps_ref, post_ref, *rest):
    piece = blocks // ch_count
    late = late_pieces(own, piece, ch_count)
    out_refs, gate_refs = rest[:parts], rest[parts : parts + late]
    pre_s, val_s, taps_s, post_s, natural, natural_taps, natural_gate, stage, in_sems = rest[parts + late :]
    channels = own * parts
    some = min(TILE, channels)
    rows = own * blocks
    main = rows + blocks
    loads = []
    for g in range(channels // some):
        here = pl.ds(g * some, some)
        loads.append(pltpu.make_async_copy(pre_ref.at[here], pre_s.at[here], in_sems.at[g, 0]))
        loads.append(pltpu.make_async_copy(val_ref.at[here], val_s.at[here], in_sems.at[g, 1]))
    taps_load = pltpu.make_async_copy(taps_ref, taps_s, in_sems.at[channels // some, 0])
    gate_load = pltpu.make_async_copy(post_ref, post_s, in_sems.at[channels // some, 1])
    for copy in loads[:2] + [taps_load] + loads[2:] + [gate_load]:
        copy.start()
    groups = taps_s.shape[0]
    taps_load.wait()
    for j in range(blocks):
        lay(natural_taps, j, taps_s[:, W * j : W * (j + 1)])
    for g in range(channels // some):
        loads[2 * g].wait()
        loads[2 * g + 1].wait()
        here = slice(g * some, (g + 1) * some)
        for j in range(blocks):
            cols = slice(W * j, W * (j + 1))
            product = pre_s[here, cols].astype(jnp.float32) * val_s[here, cols].astype(jnp.float32)
            lay(natural.at[g], j, product)
        for i in range(g * some // own, (g + 1) * some // own):
            for c in range(own):
                mine = pick(natural.at[g], own * i + c - g * some, some, blocks)
                stage[i, blocks * c : blocks * (c + 1), :] = mine.astype(jnp.bfloat16)
            taps = pick(natural_taps, own * i // group, groups, blocks)
            stage[i, rows:main, :] = taps.astype(jnp.bfloat16)
    gate_load.wait()
    place = lax.axis_index("ch")
    for d in range(ch_count):
        first = jnp.bitwise_xor(place, d) * (piece * W)
        if d < late:
            gate_refs[d][...] = post_s[:, pl.ds(pl.multiple_of(first, LANES), piece * W)]
        else:
            for j in range(piece):
                cols = pl.ds(pl.multiple_of(first + W * j, LANES), W)
                lay(natural_gate, (d - late) * piece + j, post_s[:, cols].astype(jnp.float32))
    early = piece * (ch_count - late)
    for i in range(parts):
        gate = [pick(natural_gate, own * i + c, channels, early) for c in range(own)]
        stage[i, main:, :] = jnp.concatenate(gate, 0).astype(jnp.bfloat16)
    me = lax.axis_index("ctx")
    for d in range(parts):
        out_refs[d][...] = stage[jnp.bitwise_xor(me, d)]


def pack(pre_gate, value, post_gate, taps, parts, ch_count):
    channels, block = value.shape
    own = channels // parts
    group = channels // taps.shape[0]
    blocks = block // W
    piece = blocks // ch_count
    late = late_pieces(own, piece, ch_count)
    early = piece * (ch_count - late)
    local = (own + 1) * blocks + own * early
    halves = W // LANES
    some = min(TILE, channels)
    args = [pltpu.with_memory_space_constraint(arg, pltpu.HBM) for arg in (pre_gate, value, taps, post_gate)]
    out = pl.pallas_call(
        functools.partial(pack_kernel, own, blocks, group, ch_count, parts),
        out_shape=[jax.ShapeDtypeStruct((local, W), jnp.bfloat16)] * parts
        + [jax.ShapeDtypeStruct((channels, piece * W), jnp.bfloat16)] * late,
        in_specs=[in_hbm()] * 4,
        out_specs=[whole_vmem()] * (parts + late),
        scratch_shapes=[
            pltpu.VMEM(pre_gate.shape, jnp.bfloat16),
            pltpu.VMEM(value.shape, jnp.bfloat16),
            pltpu.VMEM(taps.shape, jnp.float32),
            pltpu.VMEM(post_gate.shape, jnp.bfloat16),
            pltpu.VMEM((channels // some, blocks * halves * some, LANES), jnp.float32),
            pltpu.VMEM((blocks * halves * taps.shape[0], LANES), jnp.float32),
            pltpu.VMEM((early * halves * channels, LANES), jnp.float32),
            pltpu.VMEM((parts, local, W), jnp.bfloat16),
            pltpu.SemaphoreType.DMA((channels // some + 1, 2)),
        ],
        compiler_params=pltpu.CompilerParams(vmem_limit_bytes=16 * 2**20),
        name="pack",
    )(*args)
    return list(out[:parts]), list(out[parts:])


def partner_order(count):
    corners = [d for d in range(1, count) if bin(d >> 1).count("1") > 1]
    straight = [d for d in range(2, count, 2) if d not in corners]
    order = [0] + corners[:1] + straight + corners[1:]
    return order + [d for d in range(2, count) if d not in order] + [1]


def swap(piece, axis, count, d):
    return lax.ppermute(piece, axis, [(i, i ^ d) for i in range(count)])


def tables_kernel(own, skip_ref, outer_ref, inner_ref, turns_ref, outer_out, back_out, ahead, rear, turns_out, *rest):
    outer_s, inner_s, skip_s, sems = rest
    count, width = turns_ref.shape
    loads = [
        pltpu.make_async_copy(outer_ref, outer_s, sems.at[0]),
        pltpu.make_async_copy(inner_ref, inner_s, sems.at[1]),
        pltpu.make_async_copy(turns_ref, turns_out.at[0:count, :], sems.at[2]),
        pltpu.make_async_copy(skip_ref, skip_s, sems.at[3]),
    ]
    for copy in loads[::-1]:
        copy.start()
    loads[3].wait()
    me = lax.axis_index("ctx")
    for c in range(own):
        turns_out[count + 8 * c : count + 8 * (c + 1), :] = jnp.full((8, width), skip_s[own * me + c], jnp.float32)
    loads[0].wait()
    outer_out[...] = outer_s[...].astype(jnp.bfloat16)
    back_out[...] = outer_s[...].T.astype(jnp.bfloat16)
    loads[1].wait()
    near_cos, near_sin = inner_s[0:W, :].astype(jnp.bfloat16), inner_s[W:, :].astype(jnp.bfloat16)
    for table, sign in ((ahead, -1), (rear, 1)):
        table[0:W, 0:W] = near_cos
        table[0:W, W:] = near_sin * sign
        table[W:, 0:W] = near_sin * -sign
        table[W:, W:] = near_cos
    loads[2].wait()


def make_tables(skip, outer, inner, turns, own):
    count, width = turns.shape
    args = [pltpu.with_memory_space_constraint(arg, pltpu.HBM) for arg in (skip, outer, inner, turns)]
    narrow = (outer.shape, outer.shape[::-1], (2 * W, 2 * W), (2 * W, 2 * W))
    return pl.pallas_call(
        functools.partial(tables_kernel, own),
        out_shape=[jax.ShapeDtypeStruct(shape, jnp.bfloat16) for shape in narrow]
        + [jax.ShapeDtypeStruct((count + 8 * own, width), jnp.float32)],
        in_specs=[in_hbm()] * 4,
        out_specs=[whole_vmem()] * 5,
        scratch_shapes=[
            pltpu.VMEM(outer.shape, jnp.float32),
            pltpu.VMEM(inner.shape, jnp.float32),
            pltpu.SMEM(skip.shape, jnp.float32),
            pltpu.SemaphoreType.DMA((4,)),
        ],
        compiler_params=pltpu.CompilerParams(vmem_limit_bytes=16 * 2**20),
        name="make_tables",
    )(*args)


def conv_kernel(own, near, ch_count, parts, *rest):
    got_refs = rest[:parts]
    outer_ref, back_ref, ahead, rear, turns_ref, out_ref, x_all, r_all, z_all = rest[parts:]
    blocks = parts * near
    length = blocks * W
    chunk = math.gcd(blocks, CHUNK)
    me = lax.axis_index("ctx")
    order = partner_order(parts)
    for d, got_ref in zip(order, got_refs):
        here = pl.ds(pl.multiple_of(jnp.bitwise_xor(me, d) * near, TILE), near)
        for c in range(own + 1):
            x_all[here, W * c : W * (c + 1)] = got_ref[c * near : (c + 1) * near, :]

    def dot(left, right):
        return jnp.dot(left, right, preferred_element_type=jnp.float32)

    for first in range(0, blocks, chunk):
        here = slice(first, first + chunk)
        there = slice(blocks + first, blocks + first + chunk)
        both = dot(jnp.concatenate([outer_ref[here, :], outer_ref[there, :]], 0), x_all[...])
        real, imag = both[0:chunk, :], both[chunk:, :]
        turn_cos, turn_sin = turns_ref[here, 0:W], turns_ref[here, W:]
        rows = []
        for c in range(own + 1):
            re, im = real[:, W * c : W * (c + 1)], imag[:, W * c : W * (c + 1)]
            pair = [re * turn_cos + im * turn_sin, im * turn_cos - re * turn_sin]
            rows.append(jnp.concatenate(pair, 1).astype(jnp.bfloat16))
        spectrum = dot(jnp.concatenate(rows, 0), ahead[...])
        filt_re = spectrum[chunk * own :, 0:W] * (1.0 / length)
        filt_im = spectrum[chunk * own :, W:] * (1.0 / length)
        rows = []
        for c in range(own):
            part = spectrum[chunk * c : chunk * (c + 1), :]
            re, im = part[:, 0:W], part[:, W:]
            pair = [re * filt_re - im * filt_im, re * filt_im + im * filt_re]
            rows.append(jnp.concatenate(pair, 1).astype(jnp.bfloat16))
        middle = dot(jnp.concatenate(rows, 0), rear[...])
        for c in range(own):
            part = middle[chunk * c : chunk * (c + 1), :]
            re, im = part[:, 0:W], part[:, W:]
            cols = slice(W * c, W * (c + 1))
            r_all[here, cols] = (re * turn_cos - im * turn_sin).astype(jnp.bfloat16)
            r_all[there, cols] = (re * turn_sin + im * turn_cos).astype(jnp.bfloat16)

    conv = dot(back_ref[...], r_all[...])
    for c in range(own):
        cols = slice(W * c, W * (c + 1))
        z_all[c] = conv[:, cols] + turns_ref[blocks + 8 * c : blocks + 8 * c + 1, 0:W] * x_all[:, cols].astype(jnp.float32)
    some = out_ref.shape[1] // own
    late = late_pieces(own, some, ch_count)
    early = some * (ch_count - late)
    place = lax.axis_index("ch")
    for d, got_ref in zip(order, got_refs):
        k = jnp.bitwise_xor(me, d)
        gate = got_ref[(own + 1) * near :, :].astype(jnp.float32)
        mine = [z_all[c, pl.ds(pl.multiple_of(k * near, TILE), near), :] for c in range(own)]
        for m in range(ch_count):
            rows = [part[m * some : (m + 1) * some, :] for part in mine]
            for e in range(late, ch_count):
                at = (e - late) * some
                for c in range(own):
                    factor = jnp.where(jnp.bitwise_xor(place, e) == m, gate[c * early + at : c * early + at + some, :], 1.0)
                    rows[c] = rows[c] * factor
            out_ref[k * ch_count + m] = jnp.concatenate(rows, 0).astype(jnp.bfloat16)


def convolve(got, tables, own, near, ch_count):
    parts = len(got)
    blocks = parts * near
    owners = parts * ch_count
    return pl.pallas_call(
        functools.partial(conv_kernel, own, near, ch_count, parts),
        out_shape=jax.ShapeDtypeStruct((owners, own * blocks // owners, W), jnp.bfloat16),
        in_specs=[whole_vmem()] * (parts + len(tables)),
        out_specs=whole_vmem(),
        scratch_shapes=[
            pltpu.VMEM((blocks, W * (own + 1)), jnp.bfloat16),
            pltpu.VMEM((2 * blocks, W * own), jnp.bfloat16),
            pltpu.VMEM((own, blocks, W), jnp.float32),
        ],
        compiler_params=pltpu.CompilerParams(vmem_limit_bytes=32 * 2**20),
        cost_estimate=pl.CostEstimate(flops=16000 * blocks * W, bytes_accessed=4 * blocks * W, transcendentals=0),
        name="convolve",
    )(*got, *tables)


def unpack_kernel(own, got_ref, *rest):
    gate_refs, (out_ref, flat, gate_s, stage, sems) = rest[:-5], rest[-5:]
    sources, rows, _ = got_ref.shape
    some = rows // own
    place = lax.axis_index("ch")
    channels, width = gate_refs[0].shape
    ch_count = out_ref.shape[0] // channels
    for d in range(ch_count):
        here = pl.ds(pl.multiple_of(jnp.bitwise_xor(place, d) * channels, TILE), channels)
        gate_s[here, :] = gate_refs[d][...] if d < len(gate_refs) else jnp.ones((channels, width), jnp.bfloat16)
    copies = []
    for m in range(ch_count):
        here = slice(m * channels, (m + 1) * channels)
        for k in range(sources // ch_count):
            part = got_ref[k * ch_count + m].astype(jnp.float32)
            first = m * channels * some + k * rows
            for h in range(W // LANES):
                flat[h, first : first + rows, :] = part[:, LANES * h : LANES * (h + 1)]
        for j in range(some):
            for h in range(W // LANES):
                part = flat[h, pl.ds(m * channels * some + j, channels, stride=some), :]
                first = W * j + LANES * h
                cols = slice(first, first + LANES)
                stage[here, cols] = (part * gate_s[here, cols].astype(jnp.float32)).astype(jnp.bfloat16)
        copies.append(pltpu.make_async_copy(stage.at[here], out_ref.at[here], sems.at[m]))
        copies[m].start()
    for copy in copies:
        copy.wait()


def unpack(got, gates, own, ch_count):
    sources, rows, _ = got.shape
    shape = (sources * own, rows // own * W)
    if rows % TILE:
        ones = [jnp.ones_like(gates[0])] * (ch_count - len(gates))
        order = jnp.bitwise_xor(lax.axis_index("ch"), jnp.arange(ch_count))
        gate = jnp.stack(gates + ones)[order].reshape(shape)
        got = got.reshape(-1, ch_count, rows, W).swapaxes(0, 1)
        return (got.reshape(shape).astype(jnp.float32) * gate.astype(jnp.float32)).astype(jnp.bfloat16)
    return pl.pallas_call(
        functools.partial(unpack_kernel, own),
        out_shape=jax.ShapeDtypeStruct(shape, jnp.bfloat16),
        in_specs=[whole_vmem()] * (1 + len(gates)),
        out_specs=in_hbm(),
        scratch_shapes=[
            pltpu.VMEM((W // LANES, sources * rows, LANES), jnp.float32),
            pltpu.VMEM(shape, jnp.bfloat16),
            pltpu.VMEM(shape, jnp.bfloat16),
            pltpu.SemaphoreType.DMA((ch_count,)),
        ],
        compiler_params=pltpu.CompilerParams(vmem_limit_bytes=24 * 2**20),
        name="unpack",
    )(got, *[pltpu.with_memory_space_constraint(gate, pltpu.VMEM) for gate in gates])


def body(pre_gate, value, post_gate, filter_taps, skip):
    ctx_count = lax.axis_size("ctx")
    ch_count = lax.axis_size("ch")
    own = value.shape[0] // ctx_count
    near = value.shape[1] // W
    got, gates = pack(pre_gate, value, post_gate, filter_taps, ctx_count, ch_count)
    order = partner_order(ctx_count)
    got = [got[d] for d in order]
    tables, skip, _ = lax.optimization_barrier((dft_tables(near * ctx_count), skip, got[0]))
    tables = list(make_tables(skip, *tables, own))
    got = [swap(piece, "ctx", ctx_count, d) if d else piece for piece, d in zip(got, order)]
    for d in range(1, len(gates)):
        gates[d] = swap(gates[d], "ch", ch_count, d)
    got[1:], gates[2:] = lax.optimization_barrier((got[1:], gates[2:]))
    mixed = convolve(got, tables, own, near, ch_count)
    mixed, gates = lax.optimization_barrier((mixed, gates[::-1]))
    gates = gates[::-1]
    mixed = lax.all_to_all(mixed, ("ctx", "ch"), split_axis=0, concat_axis=0, tiled=True)
    return unpack(mixed, gates, own, ch_count)


def solution(mesh):
    placed = (P("ch", "ctx"), P("ch", "ctx"), P("ch", "ctx"), P("ch", "ctx"), P("ch"))
    return jax.shard_map(
        body, mesh=mesh, in_specs=placed, out_specs=P(None, ("ctx", "ch")), check_vma=False
    )
```

```python
import functools
import math

import jax
import jax.numpy as jnp
import numpy as np
from jax import lax
from jax.experimental import pallas as pl
from jax.experimental.pallas import tpu as pltpu
from jax.sharding import PartitionSpec as P

W = 256
LANES = 128
TILE = 16
CHUNK = 256


def whole_vmem():
    return pl.BlockSpec(memory_space=pltpu.VMEM)


def in_hbm():
    return pl.BlockSpec(memory_space=pltpu.HBM)


def dft_tables(blocks):
    length = blocks * W
    k = np.arange(blocks)[:, None]
    angle = 2 * np.pi * ((4 * k + 1) * np.arange(blocks)[None, :] % (4 * blocks)) / (4 * blocks)
    outer = np.concatenate([np.cos(angle), -np.sin(angle)], 0)
    turn = 2 * np.pi * ((4 * k + 1) * np.arange(W)[None, :]) / (4 * length)
    near = 2 * np.pi * (np.arange(W)[:, None] * np.arange(W)[None, :] % W) / W
    inner = np.concatenate([np.cos(near), np.sin(near)], 0)
    turns = np.concatenate([np.cos(turn), np.sin(turn)], 1)
    return [jnp.asarray(table, jnp.float32) for table in (outer, inner, turns)]


def lay(natural, j, value):
    count = value.shape[0]
    for h in range(W // LANES):
        first = (j * (W // LANES) + h) * count
        natural[first : first + count, :] = value[:, LANES * h : LANES * (h + 1)]


def pick(natural, channel, count, blocks):
    halves = W // LANES
    rows = [natural[pl.ds(h * count + channel, blocks, stride=halves * count), :] for h in range(halves)]
    return jnp.concatenate(rows, 1)


def late_pieces(own, piece, ch_count):
    early = max(1, ch_count // 4)
    if own * piece * early % TILE:
        early = ch_count // 2
    return ch_count - early


def pack_kernel(own, blocks, group, ch_count, parts, pre_ref, val_ref, taps_ref, post_ref, *rest):
    piece = blocks // ch_count
    late = late_pieces(own, piece, ch_count)
    out_refs, gate_refs = rest[:parts], rest[parts : parts + late]
    pre_s, val_s, taps_s, post_s, natural, natural_taps, natural_gate, stage, in_sems = rest[parts + late :]
    channels = own * parts
    some = min(TILE, channels)
    rows = own * blocks
    main = rows + blocks
    loads = []
    for g in range(channels // some):
        here = pl.ds(g * some, some)
        loads.append(pltpu.make_async_copy(pre_ref.at[here], pre_s.at[here], in_sems.at[g, 0]))
        loads.append(pltpu.make_async_copy(val_ref.at[here], val_s.at[here], in_sems.at[g, 1]))
    taps_load = pltpu.make_async_copy(taps_ref, taps_s, in_sems.at[channels // some, 0])
    gate_load = pltpu.make_async_copy(post_ref, post_s, in_sems.at[channels // some, 1])
    for copy in loads[:2] + [taps_load] + loads[2:] + [gate_load]:
        copy.start()
    groups = taps_s.shape[0]
    taps_load.wait()
    for j in range(blocks):
        lay(natural_taps, j, taps_s[:, W * j : W * (j + 1)])
    for g in range(channels // some):
        loads[2 * g].wait()
        loads[2 * g + 1].wait()
        here = slice(g * some, (g + 1) * some)
        for j in range(blocks):
            cols = slice(W * j, W * (j + 1))
            product = pre_s[here, cols].astype(jnp.float32) * val_s[here, cols].astype(jnp.float32)
            lay(natural.at[g], j, product)
        for i in range(g * some // own, (g + 1) * some // own):
            for c in range(own):
                mine = pick(natural.at[g], own * i + c - g * some, some, blocks)
                stage[i, blocks * c : blocks * (c + 1), :] = mine.astype(jnp.bfloat16)
            taps = pick(natural_taps, own * i // group, groups, blocks)
            stage[i, rows:main, :] = taps.astype(jnp.bfloat16)
    gate_load.wait()
    place = lax.axis_index("ch")
    for d in range(ch_count):
        first = jnp.bitwise_xor(place, d) * (piece * W)
        if d < late:
            gate_refs[d][...] = post_s[:, pl.ds(pl.multiple_of(first, LANES), piece * W)]
        else:
            for j in range(piece):
                cols = pl.ds(pl.multiple_of(first + W * j, LANES), W)
                lay(natural_gate, (d - late) * piece + j, post_s[:, cols].astype(jnp.float32))
    early = piece * (ch_count - late)
    for i in range(parts):
        gate = [pick(natural_gate, own * i + c, channels, early) for c in range(own)]
        stage[i, main:, :] = jnp.concatenate(gate, 0).astype(jnp.bfloat16)
    me = lax.axis_index("ctx")
    for d in range(parts):
        out_refs[d][...] = stage[jnp.bitwise_xor(me, d)]


def pack(pre_gate, value, post_gate, taps, parts, ch_count):
    channels, block = value.shape
    own = channels // parts
    group = channels // taps.shape[0]
    blocks = block // W
    piece = blocks // ch_count
    late = late_pieces(own, piece, ch_count)
    early = piece * (ch_count - late)
    local = (own + 1) * blocks + own * early
    halves = W // LANES
    some = min(TILE, channels)
    args = [pltpu.with_memory_space_constraint(arg, pltpu.HBM) for arg in (pre_gate, value, taps, post_gate)]
    out = pl.pallas_call(
        functools.partial(pack_kernel, own, blocks, group, ch_count, parts),
        out_shape=[jax.ShapeDtypeStruct((local, W), jnp.bfloat16)] * parts
        + [jax.ShapeDtypeStruct((channels, piece * W), jnp.bfloat16)] * late,
        in_specs=[in_hbm()] * 4,
        out_specs=[whole_vmem()] * (parts + late),
        scratch_shapes=[
            pltpu.VMEM(pre_gate.shape, jnp.bfloat16),
            pltpu.VMEM(value.shape, jnp.bfloat16),
            pltpu.VMEM(taps.shape, jnp.float32),
            pltpu.VMEM(post_gate.shape, jnp.bfloat16),
            pltpu.VMEM((channels // some, blocks * halves * some, LANES), jnp.float32),
            pltpu.VMEM((blocks * halves * taps.shape[0], LANES), jnp.float32),
            pltpu.VMEM((early * halves * channels, LANES), jnp.float32),
            pltpu.VMEM((parts, local, W), jnp.bfloat16),
            pltpu.SemaphoreType.DMA((channels // some + 1, 2)),
        ],
        compiler_params=pltpu.CompilerParams(vmem_limit_bytes=16 * 2**20),
        name="pack",
    )(*args)
    return list(out[:parts]), list(out[parts:])


def partner_order(count):
    corners = [d for d in range(1, count) if bin(d >> 1).count("1") > 1]
    straight = [d for d in range(2, count, 2) if d not in corners]
    order = [0] + corners[:1] + straight + corners[1:]
    return order + [d for d in range(2, count) if d not in order] + [1]


def swap(piece, axis, count, d):
    return lax.ppermute(piece, axis, [(i, i ^ d) for i in range(count)])


def tables_kernel(own, skip_ref, outer_ref, inner_ref, turns_ref, outer_out, back_out, ahead, rear, turns_out, *rest):
    outer_s, inner_s, skip_s, sems = rest
    count, width = turns_ref.shape
    loads = [
        pltpu.make_async_copy(outer_ref, outer_s, sems.at[0]),
        pltpu.make_async_copy(inner_ref, inner_s, sems.at[1]),
        pltpu.make_async_copy(turns_ref, turns_out.at[0:count, :], sems.at[2]),
        pltpu.make_async_copy(skip_ref, skip_s, sems.at[3]),
    ]
    for copy in loads[3:] + loads[:3]:
        copy.start()
    loads[3].wait()
    me = lax.axis_index("ctx")
    for c in range(own):
        turns_out[count + 8 * c : count + 8 * (c + 1), :] = jnp.full((8, width), skip_s[own * me + c], jnp.float32)
    loads[0].wait()
    outer_out[...] = outer_s[...].astype(jnp.bfloat16)
    back_out[...] = outer_s[...].T.astype(jnp.bfloat16)
    loads[1].wait()
    near_cos, near_sin = inner_s[0:W, :].astype(jnp.bfloat16), inner_s[W:, :].astype(jnp.bfloat16)
    for table, sign in ((ahead, -1), (rear, 1)):
        table[0:W, 0:W] = near_cos
        table[0:W, W:] = near_sin * sign
        table[W:, 0:W] = near_sin * -sign
        table[W:, W:] = near_cos
    loads[2].wait()


def make_tables(skip, outer, inner, turns, own):
    count, width = turns.shape
    args = [pltpu.with_memory_space_constraint(arg, pltpu.HBM) for arg in (skip, outer, inner, turns)]
    narrow = (outer.shape, outer.shape[::-1], (2 * W, 2 * W), (2 * W, 2 * W))
    return pl.pallas_call(
        functools.partial(tables_kernel, own),
        out_shape=[jax.ShapeDtypeStruct(shape, jnp.bfloat16) for shape in narrow]
        + [jax.ShapeDtypeStruct((count + 8 * own, width), jnp.float32)],
        in_specs=[in_hbm()] * 4,
        out_specs=[whole_vmem()] * 5,
        scratch_shapes=[
            pltpu.VMEM(outer.shape, jnp.float32),
            pltpu.VMEM(inner.shape, jnp.float32),
            pltpu.SMEM(skip.shape, jnp.float32),
            pltpu.SemaphoreType.DMA((4,)),
        ],
        compiler_params=pltpu.CompilerParams(vmem_limit_bytes=16 * 2**20),
        name="make_tables",
    )(*args)


def conv_kernel(own, near, ch_count, parts, *rest):
    got_refs = rest[:parts]
    outer_ref, back_ref, ahead, rear, turns_ref, out_ref, x_all, r_all, z_all = rest[parts:]
    blocks = parts * near
    length = blocks * W
    chunk = math.gcd(blocks, CHUNK)
    me = lax.axis_index("ctx")
    order = partner_order(parts)
    for d, got_ref in zip(order, got_refs):
        here = pl.ds(pl.multiple_of(jnp.bitwise_xor(me, d) * near, TILE), near)
        for c in range(own + 1):
            x_all[here, W * c : W * (c + 1)] = got_ref[c * near : (c + 1) * near, :]

    def dot(left, right):
        return jnp.dot(left, right, preferred_element_type=jnp.float32)

    for first in range(0, blocks, chunk):
        here = slice(first, first + chunk)
        there = slice(blocks + first, blocks + first + chunk)
        both = dot(jnp.concatenate([outer_ref[here, :], outer_ref[there, :]], 0), x_all[...])
        real, imag = both[0:chunk, :], both[chunk:, :]
        turn_cos, turn_sin = turns_ref[here, 0:W], turns_ref[here, W:]
        rows = []
        for c in range(own + 1):
            re, im = real[:, W * c : W * (c + 1)], imag[:, W * c : W * (c + 1)]
            pair = [re * turn_cos + im * turn_sin, im * turn_cos - re * turn_sin]
            rows.append(jnp.concatenate(pair, 1).astype(jnp.bfloat16))
        spectrum = dot(jnp.concatenate(rows, 0), ahead[...])
        filt_re = spectrum[chunk * own :, 0:W] * (1.0 / length)
        filt_im = spectrum[chunk * own :, W:] * (1.0 / length)
        rows = []
        for c in range(own):
            part = spectrum[chunk * c : chunk * (c + 1), :]
            re, im = part[:, 0:W], part[:, W:]
            pair = [re * filt_re - im * filt_im, re * filt_im + im * filt_re]
            rows.append(jnp.concatenate(pair, 1).astype(jnp.bfloat16))
        middle = dot(jnp.concatenate(rows, 0), rear[...])
        for c in range(own):
            part = middle[chunk * c : chunk * (c + 1), :]
            re, im = part[:, 0:W], part[:, W:]
            cols = slice(W * c, W * (c + 1))
            r_all[here, cols] = (re * turn_cos - im * turn_sin).astype(jnp.bfloat16)
            r_all[there, cols] = (re * turn_sin + im * turn_cos).astype(jnp.bfloat16)

    conv = dot(back_ref[...], r_all[...])
    for c in range(own):
        cols = slice(W * c, W * (c + 1))
        z_all[c] = conv[:, cols] + turns_ref[blocks + 8 * c : blocks + 8 * c + 1, 0:W] * x_all[:, cols].astype(jnp.float32)
    some = out_ref.shape[1] // own
    late = late_pieces(own, some, ch_count)
    early = some * (ch_count - late)
    place = lax.axis_index("ch")
    for d, got_ref in zip(order, got_refs):
        k = jnp.bitwise_xor(me, d)
        gate = got_ref[(own + 1) * near :, :].astype(jnp.float32)
        mine = [z_all[c, pl.ds(pl.multiple_of(k * near, TILE), near), :] for c in range(own)]
        for m in range(ch_count):
            rows = [part[m * some : (m + 1) * some, :] for part in mine]
            for e in range(late, ch_count):
                at = (e - late) * some
                for c in range(own):
                    factor = jnp.where(jnp.bitwise_xor(place, e) == m, gate[c * early + at : c * early + at + some, :], 1.0)
                    rows[c] = rows[c] * factor
            out_ref[k * ch_count + m] = jnp.concatenate(rows, 0).astype(jnp.bfloat16)


def convolve(got, tables, own, near, ch_count):
    parts = len(got)
    blocks = parts * near
    owners = parts * ch_count
    return pl.pallas_call(
        functools.partial(conv_kernel, own, near, ch_count, parts),
        out_shape=jax.ShapeDtypeStruct((owners, own * blocks // owners, W), jnp.bfloat16),
        in_specs=[whole_vmem()] * (parts + len(tables)),
        out_specs=whole_vmem(),
        scratch_shapes=[
            pltpu.VMEM((blocks, W * (own + 1)), jnp.bfloat16),
            pltpu.VMEM((2 * blocks, W * own), jnp.bfloat16),
            pltpu.VMEM((own, blocks, W), jnp.float32),
        ],
        compiler_params=pltpu.CompilerParams(vmem_limit_bytes=32 * 2**20),
        cost_estimate=pl.CostEstimate(flops=16000 * blocks * W, bytes_accessed=4 * blocks * W, transcendentals=0),
        name="convolve",
    )(*got, *tables)


def unpack_kernel(own, got_ref, *rest):
    gate_refs, (out_ref, flat, gate_s, stage, sems) = rest[:-5], rest[-5:]
    sources, rows, _ = got_ref.shape
    some = rows // own
    place = lax.axis_index("ch")
    channels, width = gate_refs[0].shape
    ch_count = out_ref.shape[0] // channels
    for d in range(ch_count):
        here = pl.ds(pl.multiple_of(jnp.bitwise_xor(place, d) * channels, TILE), channels)
        gate_s[here, :] = gate_refs[d][...] if d < len(gate_refs) else jnp.ones((channels, width), jnp.bfloat16)
    copies = []
    for m in range(ch_count):
        here = slice(m * channels, (m + 1) * channels)
        for k in range(sources // ch_count):
            part = got_ref[k * ch_count + m].astype(jnp.float32)
            first = m * channels * some + k * rows
            for h in range(W // LANES):
                flat[h, first : first + rows, :] = part[:, LANES * h : LANES * (h + 1)]
        for j in range(some):
            for h in range(W // LANES):
                part = flat[h, pl.ds(m * channels * some + j, channels, stride=some), :]
                first = W * j + LANES * h
                cols = slice(first, first + LANES)
                stage[here, cols] = (part * gate_s[here, cols].astype(jnp.float32)).astype(jnp.bfloat16)
        copies.append(pltpu.make_async_copy(stage.at[here], out_ref.at[here], sems.at[m]))
        copies[m].start()
    for copy in copies:
        copy.wait()


def unpack(got, gates, own, ch_count):
    sources, rows, _ = got.shape
    shape = (sources * own, rows // own * W)
    if rows % TILE:
        ones = [jnp.ones_like(gates[0])] * (ch_count - len(gates))
        order = jnp.bitwise_xor(lax.axis_index("ch"), jnp.arange(ch_count))
        gate = jnp.stack(gates + ones)[order].reshape(shape)
        got = got.reshape(-1, ch_count, rows, W).swapaxes(0, 1)
        return (got.reshape(shape).astype(jnp.float32) * gate.astype(jnp.float32)).astype(jnp.bfloat16)
    return pl.pallas_call(
        functools.partial(unpack_kernel, own),
        out_shape=jax.ShapeDtypeStruct(shape, jnp.bfloat16),
        in_specs=[whole_vmem()] * (1 + len(gates)),
        out_specs=in_hbm(),
        scratch_shapes=[
            pltpu.VMEM((W // LANES, sources * rows, LANES), jnp.float32),
            pltpu.VMEM(shape, jnp.bfloat16),
            pltpu.VMEM(shape, jnp.bfloat16),
            pltpu.SemaphoreType.DMA((ch_count,)),
        ],
        compiler_params=pltpu.CompilerParams(vmem_limit_bytes=24 * 2**20),
        name="unpack",
    )(got, *[pltpu.with_memory_space_constraint(gate, pltpu.VMEM) for gate in gates])


def body(pre_gate, value, post_gate, filter_taps, skip):
    ctx_count = lax.axis_size("ctx")
    ch_count = lax.axis_size("ch")
    own = value.shape[0] // ctx_count
    near = value.shape[1] // W
    got, gates = pack(pre_gate, value, post_gate, filter_taps, ctx_count, ch_count)
    order = partner_order(ctx_count)
    got = [got[d] for d in order]
    tables, skip, _ = lax.optimization_barrier((dft_tables(near * ctx_count), skip, got[0]))
    tables = list(make_tables(skip, *tables, own))
    got = [swap(piece, "ctx", ctx_count, d) if d else piece for piece, d in zip(got, order)]
    for d in range(1, len(gates)):
        gates[d] = swap(gates[d], "ch", ch_count, d)
    got[1:], gates[2:] = lax.optimization_barrier((got[1:], gates[2:]))
    mixed = convolve(got, tables, own, near, ch_count)
    mixed, gates = lax.optimization_barrier((mixed, gates[::-1]))
    gates = gates[::-1]
    mixed = lax.all_to_all(mixed, ("ctx", "ch"), split_axis=0, concat_axis=0, tiled=True)
    return unpack(mixed, gates, own, ch_count)


def solution(mesh):
    placed = (P("ch", "ctx"), P("ch", "ctx"), P("ch", "ctx"), P("ch", "ctx"), P("ch"))
    return jax.shard_map(
        body, mesh=mesh, in_specs=placed, out_specs=P(None, ("ctx", "ch")), check_vma=False
    )
```

```python
import functools
import math

import jax
import jax.numpy as jnp
import numpy as np
from jax import lax
from jax.experimental import pallas as pl
from jax.experimental.pallas import tpu as pltpu
from jax.sharding import PartitionSpec as P

W = 256
LANES = 128
TILE = 16
CHUNK = 256


def whole_vmem():
    return pl.BlockSpec(memory_space=pltpu.VMEM)


def in_hbm():
    return pl.BlockSpec(memory_space=pltpu.HBM)


def dft_tables(blocks):
    length = blocks * W
    k = np.arange(blocks)[:, None]
    angle = 2 * np.pi * ((4 * k + 1) * np.arange(blocks)[None, :] % (4 * blocks)) / (4 * blocks)
    outer = np.concatenate([np.cos(angle), -np.sin(angle)], 0)
    turn = 2 * np.pi * ((4 * k + 1) * np.arange(W)[None, :]) / (4 * length)
    near = 2 * np.pi * (np.arange(W)[:, None] * np.arange(W)[None, :] % W) / W
    inner = np.concatenate([np.cos(near), np.sin(near)], 0)
    turns = np.concatenate([np.cos(turn), np.sin(turn)], 1)
    return [jnp.asarray(table, jnp.float32) for table in (outer, inner, turns)]


def lay(natural, j, value):
    count = value.shape[0]
    for h in range(W // LANES):
        first = (j * (W // LANES) + h) * count
        natural[first : first + count, :] = value[:, LANES * h : LANES * (h + 1)]


def pick(natural, channel, count, blocks):
    halves = W // LANES
    rows = [natural[pl.ds(h * count + channel, blocks, stride=halves * count), :] for h in range(halves)]
    return jnp.concatenate(rows, 1)


def late_pieces(own, piece, ch_count):
    early = max(1, ch_count // 4)
    if own * piece * early % TILE:
        early = ch_count // 2
    return ch_count - early


def pack_kernel(own, blocks, group, ch_count, parts, pre_ref, val_ref, taps_ref, post_ref, *rest):
    piece = blocks // ch_count
    late = late_pieces(own, piece, ch_count)
    out_refs, gate_refs = rest[:parts], rest[parts : parts + late]
    pre_s, val_s, taps_s, post_s, natural, natural_taps, natural_gate, stage, in_sems = rest[parts + late :]
    channels = own * parts
    some = min(TILE, channels)
    rows = own * blocks
    main = rows + blocks
    loads = []
    for g in range(channels // some):
        here = pl.ds(g * some, some)
        loads.append(pltpu.make_async_copy(pre_ref.at[here], pre_s.at[here], in_sems.at[g, 0]))
        loads.append(pltpu.make_async_copy(val_ref.at[here], val_s.at[here], in_sems.at[g, 1]))
    taps_load = pltpu.make_async_copy(taps_ref, taps_s, in_sems.at[channels // some, 0])
    gate_load = pltpu.make_async_copy(post_ref, post_s, in_sems.at[channels // some, 1])
    for copy in loads[:2] + [taps_load] + loads[2:] + [gate_load]:
        copy.start()
    groups = taps_s.shape[0]
    taps_load.wait()
    for j in range(blocks):
        lay(natural_taps, j, taps_s[:, W * j : W * (j + 1)])
    for g in range(channels // some):
        loads[2 * g].wait()
        loads[2 * g + 1].wait()
        here = slice(g * some, (g + 1) * some)
        for j in range(blocks):
            cols = slice(W * j, W * (j + 1))
            product = pre_s[here, cols].astype(jnp.float32) * val_s[here, cols].astype(jnp.float32)
            lay(natural.at[g], j, product)
        for i in range(g * some // own, (g + 1) * some // own):
            for c in range(own):
                mine = pick(natural.at[g], own * i + c - g * some, some, blocks)
                stage[i, blocks * c : blocks * (c + 1), :] = mine.astype(jnp.bfloat16)
            taps = pick(natural_taps, own * i // group, groups, blocks)
            stage[i, rows:main, :] = taps.astype(jnp.bfloat16)
    gate_load.wait()
    place = lax.axis_index("ch")
    for d in range(ch_count):
        first = jnp.bitwise_xor(place, d) * (piece * W)
        if d < late:
            gate_refs[d][...] = post_s[:, pl.ds(pl.multiple_of(first, LANES), piece * W)]
        else:
            for j in range(piece):
                cols = pl.ds(pl.multiple_of(first + W * j, LANES), W)
                lay(natural_gate, (d - late) * piece + j, post_s[:, cols].astype(jnp.float32))
    early = piece * (ch_count - late)
    for i in range(parts):
        gate = [pick(natural_gate, own * i + c, channels, early) for c in range(own)]
        stage[i, main:, :] = jnp.concatenate(gate, 0).astype(jnp.bfloat16)
    me = lax.axis_index("ctx")
    for d in range(parts):
        out_refs[d][...] = stage[jnp.bitwise_xor(me, d)]


def pack(pre_gate, value, post_gate, taps, parts, ch_count):
    channels, block = value.shape
    own = channels // parts
    group = channels // taps.shape[0]
    blocks = block // W
    piece = blocks // ch_count
    late = late_pieces(own, piece, ch_count)
    early = piece * (ch_count - late)
    local = (own + 1) * blocks + own * early
    halves = W // LANES
    some = min(TILE, channels)
    args = [pltpu.with_memory_space_constraint(arg, pltpu.HBM) for arg in (pre_gate, value, taps, post_gate)]
    out = pl.pallas_call(
        functools.partial(pack_kernel, own, blocks, group, ch_count, parts),
        out_shape=[jax.ShapeDtypeStruct((local, W), jnp.bfloat16)] * parts
        + [jax.ShapeDtypeStruct((channels, piece * W), jnp.bfloat16)] * late,
        in_specs=[in_hbm()] * 4,
        out_specs=[whole_vmem()] * (parts + late),
        scratch_shapes=[
            pltpu.VMEM(pre_gate.shape, jnp.bfloat16),
            pltpu.VMEM(value.shape, jnp.bfloat16),
            pltpu.VMEM(taps.shape, jnp.float32),
            pltpu.VMEM(post_gate.shape, jnp.bfloat16),
            pltpu.VMEM((channels // some, blocks * halves * some, LANES), jnp.float32),
            pltpu.VMEM((blocks * halves * taps.shape[0], LANES), jnp.float32),
            pltpu.VMEM((early * halves * channels, LANES), jnp.float32),
            pltpu.VMEM((parts, local, W), jnp.bfloat16),
            pltpu.SemaphoreType.DMA((channels // some + 1, 2)),
        ],
        compiler_params=pltpu.CompilerParams(vmem_limit_bytes=16 * 2**20),
        name="pack",
    )(*args)
    return list(out[:parts]), list(out[parts:])


def partner_order(count):
    corners = [d for d in range(1, count) if bin(d >> 1).count("1") > 1]
    straight = [d for d in range(2, count, 2) if d not in corners]
    order = [0] + corners[:1] + straight + corners[1:]
    return order + [d for d in range(2, count) if d not in order] + [1]


def swap(piece, axis, count, d):
    return lax.ppermute(piece, axis, [(i, i ^ d) for i in range(count)])


def tables_kernel(own, skip_ref, outer_ref, inner_ref, turns_ref, outer_out, back_out, ahead, rear, turns_out, *rest):
    outer_s, inner_s, skip_s, sems = rest
    count, width = turns_ref.shape
    loads = [
        pltpu.make_async_copy(outer_ref, outer_s, sems.at[0]),
        pltpu.make_async_copy(inner_ref, inner_s, sems.at[1]),
        pltpu.make_async_copy(turns_ref, turns_out.at[0:count, :], sems.at[2]),
        pltpu.make_async_copy(skip_ref, skip_s, sems.at[3]),
    ]
    for copy in loads[3:] + loads[:3]:
        copy.start()
    loads[3].wait()
    me = lax.axis_index("ctx")
    for c in range(own):
        turns_out[count + 8 * c : count + 8 * (c + 1), :] = jnp.full((8, width), skip_s[own * me + c], jnp.float32)
    loads[0].wait()
    outer_out[...] = outer_s[...].astype(jnp.bfloat16)
    back_out[...] = outer_s[...].T.astype(jnp.bfloat16)
    loads[1].wait()
    near_cos, near_sin = inner_s[0:W, :].astype(jnp.bfloat16), inner_s[W:, :].astype(jnp.bfloat16)
    for table, sign in ((ahead, -1), (rear, 1)):
        table[0:W, 0:W] = near_cos
        table[0:W, W:] = near_sin * sign
        table[W:, 0:W] = near_sin * -sign
        table[W:, W:] = near_cos
    loads[2].wait()


def make_tables(skip, outer, inner, turns, own):
    count, width = turns.shape
    args = [pltpu.with_memory_space_constraint(arg, pltpu.HBM) for arg in (skip, outer, inner, turns)]
    narrow = (outer.shape, outer.shape[::-1], (2 * W, 2 * W), (2 * W, 2 * W))
    return pl.pallas_call(
        functools.partial(tables_kernel, own),
        out_shape=[jax.ShapeDtypeStruct(shape, jnp.bfloat16) for shape in narrow]
        + [jax.ShapeDtypeStruct((count + 8 * own, width), jnp.float32)],
        in_specs=[in_hbm()] * 4,
        out_specs=[whole_vmem()] * 5,
        scratch_shapes=[
            pltpu.VMEM(outer.shape, jnp.float32),
            pltpu.VMEM(inner.shape, jnp.float32),
            pltpu.SMEM(skip.shape, jnp.float32),
            pltpu.SemaphoreType.DMA((4,)),
        ],
        compiler_params=pltpu.CompilerParams(vmem_limit_bytes=16 * 2**20),
        name="make_tables",
    )(*args)


def conv_kernel(own, near, ch_count, parts, *rest):
    got_refs = rest[:parts]
    outer_ref, back_ref, ahead, rear, turns_ref, out_ref, x_all, r_all, z_all = rest[parts:]
    blocks = parts * near
    length = blocks * W
    chunk = math.gcd(blocks, CHUNK)
    me = lax.axis_index("ctx")
    order = partner_order(parts)
    for d, got_ref in zip(order, got_refs):
        here = pl.ds(pl.multiple_of(jnp.bitwise_xor(me, d) * near, TILE), near)
        for c in range(own + 1):
            x_all[here, W * c : W * (c + 1)] = got_ref[c * near : (c + 1) * near, :]

    def dot(left, right):
        return jnp.dot(left, right, preferred_element_type=jnp.float32)

    for first in range(0, blocks, chunk):
        here = slice(first, first + chunk)
        there = slice(blocks + first, blocks + first + chunk)
        both = dot(jnp.concatenate([outer_ref[here, :], outer_ref[there, :]], 0), x_all[...])
        real, imag = both[0:chunk, :], both[chunk:, :]
        turn_cos, turn_sin = turns_ref[here, 0:W], turns_ref[here, W:]
        rows = []
        for c in range(own + 1):
            re, im = real[:, W * c : W * (c + 1)], imag[:, W * c : W * (c + 1)]
            pair = [re * turn_cos + im * turn_sin, im * turn_cos - re * turn_sin]
            rows.append(jnp.concatenate(pair, 1).astype(jnp.bfloat16))
        spectrum = dot(jnp.concatenate(rows, 0), ahead[...])
        filt_re = spectrum[chunk * own :, 0:W] * (1.0 / length)
        filt_im = spectrum[chunk * own :, W:] * (1.0 / length)
        rows = []
        for c in range(own):
            part = spectrum[chunk * c : chunk * (c + 1), :]
            re, im = part[:, 0:W], part[:, W:]
            pair = [re * filt_re - im * filt_im, re * filt_im + im * filt_re]
            rows.append(jnp.concatenate(pair, 1).astype(jnp.bfloat16))
        middle = dot(jnp.concatenate(rows, 0), rear[...])
        for c in range(own):
            part = middle[chunk * c : chunk * (c + 1), :]
            re, im = part[:, 0:W], part[:, W:]
            cols = slice(W * c, W * (c + 1))
            r_all[here, cols] = (re * turn_cos - im * turn_sin).astype(jnp.bfloat16)
            r_all[there, cols] = (re * turn_sin + im * turn_cos).astype(jnp.bfloat16)

    conv = dot(back_ref[...], r_all[...])
    for c in range(own):
        cols = slice(W * c, W * (c + 1))
        z_all[c] = conv[:, cols] + turns_ref[blocks + 8 * c : blocks + 8 * c + 1, 0:W] * x_all[:, cols].astype(jnp.float32)
    some = out_ref.shape[1] // own
    late = late_pieces(own, some, ch_count)
    early = some * (ch_count - late)
    place = lax.axis_index("ch")
    for d, got_ref in zip(order, got_refs):
        k = jnp.bitwise_xor(me, d)
        gate = got_ref[(own + 1) * near :, :].astype(jnp.float32)
        mine = [z_all[c, pl.ds(pl.multiple_of(k * near, TILE), near), :] for c in range(own)]
        for m in range(ch_count):
            rows = [part[m * some : (m + 1) * some, :] for part in mine]
            for e in range(late, ch_count):
                at = (e - late) * some
                for c in range(own):
                    factor = jnp.where(jnp.bitwise_xor(place, e) == m, gate[c * early + at : c * early + at + some, :], 1.0)
                    rows[c] = rows[c] * factor
            out_ref[k * ch_count + m] = jnp.concatenate(rows, 0).astype(jnp.bfloat16)


def convolve(got, tables, own, near, ch_count):
    parts = len(got)
    blocks = parts * near
    owners = parts * ch_count
    return pl.pallas_call(
        functools.partial(conv_kernel, own, near, ch_count, parts),
        out_shape=jax.ShapeDtypeStruct((owners, own * blocks // owners, W), jnp.bfloat16),
        in_specs=[whole_vmem()] * (parts + len(tables)),
        out_specs=whole_vmem(),
        scratch_shapes=[
            pltpu.VMEM((blocks, W * (own + 1)), jnp.bfloat16),
            pltpu.VMEM((2 * blocks, W * own), jnp.bfloat16),
            pltpu.VMEM((own, blocks, W), jnp.float32),
        ],
        compiler_params=pltpu.CompilerParams(vmem_limit_bytes=32 * 2**20),
        cost_estimate=pl.CostEstimate(flops=7000 * blocks * W, bytes_accessed=4 * blocks * W, transcendentals=0),
        name="convolve",
    )(*got, *tables)


def unpack_kernel(own, got_ref, *rest):
    gate_refs, (out_ref, flat, gate_s, stage, sems) = rest[:-5], rest[-5:]
    sources, rows, _ = got_ref.shape
    some = rows // own
    place = lax.axis_index("ch")
    channels, width = gate_refs[0].shape
    ch_count = out_ref.shape[0] // channels
    for d in range(ch_count):
        here = pl.ds(pl.multiple_of(jnp.bitwise_xor(place, d) * channels, TILE), channels)
        gate_s[here, :] = gate_refs[d][...] if d < len(gate_refs) else jnp.ones((channels, width), jnp.bfloat16)
    copies = []
    for m in range(ch_count):
        here = slice(m * channels, (m + 1) * channels)
        for k in range(sources // ch_count):
            part = got_ref[k * ch_count + m].astype(jnp.float32)
            first = m * channels * some + k * rows
            for h in range(W // LANES):
                flat[h, first : first + rows, :] = part[:, LANES * h : LANES * (h + 1)]
        for j in range(some):
            for h in range(W // LANES):
                part = flat[h, pl.ds(m * channels * some + j, channels, stride=some), :]
                first = W * j + LANES * h
                cols = slice(first, first + LANES)
                stage[here, cols] = (part * gate_s[here, cols].astype(jnp.float32)).astype(jnp.bfloat16)
        copies.append(pltpu.make_async_copy(stage.at[here], out_ref.at[here], sems.at[m]))
        copies[m].start()
    for copy in copies:
        copy.wait()


def unpack(got, gates, own, ch_count):
    sources, rows, _ = got.shape
    shape = (sources * own, rows // own * W)
    if rows % TILE:
        ones = [jnp.ones_like(gates[0])] * (ch_count - len(gates))
        order = jnp.bitwise_xor(lax.axis_index("ch"), jnp.arange(ch_count))
        gate = jnp.stack(gates + ones)[order].reshape(shape)
        got = got.reshape(-1, ch_count, rows, W).swapaxes(0, 1)
        return (got.reshape(shape).astype(jnp.float32) * gate.astype(jnp.float32)).astype(jnp.bfloat16)
    return pl.pallas_call(
        functools.partial(unpack_kernel, own),
        out_shape=jax.ShapeDtypeStruct(shape, jnp.bfloat16),
        in_specs=[whole_vmem()] * (1 + len(gates)),
        out_specs=in_hbm(),
        scratch_shapes=[
            pltpu.VMEM((W // LANES, sources * rows, LANES), jnp.float32),
            pltpu.VMEM(shape, jnp.bfloat16),
            pltpu.VMEM(shape, jnp.bfloat16),
            pltpu.SemaphoreType.DMA((ch_count,)),
        ],
        compiler_params=pltpu.CompilerParams(vmem_limit_bytes=24 * 2**20),
        name="unpack",
    )(got, *[pltpu.with_memory_space_constraint(gate, pltpu.VMEM) for gate in gates])


def body(pre_gate, value, post_gate, filter_taps, skip):
    ctx_count = lax.axis_size("ctx")
    ch_count = lax.axis_size("ch")
    own = value.shape[0] // ctx_count
    near = value.shape[1] // W
    got, gates = pack(pre_gate, value, post_gate, filter_taps, ctx_count, ch_count)
    order = partner_order(ctx_count)
    got = [got[d] for d in order]
    tables, skip, _ = lax.optimization_barrier((dft_tables(near * ctx_count), skip, got[0]))
    tables = list(make_tables(skip, *tables, own))
    got = [swap(piece, "ctx", ctx_count, d) if d else piece for piece, d in zip(got, order)]
    for d in range(1, len(gates)):
        gates[d] = swap(gates[d], "ch", ch_count, d)
    got[1:], gates[2:] = lax.optimization_barrier((got[1:], gates[2:]))
    mixed = convolve(got, tables, own, near, ch_count)
    mixed, gates = lax.optimization_barrier((mixed, gates[::-1]))
    gates = gates[::-1]
    mixed = lax.all_to_all(mixed, ("ctx", "ch"), split_axis=0, concat_axis=0, tiled=True)
    return unpack(mixed, gates, own, ch_count)


def solution(mesh):
    placed = (P("ch", "ctx"), P("ch", "ctx"), P("ch", "ctx"), P("ch", "ctx"), P("ch"))
    return jax.shard_map(
        body, mesh=mesh, in_specs=placed, out_specs=P(None, ("ctx", "ch")), check_vma=False
    )
```
